32 devices in a mesh: seq: 8 (over z, core), wsh: 4 (over y, x).
Axes of the slice: x: 2, y: 2, z: 4, core: 2. Of those that a mesh axis runs over, the one named last changes fastest.
Arguments:
- x_in: bfloat16 [4, 8192, 1024], P('wsh', 'seq'), may hold values from -6 to 6
- seg_ids: int32 [4, 8192], P('wsh'), may hold values from 0 to 11, as said below
- g_norm: float32 [1024], replicated, may hold values from 0.25 to 1.75
- w_in: bfloat16 [1024, 4384], P('wsh'), may hold values from -0.1875 to 0.1875
- conv_w: float32 [4, 2304], replicated, may hold values from -3 to 3
- conv_b: float32 [2304], replicated, may hold values from -3 to 3
- dt_bias: float32 [32], replicated, may hold values from -9 to -2
- a_log: float32 [32], replicated, may hold values from 0 to 2.77
- d_skip: float32 [32], replicated, may hold values from 0.5 to 2
- g_gate: float32 [2048], replicated, may hold values from 0.25 to 1.75
- w_out: bfloat16 [2048, 1024], P('wsh'), may hold values from -0.125 to 0.125
- cotangent: bfloat16 [4, 8192, 1024], P('wsh', 'seq'), may hold values from -6 to 6
Outputs:
- out: bfloat16 [4, 8192, 1024], P('wsh', 'seq')
- x_grad: float32 [4, 8192, 1024], P('wsh', 'seq')
- g_norm_grad: float32 [1024], replicated
- w_in_grad: float32 [1024, 4384], P('wsh')
- conv_w_grad: float32 [4, 2304], replicated
- conv_b_grad: float32 [2304], replicated
- dt_bias_grad: float32 [32], replicated
- a_log_grad: float32 [32], replicated
- d_skip_grad: float32 [32], replicated
- g_gate_grad: float32 [2048], replicated
- w_out_grad: float32 [2048, 1024], P('wsh')
The draws below stay inside these ranges and needn't reach their ends.
Inputs may be any that keep to these rules, and one draw needn't show every extreme that they name: `seg_ids`: in group g (first dimension) the ids along the 8192 positions are 3g, then 3g+1, then 3g+2, each present; id 3g+1 starts within the first 1024 positions and ends within the last 1024.
All inputs are finite; a program needn't handle non-finite values.
Results may differ from the reference program's by a relative error of at most 0.012.
Values may be sent and summed in bfloat16 or wider, within the bound.
No kernel may reach another device: no remote copies, remote signals or barrier semaphores. Data moves between devices by JAX's collectives and lax.ppermute only.
A program may use at most 320 MiB of HBM per device.

```python
import jax
import jax.numpy as jnp
from jax import lax

D = 1024
HEADS = 32
STATE = 128
KERNEL = 4
STRETCH = 256
TOK_DEV = 1024
D_INNER = 2048
PROJ = 4384
CONV_CH = 2304
SPAN = 8192
N_WSH = 4


def draw_seg_ids(key, part):
    key = jax.random.fold_in(key, 11)
    first_key, second_key = jax.random.split(key)
    first_cut = jax.random.randint(first_key, (N_WSH, 1), 1, TOK_DEV)
    second_cut = jax.random.randint(second_key, (N_WSH, 1), SPAN - TOK_DEV + 1, SPAN)
    places = lax.broadcasted_iota(jnp.int32, (N_WSH, SPAN), 1)
    groups = lax.broadcasted_iota(jnp.int32, (N_WSH, SPAN), 0)
    return 3 * groups + (places >= first_cut).astype(jnp.int32) + (places >= second_cut).astype(jnp.int32)


def block_scale(key, extent, cuts, least, top_value):
    loudness, own = 1.0, jax.random.fold_in(key, 6)
    for dim, shards_of in cuts:
        steps = jnp.exp(jax.random.uniform(jax.random.fold_in(own, dim), (shards_of,), jnp.float32, least / len(cuts), top_value / len(cuts)))
        loudness = loudness * jnp.repeat(steps, extent[dim] // shards_of).reshape([-1 if axis == dim else 1 for axis in range(len(extent))])
    return loudness


def noise(own_key, extent, deviation, limit, shards=(), kind=jnp.bfloat16):
    entries = jax.random.normal(own_key, extent, jnp.float32) * deviation
    if len(shards) > 0:
        entries = block_scale(own_key, extent, shards, -0.22, 0.18) * entries
    return jnp.clip(entries, min=-limit, max=limit).astype(kind)


def setup_inputs(seed: int = 0) -> dict:
    streams_of = jax.random.split(jax.random.key(seed), 13)
    return {
        "x_in": noise(streams_of[0], (N_WSH, SPAN, D), 1.0, 6.0, ((0, 4), (1, 8))),
        "seg_ids": draw_seg_ids(jax.random.fold_in(streams_of[12], 71), 0),
        "g_norm": jnp.clip(1.0 + 0.15 * jax.random.normal(streams_of[2], (D,), jnp.float32), 0.25, 1.75),
        "w_in": noise(streams_of[3], (D, PROJ), D ** -0.5, 0.1875, ((0, 4),)),
        "conv_w": noise(streams_of[4], (KERNEL, CONV_CH), KERNEL ** -0.5, 3.0, (), jnp.float32),
        "conv_b": noise(streams_of[5], (CONV_CH,), 0.5, 3.0, (), jnp.float32),
        "dt_bias": jnp.clip(jax.random.uniform(streams_of[6], (HEADS,), jnp.float32, -9.0, -2.0), -9.0, -2.0),
        "a_log": jnp.clip(jax.random.uniform(streams_of[7], (HEADS,), jnp.float32, 0.0, 2.77), 0.0, 2.77),
        "d_skip": jnp.clip(jax.random.uniform(streams_of[8], (HEADS,), jnp.float32, 0.5, 2.0), 0.5, 2.0),
        "g_gate": jnp.clip(1.0 + 0.15 * jax.random.normal(streams_of[9], (D_INNER,), jnp.float32), 0.25, 1.75),
        "w_out": noise(streams_of[10], (D_INNER, D), D_INNER ** -0.5, 0.125, ((0, 4),)),
        "cotangent": noise(streams_of[11], (N_WSH, SPAN, D), 1.0, 6.0, ((0, 4), (1, 8))),
    }


EPSILON = 1e-05
EXACT = lax.Precision.HIGHEST

@jax.custom_vjp
def low(v):
    return lax.optimization_barrier(v.astype(jnp.bfloat16)).astype(jnp.float32)

@jax.custom_vjp
def low_back(v):
    return v

def low_keep(v):
    return (low(v), None)

def low_pass(kept, grad):
    return (grad,)

def back_keep(v):
    return (v, None)

def back_low(kept, grad):
    return (low(grad),)
low.defvjp(low_keep, low_pass)
low_back.defvjp(back_keep, back_low)

def root_mean(values):
    return lax.rsqrt(lax.optimization_barrier(jnp.mean(values * values, axis=1, keepdims=True)) + EPSILON)

def causal_conv(values, kernel, offset_bias, segment):
    length = values.shape[0]
    taps = kernel.shape[0]
    conv_total = jnp.zeros_like(values) + offset_bias[None, :]
    for offset in range(taps):
        moved_rows = jnp.concatenate([jnp.zeros((offset, values.shape[1]), values.dtype), values[:length - offset]], axis=0)
        moved_segment = jnp.concatenate([jnp.full((offset,), -1, jnp.int32), segment[:length - offset]], axis=0)
        keeping = (moved_segment == segment).astype(values.dtype)
        conv_total = conv_total + kernel[taps - 1 - offset][None, :] * moved_rows * keeping[:, None]
    return conv_total

def stretch_step(carried, pieces, decay_rates):
    state_now, previous = carried
    values, b_rows, c_rows, step_sizes, segment = pieces
    block_width = values.shape[0]
    log_steps = step_sizes * decay_rates[None, :]
    cumulative = jnp.cumsum(log_steps, axis=0)
    later_pos = lax.broadcasted_iota(jnp.int32, (block_width, block_width), 0)
    earlier_pos = lax.broadcasted_iota(jnp.int32, (block_width, block_width), 1)
    linked = (segment[:, None] == segment[None, :]) & (later_pos >= earlier_pos)
    spread_log = cumulative.T[:, :, None] - cumulative.T[:, None, :]
    decay_table = jnp.where(linked[None], jnp.exp(jnp.where(linked[None], spread_log, 0.0)), 0.0)
    intersection = jnp.dot(c_rows, b_rows.T, precision=EXACT)
    mixing = decay_table * intersection[None] * step_sizes.T[:, None, :]
    inside = jnp.einsum('hts,shp->thp', mixing, values, precision=EXACT)
    entering = jnp.exp(cumulative) * (segment == previous).astype(values.dtype)[:, None]
    outside = jnp.einsum('tn,hpn->thp', c_rows, state_now, precision=EXACT) * entering[:, :, None]
    last_segment = segment[-1]
    leaving = jnp.exp(cumulative[-1][None, :] - cumulative) * step_sizes * (segment == last_segment).astype(values.dtype)[:, None]
    fresh_state = jnp.einsum('sh,shp,sn->hpn', leaving, values, b_rows, precision=EXACT)
    keep_state = (last_segment == previous).astype(values.dtype)
    state_now = state_now * (jnp.exp(cumulative[-1]) * keep_state)[:, None, None] + fresh_state
    return ((state_now, last_segment), inside + outside)

def state_scan(values, b_rows, c_rows, step_sizes, decay_rates, segment):
    length, head_count, head_width = values.shape
    stretch_count = length // STRETCH
    pieces = (values.reshape(stretch_count, STRETCH, head_count, head_width), b_rows.reshape(stretch_count, STRETCH, b_rows.shape[1]), c_rows.reshape(stretch_count, STRETCH, c_rows.shape[1]), step_sizes.reshape(stretch_count, STRETCH, head_count), segment.reshape(stretch_count, STRETCH))
    initial = (jnp.zeros((head_count, head_width, b_rows.shape[1]), values.dtype), jnp.int32(-1))
    stepper = jax.checkpoint(lambda carried, piece: stretch_step(carried, piece, decay_rates))
    final_carry, outputs = lax.scan(stepper, initial, pieces)
    return outputs.reshape(length, head_count, head_width)

def local_mixer(gate_in, x_heads, step_raw, bc_in, conv_w, conv_b, dt_bias, a_log, d_skip, segment, channel_start, head_start):
    block_width = x_heads.shape[1]
    head_count = step_raw.shape[1]
    inner = conv_w.shape[1] - 2 * STATE
    kernel = jnp.concatenate([lax.dynamic_slice_in_dim(conv_w, channel_start, block_width, 1), conv_w[:, inner:]], axis=1)
    offset_bias = jnp.concatenate([lax.dynamic_slice_in_dim(conv_b, channel_start, block_width, 0), conv_b[inner:]], axis=0)
    mixed = jax.nn.silu(causal_conv(jnp.concatenate([x_heads, bc_in], axis=1), kernel, offset_bias, segment))
    length = mixed.shape[0]
    values = mixed[:, :block_width].reshape(length, head_count, block_width // head_count)
    b_rows = mixed[:, block_width:block_width + STATE]
    c_rows = mixed[:, block_width + STATE:]
    step_sizes = jax.nn.softplus(step_raw + lax.dynamic_slice_in_dim(dt_bias, head_start, head_count, 0)[None, :])
    decay_rates = -jnp.exp(lax.dynamic_slice_in_dim(a_log, head_start, head_count, 0))
    skip_gain = lax.dynamic_slice_in_dim(d_skip, head_start, head_count, 0)
    result = state_scan(values, b_rows, c_rows, step_sizes, decay_rates, segment) + skip_gain[None, :, None] * values
    return result.reshape(length, block_width) * jax.nn.silu(gate_in)

def block_forward(x_rows, segment, g_norm, w_in, conv_w, conv_b, dt_bias, a_log, d_skip, g_gate, w_out):
    normed = low(x_rows * root_mean(x_rows) * g_norm[None, :])
    projected = low_back(low(jnp.dot(normed, w_in, precision=EXACT)))
    inner = g_gate.shape[0]
    gated = local_mixer(projected[:, :inner], projected[:, inner:2 * inner], projected[:, 2 * inner + 2 * STATE:], projected[:, 2 * inner:2 * inner + 2 * STATE], conv_w, conv_b, dt_bias, a_log, d_skip, segment, 0, 0)
    normed_heads = low_back(low(gated * root_mean(gated) * g_gate[None, :]))
    return x_rows + jnp.dot(normed_heads, w_out, precision=EXACT)

def reference(x_in, seg_ids, g_norm, w_in, conv_w, conv_b, dt_bias, a_log, d_skip, g_gate, w_out, cotangent):

    def whole(x_rows, g_norm, w_in, conv_w, conv_b, dt_bias, a_log, d_skip, g_gate, w_out):

        def one_group(carried, pair):
            return (carried, block_forward(pair[0], pair[1], g_norm, w_in, conv_w, conv_b, dt_bias, a_log, d_skip, g_gate, w_out))
        final_carry, outputs = lax.scan(jax.checkpoint(one_group), jnp.float32(0.0), (x_rows, seg_ids))
        return outputs
    primals = (x_in.astype(jnp.float32), g_norm.astype(jnp.float32), w_in.astype(jnp.float32), conv_w.astype(jnp.float32), conv_b.astype(jnp.float32), dt_bias.astype(jnp.float32), a_log.astype(jnp.float32), d_skip.astype(jnp.float32), g_gate.astype(jnp.float32), w_out.astype(jnp.float32))
    result, pullback = jax.vjp(whole, *primals)
    grads = pullback(cotangent.astype(jnp.float32))
    return (result.astype(jnp.bfloat16), grads[0], grads[1], grads[2], grads[3], grads[4], grads[5], grads[6], grads[7], grads[8], grads[9])
```

```python
from functools import partial

import jax
import jax.numpy as jnp
from jax import lax
from jax.experimental import pallas as pl
from jax.experimental.pallas import tpu as pltpu
from jax.sharding import PartitionSpec as P

STATE = 128
CHUNK = 128
HALO = 16
EPSILON = 1e-05
EXACT = lax.Precision.HIGHEST
BF = jnp.bfloat16
F32 = jnp.float32
VMEM_LIMIT = 56 * 1024 * 1024


def dot(a, b):
    return jnp.dot(a, b, preferred_element_type=F32)


def dot_tt(a, b):
    return lax.dot_general(a, b, (((1,), (1,)), ((), ())), preferred_element_type=F32)


def dot_00(a, b):
    return lax.dot_general(a, b, (((0,), (0,)), ((), ())), preferred_element_type=F32)


def sigmoid(v):
    return 1.0 / (1.0 + jnp.exp(-v))


def params():
    return pltpu.CompilerParams(vmem_limit_bytes=VMEM_LIMIT, dimension_semantics=("arbitrary",))


def conv_kernel(x_ref, keep_ref, w_ref, b_ref, z_ref, buf):
    rows = z_ref.shape[0]
    buf[...] = x_ref[...].astype(F32)
    taps = w_ref.shape[0]
    for start in range(0, rows, CHUNK):
        keep = keep_ref[start : start + CHUNK, :]
        total = b_ref[...] + w_ref[taps - 1 : taps, :] * buf[HALO + start : HALO + start + CHUNK, :]
        for k in range(1, taps):
            moved = buf[HALO + start - k : HALO + start - k + CHUNK, :]
            total = total + w_ref[taps - 1 - k : taps - k, :] * (moved * keep[:, k : k + 1])
        z_ref[start : start + CHUNK, :] = total.astype(BF)


def conv_back_kernel(dz_ref, x_ref, keep_ref, next_ref, w_ref, dx_ref, dw_ref, db_ref, buf, dbuf):
    rows, width = dz_ref.shape
    taps = w_ref.shape[0]
    buf[...] = x_ref[...].astype(F32)
    dbuf[0:HALO, :] = jnp.zeros((HALO, width), F32)
    dbuf[HALO : HALO + rows, :] = dz_ref[...].astype(F32)
    dbuf[HALO + rows :, :] = jnp.zeros((8, width), F32)
    sums = [jnp.zeros((1, width), F32) for _ in range(taps + 1)]
    for start in range(0, rows, CHUNK):
        keep = keep_ref[start : start + CHUNK, :]
        dz = dbuf[HALO + start : HALO + start + CHUNK, :]
        sums[taps] = sums[taps] + jnp.sum(dz, axis=0, keepdims=True)
        for k in range(taps):
            moved = buf[HALO + start - k : HALO + start - k + CHUNK, :]
            if k:
                moved = moved * keep[:, k : k + 1]
            sums[k] = sums[k] + jnp.sum(dz * moved, axis=0, keepdims=True)
    for k in range(taps):
        dw_ref[taps - 1 - k : taps - k, :] = sums[k]
    db_ref[...] = sums[taps]
    for start in range(0, rows + HALO, HALO * 13):
        count = min(HALO * 13, rows + HALO - start)
        total = w_ref[taps - 1 : taps, :] * dbuf[start : start + count, :]
        nxt = next_ref[start : start + count, :]
        for k in range(1, taps):
            moved = dbuf[start + k : start + k + count, :]
            total = total + w_ref[taps - 1 - k : taps - k, :] * (moved * nxt[:, k : k + 1])
        dx_ref[start : start + count, :] = total.astype(BF)


def state_kernel(z_ref, tok_ref, spread_ref, s_ref):
    inner = s_ref.shape[1]

    @pl.when(pl.program_id(0) == 0)
    def _():
        s_ref[...] = jnp.zeros_like(s_ref)

    z = z_ref[:, : inner + STATE].astype(F32)
    mixed = z * sigmoid(z)
    factor = dot(tok_ref[...].astype(BF), spread_ref[...])
    s_ref[...] += dot_00(mixed[:, inner:].astype(BF), (mixed[:, :inner] * factor).astype(BF))


def decay_pair(tok, cum_rows, head, heads):
    gap = tok[:, heads + head : heads + head + 1] - cum_rows[head : head + 1, :]
    return jnp.exp(jnp.minimum(gap, 0.0))


def linked_mask(seg_col, seg_row):
    later = lax.broadcasted_iota(jnp.int32, (CHUNK, CHUNK), 0)
    earlier = lax.broadcasted_iota(jnp.int32, (CHUNK, CHUNK), 1)
    return (seg_col == seg_row) & (later >= earlier)


def two_heads(pair):
    lane = lax.broadcasted_iota(jnp.int32, pair.shape, 1)
    zero = jnp.zeros_like(pair)
    half = pair.shape[1] // 2
    return jnp.where(lane < half, pair, zero), jnp.where(lane >= half, pair, zero)


def inside_kernel(heads, z_ref, tok_ref, seg_ref, cum_ref, segrow_ref, spread_ref, skip_ref, y_ref):
    inner = y_ref.shape[1]
    pair_width = 2 * inner // heads
    z = z_ref[...].astype(F32)
    mixed = z * sigmoid(z)
    tok = tok_ref[...]
    xc = mixed[:, :inner]
    xt = (xc * dot(tok.astype(BF), spread_ref[...])).astype(BF)
    b_rows = mixed[:, inner : inner + STATE].astype(BF)
    c_rows = mixed[:, inner + STATE :].astype(BF)
    mask = linked_mask(seg_ref[...], segrow_ref[...])
    cross = jnp.where(mask, dot_tt(c_rows, b_rows), 0.0)
    cum_rows = cum_ref[...]
    for j in range(heads // 2):
        at = slice(j * pair_width, (j + 1) * pair_width)
        left = [(cross * decay_pair(tok, cum_rows, 2 * j + i, heads)).astype(BF) for i in (0, 1)]
        right = two_heads(xt[:, at])
        part = dot(jnp.concatenate(left, axis=1), jnp.concatenate(right, axis=0))
        y_ref[:, at] = (part + skip_ref[:, at] * xc[:, at]).astype(BF)


def gate_kernel(
    yi_ref, z_ref, gate_ref, back_ref, tok_ref, far_ref, decay_ref, gain_ref, s0_ref,
    spread_ref, spread_ent_ref, spread_leave_ref,
    sin_ref, out_ref, dgate_ref, dy_ref, dgain_ref, dskip_ref, ds_ref, state,
):
    inner = yi_ref.shape[1]

    @pl.when(pl.program_id(0) == 0)
    def _():
        state[...] = s0_ref[...]
        dgain_ref[...] = jnp.zeros_like(dgain_ref)
        dskip_ref[...] = jnp.zeros_like(dskip_ref)
        ds_ref[...] = jnp.zeros_like(ds_ref)

    z = z_ref[...].astype(F32)
    mixed = z * sigmoid(z)
    xc = mixed[:, :inner]
    b_rows = mixed[:, inner : inner + STATE].astype(BF)
    c_rows = mixed[:, inner + STATE :].astype(BF)
    tok = tok_ref[...].astype(BF)
    now = state[...]
    now_bf = now.astype(BF)
    sin_ref[0] = now_bf
    y = yi_ref[...].astype(F32) + dot(c_rows, now_bf) * dot(tok, spread_ent_ref[...])
    leave = (xc * dot(tok, spread_ref[...])) * dot(tok, spread_leave_ref[...])
    state[...] = now * decay_ref[0] + dot_00(b_rows, leave.astype(BF))
    gate = gate_ref[...].astype(F32)
    sg = sigmoid(gate)
    silu = gate * sg
    v = y * silu
    gain = gain_ref[...]
    q = lax.rsqrt(jnp.mean(v * v, axis=1, keepdims=True) + EPSILON)
    vq = v * q
    out_ref[...] = (vq * gain).astype(BF)
    back = back_ref[...].astype(F32)
    e = back * gain
    cross = jnp.mean(vq * e, axis=1, keepdims=True)
    dv = q * (e - vq * cross)
    dgain_ref[...] += jnp.sum(back * vq, axis=0, keepdims=True)
    dgate_ref[...] = (dv * y * (sg * (1.0 + gate * (1.0 - sg)))).astype(BF)
    dy = dv * silu
    dy_ref[...] = dy.astype(BF)
    dskip_ref[...] += jnp.sum(dy * xc, axis=0, keepdims=True)
    ds_ref[...] += dot_00(c_rows, (dy * dot(far_ref[...].astype(BF), spread_ent_ref[...])).astype(BF))


def back_kernel(
    heads, dy_ref, z_ref, tok_ref, seg_ref, cum_ref, segrow_ref, decay_ref, skip_ref, sin_ref, ds0_ref,
    spread_ref, spread_ent_ref, spread_leave_ref, gather_ref,
    dz_ref, tokg_ref, inlog_ref, carry_ref, dstate, dxt,
):
    inner = dy_ref.shape[1]
    pair_width = 2 * inner // heads

    @pl.when(pl.program_id(0) == 0)
    def _():
        dstate[...] = ds0_ref[...]

    z = z_ref[...].astype(F32)
    sg = sigmoid(z)
    mixed = z * sg
    tok = tok_ref[...]
    tok_bf = tok.astype(BF)
    xc = mixed[:, :inner]
    dt_wide = dot(tok_bf, spread_ref[...])
    xt = (xc * dt_wide).astype(BF)
    b_rows = mixed[:, inner : inner + STATE].astype(BF)
    c_rows = mixed[:, inner + STATE :].astype(BF)
    ent = dot(tok_bf, spread_ent_ref[...])
    leave = dot(tok_bf, spread_leave_ref[...])
    dy = dy_ref[...]
    sin = sin_ref[0]
    ds = dstate[...]
    ds_bf = ds.astype(BF)
    dye = dy.astype(F32) * ent
    tokg = dot((dye * dot(c_rows, sin)).astype(BF), gather_ref[1])
    dye = dye.astype(BF)
    dc = dot_tt(dye, sin)
    xt_f = xt.astype(F32)
    dx_state = dot(b_rows, ds_bf) * leave
    dxt[...] = dx_state
    tokg = tokg + dot((xt_f * dx_state).astype(BF), gather_ref[2])
    db = dot_tt((xt_f * leave).astype(BF), ds_bf)
    carry_ref[0] = jnp.sum(ds * sin.astype(F32), axis=0, keepdims=True)
    dstate[...] = ds * decay_ref[0] + dot_00(c_rows, dye)
    mask = linked_mask(seg_ref[...], segrow_ref[...])
    cross = jnp.where(mask, dot_tt(c_rows, b_rows), 0.0)
    later = lax.broadcasted_iota(jnp.int32, (CHUNK, CHUNK), 0)
    earlier = lax.broadcasted_iota(jnp.int32, (CHUNK, CHUNK), 1)
    before = (later < earlier).astype(BF)
    upto = (later >= earlier).astype(F32)
    cum_rows = cum_ref[...]
    dcross = jnp.zeros((CHUNK, CHUNK), F32)
    for j in range(heads // 2):
        at = slice(j * pair_width, (j + 1) * pair_width)
        xp = xt[:, at]
        dys = two_heads(dy[:, at])
        lefts = []
        for i in (0, 1):
            head = 2 * j + i
            decay = decay_pair(tok, cum_rows, head, heads)
            lefts.append((cross * decay).astype(BF))
            w = dot_tt(dys[i], xp) * decay
            dcross = dcross + w
            spans = dot((w * cross).astype(BF), before)
            inlog_ref[head : head + 1, :] = jnp.sum(spans * upto, axis=0, keepdims=True)
        dxt[:, at] += dot_00(jnp.concatenate(lefts, axis=0), jnp.concatenate(dys, axis=0))
    dcross = jnp.where(mask, dcross, 0.0).astype(BF)
    dc = dc + dot(dcross, b_rows)
    db = db + dot_00(dcross, c_rows)
    dx = dxt[...]
    tokg_ref[...] = tokg + dot((xc * dx).astype(BF), gather_ref[0])
    slope = sg * (1.0 + z * (1.0 - sg))
    dz_ref[:, :inner] = ((dx * dt_wide + skip_ref[...] * dy.astype(F32)) * slope[:, :inner]).astype(BF)
    dz_ref[:, inner : inner + STATE] = (db * slope[:, inner : inner + STATE]).astype(BF)
    dz_ref[:, inner + STATE :] = (dc * slope[:, inner + STATE :]).astype(BF)


def gather_rows(shard):
    return lax.all_gather(shard, "wsh", axis=0, tiled=True)


def reduce_rows(term):
    part = lax.psum_scatter(term, "wsh", scatter_dimension=0, tiled=True)
    return lax.psum(part, "seq").astype(F32)


def on_device(
    x_in, seg_ids, g_norm, w_in, conv_w, conv_b, dt_bias, a_log, d_skip, g_gate, w_out, cotangent
):
    seqs = lax.axis_size("seq")
    me = lax.axis_index("seq")
    toks = x_in.shape[1]
    width = x_in.shape[2]
    inner = g_gate.shape[0]
    heads = dt_bias.shape[0]
    head_width = inner // heads
    conv_width = conv_w.shape[1]
    taps = conv_w.shape[0]
    chunks = toks // CHUNK
    sds = jax.ShapeDtypeStruct

    wx = gather_rows(w_in[:, inner:])
    wg = gather_rows(w_in[:, :inner])
    wo = gather_rows(w_out)

    up = [(i, i + 1) for i in range(seqs - 1)]
    down = [(i + 1, i) for i in range(seqs - 1)]
    halo = lax.ppermute(x_in[0, toks - HALO :], "seq", up)
    x_ext = jnp.concatenate([halo, x_in[0]], axis=0).astype(F32)
    r_ext = lax.rsqrt(jnp.mean(x_ext * x_ext, axis=1, keepdims=True) + EPSILON)
    normed_ext = (x_ext * r_ext * g_norm[None, :]).astype(BF)
    normed = normed_ext[HALO:]
    proj = dot(normed_ext, wx).astype(BF)
    gate = dot(normed, wg).astype(BF)
    cot = cotangent[0]
    back = dot_tt(cot, wo).astype(BF)

    start = me * toks
    seg_pad = jnp.concatenate([jnp.full((HALO,), -1, jnp.int32), seg_ids[0], jnp.full((8,), -2, jnp.int32)])
    near = lax.dynamic_slice_in_dim(seg_pad, start, toks + HALO + 8, 0)
    seg = near[HALO : HALO + toks]
    keep = jnp.stack([(near[HALO - k : HALO - k + toks] == seg) for k in range(taps)], axis=1).astype(F32)
    ext_seg = near[: toks + HALO]
    place = jnp.arange(toks + HALO)
    keep_next = jnp.stack(
        [(near[k : k + toks + HALO] == ext_seg) & (place + k < toks + HALO) for k in range(taps)], axis=1
    ).astype(F32)
    seg_before = near[HALO - 1]
    seg_f = seg.astype(F32)
    seg_chunk = seg.reshape(chunks, CHUNK)
    last_chunk = seg_chunk[:, -1]
    prev_chunk = jnp.concatenate([seg_before[None], last_chunk[:-1]])

    step_raw = proj[HALO:, conv_width:].astype(F32) + dt_bias[None, :]
    dt = jax.nn.softplus(step_raw)
    rates = -jnp.exp(a_log)
    logs = (dt * rates[None, :]).reshape(chunks, CHUNK, heads)
    tri = jnp.tril(jnp.ones((CHUNK, CHUNK), F32))
    cum = jnp.einsum("ts,csh->cth", tri, logs, precision=EXACT)
    last = cum[:, -1]
    before = jnp.einsum("cd,dh->ch", jnp.tril(jnp.ones((chunks, chunks), F32), -1), last, precision=EXACT)
    after = jnp.einsum("cd,dh->ch", jnp.triu(jnp.ones((chunks, chunks), F32), 1), last, precision=EXACT)
    total_log = jnp.sum(last, axis=0)
    enter = jnp.exp(cum) * (seg_chunk == prev_chunk[:, None])[:, :, None]
    leave_log = last[:, None] - cum
    leave = jnp.exp(leave_log) * (seg_chunk == last_chunk[:, None])[:, :, None]
    far_enter = jnp.exp(cum + before[:, None]) * (seg_chunk == seg_before)[:, :, None]
    far_leave = (
        jnp.exp(leave_log + after[:, None]) * (seg_chunk == seg[-1])[:, :, None] * dt.reshape(chunks, CHUNK, heads)
    )
    chunk_decay = jnp.exp(last) * (last_chunk == prev_chunk)[:, None]
    decay_wide = jnp.repeat(chunk_decay, head_width, axis=1)[:, None, :]
    flat = lambda v: v.reshape(toks, heads)
    tok = jnp.concatenate([dt, flat(cum), flat(enter), flat(leave)], axis=1)
    far = jnp.concatenate([flat(far_leave), flat(far_leave), flat(far_enter), flat(far_enter)], axis=1)
    cum_rows = flat(cum).T
    seg_row = seg_f[None, :]
    seg_col = seg_f[:, None]
    lanes = 4 * heads
    owner = jnp.arange(inner)[None, :] // head_width
    slot = jnp.arange(lanes)[:, None]
    spread, spread_ent, spread_leave = [(slot == owner + i * heads).astype(BF) for i in (0, 2, 3)]
    gather = jnp.stack([(slot == owner + i * heads).astype(BF).T for i in (0, 1, 2)])
    skip_wide = jnp.repeat(d_skip, head_width)[None, :]

    block = 256
    z = pl.pallas_call(
        conv_kernel,
        grid=(conv_width // block,),
        in_specs=[
            pl.BlockSpec((toks + HALO, block), lambda i: (0, i)),
            pl.BlockSpec((toks, taps), lambda i: (0, 0)),
            pl.BlockSpec((taps, block), lambda i: (0, i)),
            pl.BlockSpec((1, block), lambda i: (0, i)),
        ],
        out_specs=pl.BlockSpec((toks, block), lambda i: (0, i)),
        out_shape=sds((toks, conv_width), BF),
        scratch_shapes=[pltpu.VMEM((toks + HALO, block), F32)],
        compiler_params=params(),
        name="conv",
    )(proj, keep, conv_w, conv_b[None, :])

    rows = lambda n: pl.BlockSpec((CHUNK, n), lambda i: (i, 0))
    whole = lambda a, b: pl.BlockSpec((a, b), lambda i: (0, 0))
    own_state = pl.pallas_call(
        state_kernel,
        grid=(chunks,),
        in_specs=[rows(conv_width), rows(lanes), whole(lanes, inner)],
        out_specs=whole(STATE, inner),
        out_shape=sds((STATE, inner), F32),
        compiler_params=params(),
        name="own_state",
    )(z, far, spread)

    logs_all = lax.all_gather(total_log, "seq", axis=0)
    ids = jnp.arange(seqs)
    ends = seg_ids[0].reshape(seqs, toks)[:, -1]
    starts_before = jnp.concatenate([jnp.full((1,), -1, jnp.int32), ends[:-1]])
    between = (ids[None, :] > jnp.minimum(ids, me)[:, None]) & (ids[None, :] < jnp.maximum(ids, me)[:, None])
    gap = jnp.exp(jnp.sum(jnp.where(between[:, :, None], logs_all[None], 0.0), axis=1))
    from_past = gap * ((ids < me) & (ends == seg_before))[:, None]
    from_next = gap * ((ids > me) & (starts_before == seg[-1]))[:, None]

    def combine(own, weights):
        every = lax.all_gather(own.astype(BF), "seq", axis=0)
        wide = jnp.repeat(weights, head_width, axis=1)[:, None, :]
        return jnp.sum(every.astype(F32) * wide, axis=0)

    y_inside = pl.pallas_call(
        partial(inside_kernel, heads),
        grid=(chunks,),
        in_specs=[
            rows(conv_width), rows(lanes), rows(1),
            pl.BlockSpec((heads, CHUNK), lambda i: (0, i)),
            pl.BlockSpec((1, CHUNK), lambda i: (0, i)),
            whole(lanes, inner), whole(1, inner),
        ],
        out_specs=rows(inner),
        out_shape=sds((toks, inner), BF),
        compiler_params=params(),
        name="inside",
    )(z, tok, seg_col, cum_rows, seg_row, spread, skip_wide)
    first_state = combine(own_state, from_past)

    states, gated_out, dgate, dy, dgain, dskip_wide, own_ds = pl.pallas_call(
        gate_kernel,
        grid=(chunks,),
        in_specs=[
            rows(inner), rows(conv_width), rows(inner), rows(inner), rows(lanes), rows(lanes),
            pl.BlockSpec((1, 1, inner), lambda i: (i, 0, 0)),
            whole(1, inner), whole(STATE, inner),
            whole(lanes, inner), whole(lanes, inner), whole(lanes, inner),
        ],
        out_specs=[
            pl.BlockSpec((1, STATE, inner), lambda i: (i, 0, 0)),
            rows(inner), rows(inner), rows(inner),
            whole(1, inner), whole(1, inner), whole(STATE, inner),
        ],
        out_shape=[
            sds((chunks, STATE, inner), BF),
            sds((toks, inner), BF), sds((toks, inner), BF), sds((toks, inner), BF),
            sds((1, inner), F32), sds((1, inner), F32), sds((STATE, inner), F32),
        ],
        scratch_shapes=[pltpu.VMEM((STATE, inner), F32)],
        compiler_params=params(),
        name="gate",
    )(y_inside, z, gate, back, tok, far, decay_wide, g_gate[None, :], first_state, spread, spread_ent, spread_leave)

    last_ds = combine(own_ds, from_next)
    result = (x_ext[HALO:] + dot(gated_out, wo)).astype(BF)
    w_out_grad = reduce_rows(dot_00(gated_out, cot).astype(BF))
    gate_term = dot_00(normed, dgate).astype(BF)
    gate_rows = reduce_rows(gate_term)

    flip = lambda n: pl.BlockSpec((CHUNK, n), lambda i: (chunks - 1 - i, 0))
    dz, tokg, inlog, carry = pl.pallas_call(
        partial(back_kernel, heads),
        grid=(chunks,),
        in_specs=[
            flip(inner), flip(conv_width), flip(lanes), flip(1),
            pl.BlockSpec((heads, CHUNK), lambda i: (0, chunks - 1 - i)),
            pl.BlockSpec((1, CHUNK), lambda i: (0, chunks - 1 - i)),
            pl.BlockSpec((1, 1, inner), lambda i: (chunks - 1 - i, 0, 0)),
            whole(1, inner),
            pl.BlockSpec((1, STATE, inner), lambda i: (chunks - 1 - i, 0, 0)),
            whole(STATE, inner),
            whole(lanes, inner), whole(lanes, inner), whole(lanes, inner),
            pl.BlockSpec((3, inner, lanes), lambda i: (0, 0, 0)),
        ],
        out_specs=[
            flip(conv_width), flip(lanes),
            pl.BlockSpec((heads, CHUNK), lambda i: (0, chunks - 1 - i)),
            pl.BlockSpec((1, 1, inner), lambda i: (chunks - 1 - i, 0, 0)),
        ],
        out_shape=[
            sds((toks, conv_width), BF), sds((toks, lanes), F32), sds((heads, toks), F32),
            sds((chunks, 1, inner), F32),
        ],
        scratch_shapes=[pltpu.VMEM((STATE, inner), F32), pltpu.VMEM((CHUNK, inner), F32)],
        compiler_params=params(),
        name="scan_back",
    )(
        dy, z, tok, seg_col, cum_rows, seg_row, decay_wide, skip_wide, states, last_ds,
        spread, spread_ent, spread_leave, gather,
    )

    dxbc, dconv_w, dconv_b = pl.pallas_call(
        conv_back_kernel,
        grid=(conv_width // block,),
        in_specs=[
            pl.BlockSpec((toks, block), lambda i: (0, i)),
            pl.BlockSpec((toks + HALO, block), lambda i: (0, i)),
            pl.BlockSpec((toks, taps), lambda i: (0, 0)),
            pl.BlockSpec((toks + HALO, taps), lambda i: (0, 0)),
            pl.BlockSpec((taps, block), lambda i: (0, i)),
        ],
        out_specs=[
            pl.BlockSpec((toks + HALO, block), lambda i: (0, i)),
            pl.BlockSpec((taps, block), lambda i: (0, i)),
            pl.BlockSpec((1, block), lambda i: (0, i)),
        ],
        out_shape=[
            sds((toks + HALO, conv_width), BF), sds((taps, conv_width), F32), sds((1, conv_width), F32),
        ],
        scratch_shapes=[
            pltpu.VMEM((toks + HALO, block), F32), pltpu.VMEM((toks + HALO + 8, block), F32),
        ],
        compiler_params=params(),
        name="conv_back",
    )(dz, proj, keep, keep_next, conv_w)

    tokg = tokg.reshape(chunks, CHUNK, lanes)
    from_dx, from_enter, from_leave = [tokg[:, :, i * heads : (i + 1) * heads] for i in range(3)]
    whole_chunk = jnp.sum(carry.reshape(chunks, heads, head_width), axis=2) * chunk_decay
    dlog = (
        inlog.T.reshape(chunks, CHUNK, heads)
        + jnp.einsum("ut,cth->cuh", tri.T, from_enter, precision=EXACT)
        + jnp.einsum("us,csh->cuh", tri - jnp.eye(CHUNK, dtype=F32), from_leave, precision=EXACT)
        + whole_chunk[:, None, :]
    )
    dlog = flat(dlog)
    drate = jnp.sum(dlog * dt, axis=0)
    dstep = (flat(from_dx) + dlog * rates[None, :]) * jax.nn.sigmoid(step_raw)
    dstep_bf = dstep.astype(BF)

    dproj = jnp.concatenate([dxbc, jnp.pad(dstep_bf, ((HALO, 0), (0, 0)))], axis=1)
    x_rows = reduce_rows(dot_00(normed_ext, dproj).astype(BF))
    w_in_grad = jnp.concatenate([gate_rows, x_rows], axis=1)
    dn_ext = dot_tt(dproj, wx)
    over = lax.ppermute(dn_ext[:HALO], "seq", down)
    dn = dn_ext[HALO:] + dot_tt(dgate, wg)
    dn = dn + jnp.pad(over, ((toks - HALO, 0), (0, 0)))
    x_f = x_ext[HALO:]
    r = r_ext[HALO:]
    f = dn * g_norm[None, :]
    x_grad = cot.astype(F32) + r * f - x_f * (r * r * r) * jnp.mean(f * x_f, axis=1, keepdims=True)
    g_norm_part = jnp.sum(dn * x_f * r, axis=0)

    small = (
        g_norm_part,
        dconv_w,
        dconv_b[0],
        jnp.sum(dstep, axis=0),
        drate * rates,
        jnp.sum(dskip_wide.reshape(heads, head_width), axis=1),
        dgain[0],
    )
    small = lax.psum(small, ("seq", "wsh"))
    return (result[None], x_grad[None], small[0], w_in_grad) + tuple(small[1:]) + (w_out_grad,)


def solution(mesh):
    tokens = P("wsh", "seq", None)
    owned = P("wsh", None)
    return jax.shard_map(
        on_device,
        mesh=mesh,
        in_specs=(tokens, owned, P(), owned, P(), P(), P(), P(), P(), P(), owned, tokens),
        out_specs=(tokens, tokens, P(), owned, P(), P(), P(), P(), P(), P(), owned),
        check_vma=False,
    )
```

```python
from functools import partial

import jax
import jax.numpy as jnp
from jax import lax
from jax.experimental import pallas as pl
from jax.experimental.pallas import tpu as pltpu
from jax.sharding import PartitionSpec as P

STATE = 128
CHUNK = 128
HALO = 16
EPSILON = 1e-05
EXACT = lax.Precision.HIGHEST
BF = jnp.bfloat16
F32 = jnp.float32
VMEM_LIMIT = 56 * 1024 * 1024


def dot(a, b):
    return jnp.dot(a, b, preferred_element_type=F32)


def dot_tt(a, b):
    return lax.dot_general(a, b, (((1,), (1,)), ((), ())), preferred_element_type=F32)


def dot_00(a, b):
    return lax.dot_general(a, b, (((0,), (0,)), ((), ())), preferred_element_type=F32)


def sigmoid(v):
    return 1.0 / (1.0 + jnp.exp(-v))


def params():
    return pltpu.CompilerParams(vmem_limit_bytes=VMEM_LIMIT, dimension_semantics=("arbitrary",))


def conv_kernel(x_ref, keep_ref, w_ref, b_ref, z_ref, buf):
    rows = z_ref.shape[0]
    buf[...] = x_ref[...].astype(F32)
    taps = w_ref.shape[0]
    for start in range(0, rows, CHUNK):
        keep = keep_ref[start : start + CHUNK, :]
        total = b_ref[...] + w_ref[taps - 1 : taps, :] * buf[HALO + start : HALO + start + CHUNK, :]
        for k in range(1, taps):
            moved = buf[HALO + start - k : HALO + start - k + CHUNK, :]
            total = total + w_ref[taps - 1 - k : taps - k, :] * (moved * keep[:, k : k + 1])
        z_ref[start : start + CHUNK, :] = total.astype(BF)


def conv_back_kernel(dz_ref, x_ref, keep_ref, next_ref, w_ref, dx_ref, dw_ref, db_ref, buf, dbuf):
    rows, width = dz_ref.shape
    taps = w_ref.shape[0]
    buf[...] = x_ref[...].astype(F32)
    dbuf[0:HALO, :] = jnp.zeros((HALO, width), F32)
    dbuf[HALO : HALO + rows, :] = dz_ref[...].astype(F32)
    dbuf[HALO + rows :, :] = jnp.zeros((8, width), F32)
    sums = [jnp.zeros((1, width), F32) for _ in range(taps + 1)]
    for start in range(0, rows, CHUNK):
        keep = keep_ref[start : start + CHUNK, :]
        dz = dbuf[HALO + start : HALO + start + CHUNK, :]
        sums[taps] = sums[taps] + jnp.sum(dz, axis=0, keepdims=True)
        for k in range(taps):
            moved = buf[HALO + start - k : HALO + start - k + CHUNK, :]
            if k:
                moved = moved * keep[:, k : k + 1]
            sums[k] = sums[k] + jnp.sum(dz * moved, axis=0, keepdims=True)
    for k in range(taps):
        dw_ref[taps - 1 - k : taps - k, :] = sums[k]
    db_ref[...] = sums[taps]
    for start in range(0, rows + HALO, HALO * 13):
        count = min(HALO * 13, rows + HALO - start)
        total = w_ref[taps - 1 : taps, :] * dbuf[start : start + count, :]
        nxt = next_ref[start : start + count, :]
        for k in range(1, taps):
            moved = dbuf[start + k : start + k + count, :]
            total = total + w_ref[taps - 1 - k : taps - k, :] * (moved * nxt[:, k : k + 1])
        dx_ref[start : start + count, :] = total.astype(BF)


def state_kernel(z_ref, tok_ref, spread_ref, log_ref, s_ref, total):
    inner = s_ref.shape[1]

    @pl.when(pl.program_id(0) == 0)
    def _():
        total[...] = jnp.zeros_like(total)

    z = z_ref[:, : inner + STATE].astype(F32)
    mixed = z * sigmoid(z)
    factor = dot(tok_ref[...].astype(BF), spread_ref[...])
    total[...] += dot_00(mixed[:, inner:].astype(BF), (mixed[:, :inner] * factor).astype(BF))

    @pl.when(pl.program_id(0) == pl.num_programs(0) - 1)
    def _():
        s_ref[:STATE, :] = total[...].astype(BF)
        rest = jnp.broadcast_to(log_ref[...], (HALO, inner))
        for i in range(3):
            piece = rest.astype(BF)
            s_ref[STATE + i * HALO : STATE + (i + 1) * HALO, :] = piece
            rest = rest - piece.astype(F32)


def decay_pair(tok, cum_rows, head, heads):
    gap = tok[:, heads + head : heads + head + 1] - cum_rows[head : head + 1, :]
    return jnp.exp(jnp.minimum(gap, 0.0))


def linked_mask(seg_col, seg_row):
    later = lax.broadcasted_iota(jnp.int32, (CHUNK, CHUNK), 0)
    earlier = lax.broadcasted_iota(jnp.int32, (CHUNK, CHUNK), 1)
    return (seg_col == seg_row) & (later >= earlier)


def two_heads(pair):
    lane = lax.broadcasted_iota(jnp.int32, pair.shape, 1)
    zero = jnp.zeros_like(pair)
    half = pair.shape[1] // 2
    return jnp.where(lane < half, pair, zero), jnp.where(lane >= half, pair, zero)


def inside_kernel(heads, z_ref, tok_ref, seg_ref, cum_ref, segrow_ref, spread_ref, skip_ref, y_ref):
    inner = y_ref.shape[1]
    pair_width = 2 * inner // heads
    z = z_ref[...].astype(F32)
    mixed = z * sigmoid(z)
    tok = tok_ref[...]
    xc = mixed[:, :inner]
    xt = (xc * dot(tok.astype(BF), spread_ref[...])).astype(BF)
    b_rows = mixed[:, inner : inner + STATE].astype(BF)
    c_rows = mixed[:, inner + STATE :].astype(BF)
    mask = linked_mask(seg_ref[...], segrow_ref[...])
    cross = jnp.where(mask, dot_tt(c_rows, b_rows), 0.0)
    cum_rows = cum_ref[...]
    for j in range(heads // 2):
        at = slice(j * pair_width, (j + 1) * pair_width)
        left = [(cross * decay_pair(tok, cum_rows, 2 * j + i, heads)).astype(BF) for i in (0, 1)]
        right = two_heads(xt[:, at])
        part = dot(jnp.concatenate(left, axis=1), jnp.concatenate(right, axis=0))
        y_ref[:, at] = (part + skip_ref[:, at] * xc[:, at]).astype(BF)


def gate_kernel(
    yi_ref, z_ref, gate_ref, back_ref, tok_ref, far_ref, decay_ref, gain_ref, s0_ref,
    spread_ref, spread_ent_ref, spread_leave_ref,
    sin_ref, out_ref, dgate_ref, dy_ref, dgain_ref, dskip_ref, ds_out_ref, state, ds_ref,
):
    inner = yi_ref.shape[1]

    @pl.when(pl.program_id(0) == 0)
    def _():
        state[...] = s0_ref[...]
        dgain_ref[...] = jnp.zeros_like(dgain_ref)
        dskip_ref[...] = jnp.zeros_like(dskip_ref)
        ds_ref[...] = jnp.zeros_like(ds_ref)

    z = z_ref[...].astype(F32)
    mixed = z * sigmoid(z)
    xc = mixed[:, :inner]
    b_rows = mixed[:, inner : inner + STATE].astype(BF)
    c_rows = mixed[:, inner + STATE :].astype(BF)
    tok = tok_ref[...].astype(BF)
    now = state[...]
    now_bf = now.astype(BF)
    sin_ref[0] = now_bf
    y = yi_ref[...].astype(F32) + dot(c_rows, now_bf) * dot(tok, spread_ent_ref[...])
    leave = (xc * dot(tok, spread_ref[...])) * dot(tok, spread_leave_ref[...])
    state[...] = now * decay_ref[0] + dot_00(b_rows, leave.astype(BF))
    gate = gate_ref[...].astype(F32)
    sg = sigmoid(gate)
    silu = gate * sg
    v = y * silu
    gain = gain_ref[...]
    q = lax.rsqrt(jnp.mean(v * v, axis=1, keepdims=True) + EPSILON)
    vq = v * q
    out_ref[...] = (vq * gain).astype(BF)
    back = back_ref[...].astype(F32)
    e = back * gain
    cross = jnp.mean(vq * e, axis=1, keepdims=True)
    dv = q * (e - vq * cross)
    dgain_ref[...] += jnp.sum(back * vq, axis=0, keepdims=True)
    dgate_ref[...] = (dv * y * (sg * (1.0 + gate * (1.0 - sg)))).astype(BF)
    dy = dv * silu
    dy_ref[...] = dy.astype(BF)
    dskip_ref[...] += jnp.sum(dy * xc, axis=0, keepdims=True)
    ds_ref[...] += dot_00(c_rows, (dy * dot(far_ref[...].astype(BF), spread_ent_ref[...])).astype(BF))

    @pl.when(pl.program_id(0) == pl.num_programs(0) - 1)
    def _():
        ds_out_ref[...] = ds_ref[...].astype(BF)


def back_kernel(
    heads, dy_ref, z_ref, tok_ref, seg_ref, cum_ref, segrow_ref, decay_ref, skip_ref, sin_ref, ds0_ref,
    spread_ref, spread_ent_ref, spread_leave_ref, gather_ref,
    dz_ref, tokg_ref, inlog_ref, carry_ref, dstate, dxt,
):
    inner = dy_ref.shape[1]
    pair_width = 2 * inner // heads

    @pl.when(pl.program_id(0) == 0)
    def _():
        dstate[...] = ds0_ref[...]

    z = z_ref[...].astype(F32)
    sg = sigmoid(z)
    mixed = z * sg
    tok = tok_ref[...]
    tok_bf = tok.astype(BF)
    xc = mixed[:, :inner]
    dt_wide = dot(tok_bf, spread_ref[...])
    xt = (xc * dt_wide).astype(BF)
    b_rows = mixed[:, inner : inner + STATE].astype(BF)
    c_rows = mixed[:, inner + STATE :].astype(BF)
    ent = dot(tok_bf, spread_ent_ref[...])
    leave = dot(tok_bf, spread_leave_ref[...])
    dy = dy_ref[...]
    sin = sin_ref[0]
    ds = dstate[...]
    ds_bf = ds.astype(BF)
    dye = dy.astype(F32) * ent
    tokg = dot((dye * dot(c_rows, sin)).astype(BF), gather_ref[1])
    dye = dye.astype(BF)
    dc = dot_tt(dye, sin)
    xt_f = xt.astype(F32)
    dx_state = dot(b_rows, ds_bf) * leave
    dxt[...] = dx_state
    tokg = tokg + dot((xt_f * dx_state).astype(BF), gather_ref[2])
    db = dot_tt((xt_f * leave).astype(BF), ds_bf)
    carry_ref[0] = jnp.sum(ds * sin.astype(F32), axis=0, keepdims=True)
    dstate[...] = ds * decay_ref[0] + dot_00(c_rows, dye)
    mask = linked_mask(seg_ref[...], segrow_ref[...])
    cross = jnp.where(mask, dot_tt(c_rows, b_rows), 0.0)
    later = lax.broadcasted_iota(jnp.int32, (CHUNK, CHUNK), 0)
    earlier = lax.broadcasted_iota(jnp.int32, (CHUNK, CHUNK), 1)
    before = (later < earlier).astype(BF)
    upto = (later >= earlier).astype(F32)
    cum_rows = cum_ref[...]
    dcross = jnp.zeros((CHUNK, CHUNK), F32)
    for j in range(heads // 2):
        at = slice(j * pair_width, (j + 1) * pair_width)
        xp = xt[:, at]
        dys = two_heads(dy[:, at])
        lefts = []
        for i in (0, 1):
            head = 2 * j + i
            decay = decay_pair(tok, cum_rows, head, heads)
            lefts.append((cross * decay).astype(BF))
            w = dot_tt(dys[i], xp) * decay
            dcross = dcross + w
            spans = dot((w * cross).astype(BF), before)
            inlog_ref[head : head + 1, :] = jnp.sum(spans * upto, axis=0, keepdims=True)
        dxt[:, at] += dot_00(jnp.concatenate(lefts, axis=0), jnp.concatenate(dys, axis=0))
    dcross = jnp.where(mask, dcross, 0.0).astype(BF)
    dc = dc + dot(dcross, b_rows)
    db = db + dot_00(dcross, c_rows)
    dx = dxt[...]
    tokg_ref[...] = tokg + dot((xc * dx).astype(BF), gather_ref[0])
    slope = sg * (1.0 + z * (1.0 - sg))
    dz_ref[:, :inner] = ((dx * dt_wide + skip_ref[...] * dy.astype(F32)) * slope[:, :inner]).astype(BF)
    dz_ref[:, inner : inner + STATE] = (db * slope[:, inner : inner + STATE]).astype(BF)
    dz_ref[:, inner + STATE :] = (dc * slope[:, inner + STATE :]).astype(BF)


def add(a, b):
    return (a.astype(F32) + b.astype(F32)).astype(BF)


def across(value, axis, bit):
    count = lax.axis_size(axis)
    return lax.ppermute(value, axis, [(i, i ^ bit) for i in range(count)])


def direct():
    return lax.axis_size("wsh") == 4 and lax.axis_size("seq") == 8


def fetch(half):
    rows = half.shape[0] // 2
    by_x, by_y = across(half, "wsh", 1), across(half, "wsh", 2)
    far_a, far_b = across(by_y[:rows], "wsh", 1), across(by_x[rows:], "wsh", 2)
    return jnp.concatenate([by_x, by_y, far_a, far_b], axis=0)


def gather_weights(shard, gate_shard, out_shard):
    if not direct():
        return tuple(lax.all_gather(v, "wsh", axis=0, tiled=True) for v in (shard, gate_shard, out_shard))
    core, w = lax.axis_index("seq") % 2, lax.axis_index("wsh")
    rows = shard.shape[0]
    half, quarter = rows // 2, rows // 4
    own = lax.dynamic_slice_in_dim(shard, core * half, half, 0)
    by_x, by_y = across(own, "wsh", 1), across(own, "wsh", 2)
    far_a, far_b = across(by_y[:quarter], "wsh", 1), across(by_x[quarter:], "wsh", 2)
    far_a, far_b, gate_shard, out_shard = lax.optimization_barrier((far_a, far_b, gate_shard, out_shard))
    out = lax.dynamic_update_slice_in_dim(
        jnp.zeros((4 * rows, shard.shape[1]), shard.dtype), shard, w * rows, 0
    )
    for piece, k, extra in ((by_x, 1, 0), (by_y, 2, 0), (far_a, 3, 0), (far_b, 3, quarter)):
        other = across(piece, "seq", 1)
        for part, place in ((piece, core), (other, 1 - core)):
            out = lax.dynamic_update_slice_in_dim(out, part, (w ^ k) * rows + place * half + extra, 0)
    return (out,) + gather_two(gate_shard, out_shard)


def gather_two(gate_shard, out_shard):
    core, w = lax.axis_index("seq") % 2, lax.axis_index("wsh")
    rows = gate_shard.shape[0]
    folded = jnp.concatenate([out_shard[:rows], out_shard[rows:]], axis=1)
    mine = fetch(jnp.where(core == 0, gate_shard, folded))
    other = across(mine, "seq", 1)
    gates, outs = jnp.where(core == 0, mine, other), jnp.where(core == 0, other, mine)
    gate_full = lax.dynamic_update_slice_in_dim(
        jnp.zeros((4 * rows, gate_shard.shape[1]), BF), gate_shard, w * rows, 0
    )
    out_full = lax.dynamic_update_slice_in_dim(
        jnp.zeros((8 * rows, out_shard.shape[1]), BF), out_shard, w * 2 * rows, 0
    )
    width = out_shard.shape[1]
    for k in (1, 2, 3):
        at = slice((k - 1) * rows, k * rows)
        gate_full = lax.dynamic_update_slice_in_dim(gate_full, gates[at], (w ^ k) * rows, 0)
        for i in (0, 1):
            piece = outs[at, i * width : (i + 1) * width]
            out_full = lax.dynamic_update_slice_in_dim(out_full, piece, ((w ^ k) * 2 + i) * rows, 0)
    return gate_full, out_full


def columns_for(left, place):
    w = lax.axis_index("wsh")
    rows = left.shape[1] // 4
    half = rows // 2
    return jnp.concatenate(
        [lax.dynamic_slice_in_dim(left, (w ^ k) * rows + place * half, half, 1) for k in range(4)], axis=1
    )


def reduce_product(left, right, beside):
    if not direct():
        term = dot_00(left, right).astype(BF)
        part = lax.psum_scatter(term, "wsh", scatter_dimension=0, tiled=True)
        return lax.psum(part, "seq").astype(F32), right, beside
    me = lax.axis_index("seq")
    core, z = me % 2, me // 2
    sent = across(dot_00(columns_for(left, 1 - core), right).astype(BF), "seq", 1)
    chip = add(dot_00(columns_for(left, core), right), sent)
    chip, right = lax.optimization_barrier((chip, right))
    half = chip.shape[0] // 4
    quarter = half // 2
    a = [chip[k * half : k * half + quarter] for k in range(4)]
    b = [chip[k * half + quarter : (k + 1) * half] for k in range(4)]
    by_x = across(jnp.concatenate([a[1], a[3]], axis=0), "wsh", 1)
    by_y = across(jnp.concatenate([b[2], b[3]], axis=0), "wsh", 2)
    a2 = across(add(a[2], by_x[quarter:]), "wsh", 2)
    b1 = across(add(b[1], by_y[quarter:]), "wsh", 1)
    plane = jnp.concatenate([add(add(a[0], by_x[:quarter]), a2), add(add(b[0], by_y[:quarter]), b1)], axis=0)
    plane, beside = lax.optimization_barrier((plane, beside))
    z_low, z_high = z % 2, z // 2
    cut = lambda v, i: lax.dynamic_slice_in_dim(v, i * (v.shape[0] // 2), v.shape[0] // 2, 0)
    join = lambda own, other, i: jnp.where(
        i == 0, jnp.concatenate([own, other], axis=0), jnp.concatenate([other, own], axis=0)
    )
    one = add(cut(plane, z_low), across(cut(plane, 1 - z_low), "seq", 2))
    two = add(cut(one, z_high), across(cut(one, 1 - z_high), "seq", 4))
    one = join(two, across(two, "seq", 4), z_high)
    all_z = join(one, across(one, "seq", 2), z_low)
    return join(all_z, across(all_z, "seq", 1), core).astype(F32), right, beside


def core_sums(normed, dgate, gated_out, cot):
    planes = lax.axis_size("wsh")
    core = lax.axis_index("seq") % 2
    half = normed.shape[1] // planes // 2

    def product(left, start, right):
        rows = left.shape[1] // planes
        picked = [lax.dynamic_slice_in_dim(left, w * rows + start, half, 1) for w in range(planes)]
        return dot_00(jnp.concatenate(picked, axis=1), right).astype(BF)

    def part(place):
        outs = [product(gated_out, (2 * place + i) * half, cot) for i in (0, 1)]
        return jnp.concatenate([product(normed, place * half, dgate)] + outs, axis=1)

    sent = across(part(1 - core), "seq", 1)
    return add(part(core), sent)


def sum_over(value, axis, groups, count):
    every = lax.all_to_all(
        value, axis, split_axis=0, concat_axis=0, tiled=True, axis_index_groups=groups
    )
    rows = every.shape[0] // count
    total = every[:rows].astype(F32)
    for i in range(1, count):
        total = total + every[i * rows : (i + 1) * rows].astype(F32)
    return total.astype(BF)


def same_core():
    seqs = lax.axis_size("seq")
    return [list(range(i, seqs, 2)) for i in (0, 1)]


def spread_back(part, inner):
    core = lax.axis_index("seq") % 2
    other = across(part, "seq", 1)
    low, high = jnp.where(core == 0, part, other), jnp.where(core == 0, other, part)
    width = (part.shape[1] - inner) // 2
    outs = [v[:, inner + i * width : inner + (i + 1) * width] for v in (low, high) for i in (0, 1)]
    return (
        jnp.concatenate([low[:, :inner], high[:, :inner]], axis=0).astype(F32),
        jnp.concatenate(outs, axis=0).astype(F32),
    )


def sum_small(parts):
    if not direct():
        return lax.psum(parts, ("seq", "wsh"))
    flat = jnp.concatenate([p.reshape(-1) for p in parts])
    size = flat.shape[0]
    flat = jnp.pad(flat, (0, -size % 1024)).reshape(-1, 128)
    for axis, bit in (("seq", 1), ("seq", 2), ("seq", 4), ("wsh", 1), ("wsh", 2)):
        flat = flat + across(flat, axis, bit)
    flat = flat.reshape(-1)
    out, at = [], 0
    for p in parts:
        out.append(flat[at : at + p.size].reshape(p.shape))
        at += p.size
    return tuple(out)


def on_device(
    x_in, seg_ids, g_norm, w_in, conv_w, conv_b, dt_bias, a_log, d_skip, g_gate, w_out, cotangent
):
    seqs = lax.axis_size("seq")
    me = lax.axis_index("seq")
    toks = x_in.shape[1]
    width = x_in.shape[2]
    inner = g_gate.shape[0]
    heads = dt_bias.shape[0]
    head_width = inner // heads
    conv_width = conv_w.shape[1]
    taps = conv_w.shape[0]
    chunks = toks // CHUNK
    sds = jax.ShapeDtypeStruct

    used = w_in.shape[1] - inner
    wx, wg, wo = gather_weights(jnp.pad(w_in[:, inner:], ((0, 0), (0, -used % 128))), w_in[:, :inner], w_out)

    up = [(i, i + 1) for i in range(seqs - 1)]
    down = [(i + 1, i) for i in range(seqs - 1)]
    halo = lax.ppermute(x_in[0, toks - HALO :], "seq", up)
    x_ext = jnp.concatenate([halo, x_in[0]], axis=0).astype(F32)
    r_ext = lax.rsqrt(jnp.mean(x_ext * x_ext, axis=1, keepdims=True) + EPSILON)
    start = me * toks
    seg_pad = jnp.concatenate([jnp.full((HALO,), -1, jnp.int32), seg_ids[0], jnp.full((8,), -2, jnp.int32)])
    near = lax.dynamic_slice_in_dim(seg_pad, start, toks + HALO + 8, 0)
    seg = near[HALO : HALO + toks]
    keep = jnp.stack([(near[HALO - k : HALO - k + toks] == seg) for k in range(taps)], axis=1).astype(F32)
    ext_seg = near[: toks + HALO]
    place = jnp.arange(toks + HALO)
    keep_next = jnp.stack(
        [(near[k : k + toks + HALO] == ext_seg) & (place + k < toks + HALO) for k in range(taps)], axis=1
    ).astype(F32)
    seg_before = near[HALO - 1]
    seg_f = seg.astype(F32)
    seg_chunk = seg.reshape(chunks, CHUNK)
    last_chunk = seg_chunk[:, -1]
    prev_chunk = jnp.concatenate([seg_before[None], last_chunk[:-1]])
    lanes = 4 * heads
    owner = jnp.arange(inner)[None, :] // head_width
    slot = jnp.arange(lanes)[:, None]
    spread, spread_ent, spread_leave = [(slot == owner + i * heads).astype(BF) for i in (0, 2, 3)]
    gather = jnp.stack([(slot == owner + i * heads).astype(BF).T for i in (0, 1, 2)])
    skip_wide = jnp.repeat(d_skip, head_width)[None, :]
    tri = jnp.tril(jnp.ones((CHUNK, CHUNK), F32))
    seg_row = seg_f[None, :]
    seg_col = seg_f[:, None]
    fixed = (keep, keep_next, seg_row, seg_col, spread, spread_ent, spread_leave, gather, skip_wide)
    x_ext, fixed = lax.optimization_barrier((x_ext, fixed))
    keep, keep_next, seg_row, seg_col, spread, spread_ent, spread_leave, gather, skip_wide = fixed
    normed_ext = (x_ext * r_ext * g_norm[None, :]).astype(BF)
    normed = normed_ext[HALO:]
    proj = dot(normed_ext, wx).astype(BF)
    gate = dot(normed, wg).astype(BF)
    cot = cotangent[0]
    back = dot_tt(cot, wo).astype(BF)

    step_raw = proj[HALO:, conv_width : conv_width + heads].astype(F32) + dt_bias[None, :]
    dt = jax.nn.softplus(step_raw)
    rates = -jnp.exp(a_log)
    logs = (dt * rates[None, :]).reshape(chunks, CHUNK, heads)
    cum = jnp.einsum("ts,csh->cth", tri, logs, precision=EXACT)
    last = cum[:, -1]
    before = jnp.einsum("cd,dh->ch", jnp.tril(jnp.ones((chunks, chunks), F32), -1), last, precision=EXACT)
    after = jnp.einsum("cd,dh->ch", jnp.triu(jnp.ones((chunks, chunks), F32), 1), last, precision=EXACT)
    total_log = jnp.sum(last, axis=0)
    enter = jnp.exp(cum) * (seg_chunk == prev_chunk[:, None])[:, :, None]
    leave_log = last[:, None] - cum
    leave = jnp.exp(leave_log) * (seg_chunk == last_chunk[:, None])[:, :, None]
    far_enter = jnp.exp(cum + before[:, None]) * (seg_chunk == seg_before)[:, :, None]
    far_leave = (
        jnp.exp(leave_log + after[:, None]) * (seg_chunk == seg[-1])[:, :, None] * dt.reshape(chunks, CHUNK, heads)
    )
    chunk_decay = jnp.exp(last) * (last_chunk == prev_chunk)[:, None]
    decay_wide = jnp.repeat(chunk_decay, head_width, axis=1)[:, None, :]
    flat = lambda v: v.reshape(toks, heads)
    tok = jnp.concatenate([dt, flat(cum), flat(enter), flat(leave)], axis=1)
    far = jnp.concatenate([flat(far_leave), flat(far_leave), flat(far_enter), flat(far_enter)], axis=1)
    cum_rows = flat(cum).T
    block = 256
    z = pl.pallas_call(
        conv_kernel,
        grid=(conv_width // block,),
        in_specs=[
            pl.BlockSpec((toks + HALO, block), lambda i: (0, i)),
            pl.BlockSpec((toks, taps), lambda i: (0, 0)),
            pl.BlockSpec((taps, block), lambda i: (0, i)),
            pl.BlockSpec((1, block), lambda i: (0, i)),
        ],
        out_specs=pl.BlockSpec((toks, block), lambda i: (0, i)),
        out_shape=sds((toks, conv_width), BF),
        scratch_shapes=[pltpu.VMEM((toks + HALO, block), F32)],
        compiler_params=params(),
        name="conv",
    )(proj, keep, conv_w, conv_b[None, :])

    rows = lambda n: pl.BlockSpec((CHUNK, n), lambda i: (i, 0))
    whole = lambda a, b: pl.BlockSpec((a, b), lambda i: (0, 0))
    own_state = pl.pallas_call(
        state_kernel,
        grid=(chunks,),
        in_specs=[rows(conv_width), rows(lanes), whole(lanes, inner), whole(1, inner)],
        out_specs=whole(STATE + 3 * HALO, inner),
        out_shape=sds((STATE + 3 * HALO, inner), BF),
        scratch_shapes=[pltpu.VMEM((STATE, inner), F32)],
        compiler_params=params(),
        name="own_state",
    )(z, far, spread, jnp.repeat(total_log, head_width)[None, :])

    every = lax.all_gather(own_state, "seq", axis=0)
    logs_all = sum(every[:, STATE + i * HALO].astype(F32) for i in range(3))
    ids = jnp.arange(seqs)
    ends = seg_ids[0].reshape(seqs, toks)[:, -1]
    starts_before = jnp.concatenate([jnp.full((1,), -1, jnp.int32), ends[:-1]])
    between = (ids[None, :] > jnp.minimum(ids, me)[:, None]) & (ids[None, :] < jnp.maximum(ids, me)[:, None])
    gap = jnp.exp(jnp.sum(jnp.where(between[:, :, None], logs_all[None], 0.0), axis=1))
    from_past = gap * ((ids < me) & (ends == seg_before))[:, None]
    from_next = gap * ((ids > me) & (starts_before == seg[-1]))[:, None]

    def combine(states, weights):
        return jnp.sum(states[:, :STATE].astype(F32) * weights[:, None, :], axis=0)

    y_inside = pl.pallas_call(
        partial(inside_kernel, heads),
        grid=(chunks,),
        in_specs=[
            rows(conv_width), rows(lanes), rows(1),
            pl.BlockSpec((heads, CHUNK), lambda i: (0, i)),
            pl.BlockSpec((1, CHUNK), lambda i: (0, i)),
            whole(lanes, inner), whole(1, inner),
        ],
        out_specs=rows(inner),
        out_shape=sds((toks, inner), BF),
        compiler_params=params(),
        name="inside",
    )(z, tok, seg_col, cum_rows, seg_row, spread, skip_wide)
    first_state = combine(every, from_past)

    states, gated_out, dgate, dy, dgain, dskip_wide, own_ds = pl.pallas_call(
        gate_kernel,
        grid=(chunks,),
        in_specs=[
            rows(inner), rows(conv_width), rows(inner), rows(inner), rows(lanes), rows(lanes),
            pl.BlockSpec((1, 1, inner), lambda i: (i, 0, 0)),
            whole(1, inner), whole(STATE, inner),
            whole(lanes, inner), whole(lanes, inner), whole(lanes, inner),
        ],
        out_specs=[
            pl.BlockSpec((1, STATE, inner), lambda i: (i, 0, 0)),
            rows(inner), rows(inner), rows(inner),
            whole(1, inner), whole(1, inner), whole(STATE, inner),
        ],
        out_shape=[
            sds((chunks, STATE, inner), BF),
            sds((toks, inner), BF), sds((toks, inner), BF), sds((toks, inner), BF),
            sds((1, inner), F32), sds((1, inner), F32), sds((STATE, inner), BF),
        ],
        scratch_shapes=[pltpu.VMEM((STATE, inner), F32)] * 2,
        compiler_params=params(),
        name="gate",
    )(y_inside, z, gate, back, tok, far, decay_wide, g_gate[None, :], first_state, spread, spread_ent, spread_leave)

    last_ds = combine(lax.all_gather(own_ds, "seq", axis=0), from_next)
    result = (x_ext[HALO:] + dot(gated_out, wo)).astype(BF)
    sums = core_sums(normed, dgate, gated_out, cot)
    last_ds, sums = lax.optimization_barrier((last_ds, sums))
    sums = sum_over(sums, "wsh", None, lax.axis_size("wsh"))

    flip = lambda n: pl.BlockSpec((CHUNK, n), lambda i: (chunks - 1 - i, 0))
    dz, tokg, inlog, carry = pl.pallas_call(
        partial(back_kernel, heads),
        grid=(chunks,),
        in_specs=[
            flip(inner), flip(conv_width), flip(lanes), flip(1),
            pl.BlockSpec((heads, CHUNK), lambda i: (0, chunks - 1 - i)),
            pl.BlockSpec((1, CHUNK), lambda i: (0, chunks - 1 - i)),
            pl.BlockSpec((1, 1, inner), lambda i: (chunks - 1 - i, 0, 0)),
            whole(1, inner),
            pl.BlockSpec((1, STATE, inner), lambda i: (chunks - 1 - i, 0, 0)),
            whole(STATE, inner),
            whole(lanes, inner), whole(lanes, inner), whole(lanes, inner),
            pl.BlockSpec((3, inner, lanes), lambda i: (0, 0, 0)),
        ],
        out_specs=[
            flip(conv_width), flip(lanes),
            pl.BlockSpec((heads, CHUNK), lambda i: (0, chunks - 1 - i)),
            pl.BlockSpec((1, 1, inner), lambda i: (chunks - 1 - i, 0, 0)),
        ],
        out_shape=[
            sds((toks, conv_width), BF), sds((toks, lanes), F32), sds((heads, toks), F32),
            sds((chunks, 1, inner), F32),
        ],
        scratch_shapes=[pltpu.VMEM((STATE, inner), F32), pltpu.VMEM((CHUNK, inner), F32)],
        compiler_params=params(),
        name="scan_back",
    )(
        dy, z, tok, seg_col, cum_rows, seg_row, decay_wide, skip_wide, states, last_ds,
        spread, spread_ent, spread_leave, gather,
    )

    dz, sums = lax.optimization_barrier((dz, sums))
    sums = sum_over(sums, "seq", same_core(), seqs // 2)

    dxbc, dconv_w, dconv_b = pl.pallas_call(
        conv_back_kernel,
        grid=(conv_width // block,),
        in_specs=[
            pl.BlockSpec((toks, block), lambda i: (0, i)),
            pl.BlockSpec((toks + HALO, block), lambda i: (0, i)),
            pl.BlockSpec((toks, taps), lambda i: (0, 0)),
            pl.BlockSpec((toks + HALO, taps), lambda i: (0, 0)),
            pl.BlockSpec((taps, block), lambda i: (0, i)),
        ],
        out_specs=[
            pl.BlockSpec((toks + HALO, block), lambda i: (0, i)),
            pl.BlockSpec((taps, block), lambda i: (0, i)),
            pl.BlockSpec((1, block), lambda i: (0, i)),
        ],
        out_shape=[
            sds((toks + HALO, conv_width), BF), sds((taps, conv_width), F32), sds((1, conv_width), F32),
        ],
        scratch_shapes=[
            pltpu.VMEM((toks + HALO, block), F32), pltpu.VMEM((toks + HALO + 8, block), F32),
        ],
        compiler_params=params(),
        name="conv_back",
    )(dz, proj, keep, keep_next, conv_w)

    tokg = tokg.reshape(chunks, CHUNK, lanes)
    from_dx, from_enter, from_leave = [tokg[:, :, i * heads : (i + 1) * heads] for i in range(3)]
    whole_chunk = jnp.sum(carry.reshape(chunks, heads, head_width), axis=2) * chunk_decay
    dlog = (
        inlog.T.reshape(chunks, CHUNK, heads)
        + jnp.einsum("ut,cth->cuh", tri.T, from_enter, precision=EXACT)
        + jnp.einsum("us,csh->cuh", tri - jnp.eye(CHUNK, dtype=F32), from_leave, precision=EXACT)
        + whole_chunk[:, None, :]
    )
    dlog = flat(dlog)
    drate = jnp.sum(dlog * dt, axis=0)
    dstep = (flat(from_dx) + dlog * rates[None, :]) * jax.nn.sigmoid(step_raw)
    dstep_bf = dstep.astype(BF)

    dxbc, sums = lax.optimization_barrier((dxbc, sums))
    sums = lax.all_gather(sums, "seq", axis=0, tiled=True, axis_index_groups=same_core())
    dproj = jnp.concatenate([dxbc, jnp.pad(dstep_bf, ((HALO, 0), (0, -heads % 128)))], axis=1)
    x_rows, dproj, sums = reduce_product(normed_ext, dproj, sums)
    x_rows = x_rows[:, :used]
    gate_rows, w_out_grad = spread_back(sums, inner)
    w_in_grad = jnp.concatenate([gate_rows, x_rows], axis=1)
    dn_ext = dot_tt(dproj, wx)
    over = lax.ppermute(dn_ext[:HALO], "seq", down)
    dn = dn_ext[HALO:] + dot_tt(dgate, wg)
    dn = dn + jnp.pad(over, ((toks - HALO, 0), (0, 0)))
    x_f = x_ext[HALO:]
    r = r_ext[HALO:]
    f = dn * g_norm[None, :]
    x_grad = cot.astype(F32) + r * f - x_f * (r * r * r) * jnp.mean(f * x_f, axis=1, keepdims=True)
    g_norm_part = jnp.sum(dn * x_f * r, axis=0)

    small = (
        g_norm_part,
        dconv_w,
        dconv_b[0],
        jnp.sum(dstep, axis=0),
        drate * rates,
        jnp.sum(dskip_wide.reshape(heads, head_width), axis=1),
        dgain[0],
    )
    small = sum_small(small)
    return (result[None], x_grad[None], small[0], w_in_grad) + tuple(small[1:]) + (w_out_grad,)


def solution(mesh):
    tokens = P("wsh", "seq", None)
    owned = P("wsh", None)
    return jax.shard_map(
        on_device,
        mesh=mesh,
        in_specs=(tokens, owned, P(), owned, P(), P(), P(), P(), P(), P(), owned, tokens),
        out_specs=(tokens, tokens, P(), owned, P(), P(), P(), P(), P(), P(), owned),
        check_vma=False,
    )
```

```python
from functools import partial

import jax
import jax.numpy as jnp
from jax import lax
from jax.experimental import pallas as pl
from jax.experimental.pallas import tpu as pltpu
from jax.sharding import PartitionSpec as P

STATE = 128
CHUNK = 128
HALO = 16
EPSILON = 1e-05
EXACT = lax.Precision.HIGHEST
BF = jnp.bfloat16
F32 = jnp.float32
VMEM_LIMIT = 56 * 1024 * 1024


def dot(a, b):
    return jnp.dot(a, b, preferred_element_type=F32)


def dot_tt(a, b):
    return lax.dot_general(a, b, (((1,), (1,)), ((), ())), preferred_element_type=F32)


def dot_00(a, b):
    return lax.dot_general(a, b, (((0,), (0,)), ((), ())), preferred_element_type=F32)


def sigmoid(v):
    return 0.5 + 0.5 * jnp.tanh(0.5 * v)


def params():
    return pltpu.CompilerParams(vmem_limit_bytes=VMEM_LIMIT, dimension_semantics=("arbitrary",))


def conv_kernel(x_ref, keep_ref, w_ref, b_ref, mixed_ref, slope_ref, buf):
    rows = mixed_ref.shape[0]
    buf[...] = x_ref[...].astype(F32)
    taps = w_ref.shape[0]
    for start in range(0, rows, CHUNK):
        keep = keep_ref[start : start + CHUNK, :]
        total = b_ref[...] + w_ref[taps - 1 : taps, :] * buf[HALO + start : HALO + start + CHUNK, :]
        for k in range(1, taps):
            moved = buf[HALO + start - k : HALO + start - k + CHUNK, :]
            total = total + w_ref[taps - 1 - k : taps - k, :] * (moved * keep[:, k : k + 1])
        sg = sigmoid(total)
        mixed = total * sg
        mixed_ref[start : start + CHUNK, :] = mixed.astype(BF)
        slope_ref[start : start + CHUNK, :] = (sg + mixed * (1.0 - sg)).astype(BF)


def conv_back_kernel(dz_ref, x_ref, keep_ref, next_ref, w_ref, dx_ref, dw_ref, db_ref, buf, dbuf):
    rows, width = dz_ref.shape
    taps = w_ref.shape[0]
    buf[...] = x_ref[...].astype(F32)
    dbuf[0:HALO, :] = jnp.zeros((HALO, width), F32)
    dbuf[HALO : HALO + rows, :] = dz_ref[...].astype(F32)
    dbuf[HALO + rows :, :] = jnp.zeros((8, width), F32)
    sums = [jnp.zeros((1, width), F32) for _ in range(taps + 1)]
    for start in range(0, rows, CHUNK):
        keep = keep_ref[start : start + CHUNK, :]
        dz = dbuf[HALO + start : HALO + start + CHUNK, :]
        sums[taps] = sums[taps] + jnp.sum(dz, axis=0, keepdims=True)
        for k in range(taps):
            moved = buf[HALO + start - k : HALO + start - k + CHUNK, :]
            if k:
                moved = moved * keep[:, k : k + 1]
            sums[k] = sums[k] + jnp.sum(dz * moved, axis=0, keepdims=True)
    for k in range(taps):
        dw_ref[taps - 1 - k : taps - k, :] = sums[k]
    db_ref[...] = sums[taps]
    for start in range(0, rows + HALO, HALO * 13):
        count = min(HALO * 13, rows + HALO - start)
        total = w_ref[taps - 1 : taps, :] * dbuf[start : start + count, :]
        nxt = next_ref[start : start + count, :]
        for k in range(1, taps):
            moved = dbuf[start + k : start + k + count, :]
            total = total + w_ref[taps - 1 - k : taps - k, :] * (moved * nxt[:, k : k + 1])
        dx_ref[start : start + count, :] = total.astype(BF)


def state_kernel(mixed_ref, tok_ref, spread_ref, log_ref, s_ref, total):
    inner = s_ref.shape[1]

    @pl.when(pl.program_id(0) == 0)
    def _():
        total[...] = jnp.zeros_like(total)

    factor = dot(tok_ref[...].astype(BF), spread_ref[...])
    left = (mixed_ref[:, :inner].astype(F32) * factor).astype(BF)
    total[...] += dot_00(mixed_ref[:, inner : inner + STATE], left)

    @pl.when(pl.program_id(0) == pl.num_programs(0) - 1)
    def _():
        s_ref[:STATE, :] = total[...].astype(BF)
        rest = jnp.broadcast_to(log_ref[...], (HALO, inner))
        for i in range(3):
            piece = rest.astype(BF)
            s_ref[STATE + i * HALO : STATE + (i + 1) * HALO, :] = piece
            rest = rest - piece.astype(F32)


def decay_pair(tok, cum_rows, head, heads):
    gap = tok[:, heads + head : heads + head + 1] - cum_rows[head : head + 1, :]
    return jnp.exp(jnp.minimum(gap, 0.0))


def linked_mask(seg_col, seg_row):
    later = lax.broadcasted_iota(jnp.int32, (CHUNK, CHUNK), 0)
    earlier = lax.broadcasted_iota(jnp.int32, (CHUNK, CHUNK), 1)
    return (seg_col == seg_row) & (later >= earlier)


def two_heads(pair):
    lane = lax.broadcasted_iota(jnp.int32, pair.shape, 1)
    zero = jnp.zeros_like(pair)
    half = pair.shape[1] // 2
    return jnp.where(lane < half, pair, zero), jnp.where(lane >= half, pair, zero)


def inside_kernel(heads, mixed_ref, tok_ref, seg_ref, cum_ref, segrow_ref, spread_ref, skip_ref, y_ref):
    inner = y_ref.shape[1]
    pair_width = 2 * inner // heads
    tok = tok_ref[...]
    xc = mixed_ref[:, :inner].astype(F32)
    xt = (xc * dot(tok.astype(BF), spread_ref[...])).astype(BF)
    b_rows = mixed_ref[:, inner : inner + STATE]
    c_rows = mixed_ref[:, inner + STATE :]
    mask = linked_mask(seg_ref[...], segrow_ref[...])
    cross = jnp.where(mask, dot_tt(c_rows, b_rows), 0.0)
    cum_rows = cum_ref[...]
    for j in range(heads // 2):
        at = slice(j * pair_width, (j + 1) * pair_width)
        left = [(cross * decay_pair(tok, cum_rows, 2 * j + i, heads)).astype(BF) for i in (0, 1)]
        right = two_heads(xt[:, at])
        part = dot(jnp.concatenate(left, axis=1), jnp.concatenate(right, axis=0))
        y_ref[:, at] = (part + skip_ref[:, at] * xc[:, at]).astype(BF)


def gate_kernel(
    yi_ref, mixed_ref, gate_ref, back_ref, tok_ref, far_ref, decay_ref, gain_ref, s0_ref,
    spread_ref, spread_ent_ref, spread_leave_ref,
    sin_ref, out_ref, dgate_ref, dy_ref, dgain_ref, dskip_ref, ds_out_ref, state, ds_ref,
):
    inner = yi_ref.shape[1]

    @pl.when(pl.program_id(0) == 0)
    def _():
        state[...] = s0_ref[...]
        dgain_ref[...] = jnp.zeros_like(dgain_ref)
        dskip_ref[...] = jnp.zeros_like(dskip_ref)
        ds_ref[...] = jnp.zeros_like(ds_ref)

    xc = mixed_ref[:, :inner].astype(F32)
    b_rows = mixed_ref[:, inner : inner + STATE]
    c_rows = mixed_ref[:, inner + STATE :]
    tok = tok_ref[...].astype(BF)
    now = state[...]
    now_bf = now.astype(BF)
    sin_ref[0] = now_bf
    y = yi_ref[...].astype(F32) + dot(c_rows, now_bf) * dot(tok, spread_ent_ref[...])
    leave = (xc * dot(tok, spread_ref[...])) * dot(tok, spread_leave_ref[...])
    state[...] = now * decay_ref[0] + dot_00(b_rows, leave.astype(BF))
    gate = gate_ref[...].astype(F32)
    sg = sigmoid(gate)
    silu = gate * sg
    v = y * silu
    gain = gain_ref[...]
    q = lax.rsqrt(jnp.mean(v * v, axis=1, keepdims=True) + EPSILON)
    vq = v * q
    out_ref[...] = (vq * gain).astype(BF)
    back = back_ref[...].astype(F32)
    e = back * gain
    cross = jnp.mean(vq * e, axis=1, keepdims=True)
    dv = q * (e - vq * cross)
    dgain_ref[...] += jnp.sum(back * vq, axis=0, keepdims=True)
    dgate_ref[...] = (dv * y * (sg * (1.0 + gate * (1.0 - sg)))).astype(BF)
    dy = dv * silu
    dy_ref[...] = dy.astype(BF)
    dskip_ref[...] += jnp.sum(dy * xc, axis=0, keepdims=True)
    ds_ref[...] += dot_00(c_rows, (dy * dot(far_ref[...].astype(BF), spread_ent_ref[...])).astype(BF))

    @pl.when(pl.program_id(0) == pl.num_programs(0) - 1)
    def _():
        ds_out_ref[...] = ds_ref[...].astype(BF)


def back_kernel(
    heads, dy_ref, mixed_ref, slope_ref, tok_ref, seg_ref, cum_ref, segrow_ref, decay_ref, skip_ref, sin_ref, ds0_ref,
    spread_ref, spread_ent_ref, spread_leave_ref, gather_ref,
    dz_ref, tokg_ref, inlog_ref, carry_ref, dstate, dxt,
):
    inner = dy_ref.shape[1]
    pair_width = 2 * inner // heads

    @pl.when(pl.program_id(0) == 0)
    def _():
        dstate[...] = ds0_ref[...]

    tok = tok_ref[...]
    tok_bf = tok.astype(BF)
    xc = mixed_ref[:, :inner].astype(F32)
    dt_wide = dot(tok_bf, spread_ref[...])
    xt = (xc * dt_wide).astype(BF)
    b_rows = mixed_ref[:, inner : inner + STATE]
    c_rows = mixed_ref[:, inner + STATE :]
    ent = dot(tok_bf, spread_ent_ref[...])
    leave = dot(tok_bf, spread_leave_ref[...])
    dy = dy_ref[...]
    sin = sin_ref[0]
    ds = dstate[...]
    ds_bf = ds.astype(BF)
    dye = dy.astype(F32) * ent
    tokg = dot((dye * dot(c_rows, sin)).astype(BF), gather_ref[1])
    dye = dye.astype(BF)
    dc = dot_tt(dye, sin)
    xt_f = xt.astype(F32)
    dx_state = dot(b_rows, ds_bf) * leave
    dxt[...] = dx_state
    tokg = tokg + dot((xt_f * dx_state).astype(BF), gather_ref[2])
    db = dot_tt((xt_f * leave).astype(BF), ds_bf)
    carry_ref[0] = jnp.sum(ds * sin.astype(F32), axis=0, keepdims=True)
    dstate[...] = ds * decay_ref[0] + dot_00(c_rows, dye)
    mask = linked_mask(seg_ref[...], segrow_ref[...])
    cross = jnp.where(mask, dot_tt(c_rows, b_rows), 0.0)
    later = lax.broadcasted_iota(jnp.int32, (CHUNK, CHUNK), 0)
    earlier = lax.broadcasted_iota(jnp.int32, (CHUNK, CHUNK), 1)
    before = (later < earlier).astype(BF)
    upto = (later >= earlier).astype(F32)
    cum_rows = cum_ref[...]
    dcross = jnp.zeros((CHUNK, CHUNK), F32)
    for j in range(heads // 2):
        at = slice(j * pair_width, (j + 1) * pair_width)
        xp = xt[:, at]
        dys = two_heads(dy[:, at])
        lefts = []
        for i in (0, 1):
            head = 2 * j + i
            decay = decay_pair(tok, cum_rows, head, heads)
            lefts.append((cross * decay).astype(BF))
            w = dot_tt(dys[i], xp) * decay
            dcross = dcross + w
            spans = dot((w * cross).astype(BF), before)
            inlog_ref[head : head + 1, :] = jnp.sum(spans * upto, axis=0, keepdims=True)
        dxt[:, at] += dot_00(jnp.concatenate(lefts, axis=0), jnp.concatenate(dys, axis=0))
    dcross = jnp.where(mask, dcross, 0.0).astype(BF)
    dc = dc + dot(dcross, b_rows)
    db = db + dot_00(dcross, c_rows)
    dx = dxt[...]
    tokg_ref[...] = tokg + dot((xc * dx).astype(BF), gather_ref[0])
    slope = slope_ref[...].astype(F32)
    dz_ref[:, :inner] = ((dx * dt_wide + skip_ref[...] * dy.astype(F32)) * slope[:, :inner]).astype(BF)
    dz_ref[:, inner : inner + STATE] = (db * slope[:, inner : inner + STATE]).astype(BF)
    dz_ref[:, inner + STATE :] = (dc * slope[:, inner + STATE :]).astype(BF)


def add(a, b):
    return (a.astype(F32) + b.astype(F32)).astype(BF)


def across(value, axis, bit):
    count = lax.axis_size(axis)
    return lax.ppermute(value, axis, [(i, i ^ bit) for i in range(count)])


def direct():
    return lax.axis_size("wsh") == 4 and lax.axis_size("seq") == 8


def fetch(half):
    rows = half.shape[0] // 2
    by_x, by_y = across(half, "wsh", 1), across(half, "wsh", 2)
    far_a, far_b = across(by_y[:rows], "wsh", 1), across(by_x[rows:], "wsh", 2)
    return jnp.concatenate([by_x, by_y, far_a, far_b], axis=0)


def gather_weights(shard, gate_shard, out_shard):
    if not direct():
        return tuple(lax.all_gather(v, "wsh", axis=0, tiled=True) for v in (shard, gate_shard, out_shard))
    core, w = lax.axis_index("seq") % 2, lax.axis_index("wsh")
    rows = shard.shape[0]
    half, quarter = rows // 2, rows // 4
    own = lax.dynamic_slice_in_dim(shard, core * half, half, 0)
    by_x, by_y = across(own, "wsh", 1), across(own, "wsh", 2)
    far_a, far_b = across(by_y[:quarter], "wsh", 1), across(by_x[quarter:], "wsh", 2)
    far_a, far_b, gate_shard, out_shard = lax.optimization_barrier((far_a, far_b, gate_shard, out_shard))
    out = lax.dynamic_update_slice_in_dim(
        jnp.zeros((4 * rows, shard.shape[1]), shard.dtype), shard, w * rows, 0
    )
    for piece, k, extra in ((by_x, 1, 0), (by_y, 2, 0), (far_a, 3, 0), (far_b, 3, quarter)):
        other = across(piece, "seq", 1)
        for part, place in ((piece, core), (other, 1 - core)):
            out = lax.dynamic_update_slice_in_dim(out, part, (w ^ k) * rows + place * half + extra, 0)
    return (out,) + gather_two(gate_shard, out_shard)


def gather_two(gate_shard, out_shard):
    core, w = lax.axis_index("seq") % 2, lax.axis_index("wsh")
    rows = gate_shard.shape[0]
    folded = jnp.concatenate([out_shard[:rows], out_shard[rows:]], axis=1)
    mine = fetch(jnp.where(core == 0, gate_shard, folded))
    other = across(mine, "seq", 1)
    gates, outs = jnp.where(core == 0, mine, other), jnp.where(core == 0, other, mine)
    gate_full = lax.dynamic_update_slice_in_dim(
        jnp.zeros((4 * rows, gate_shard.shape[1]), BF), gate_shard, w * rows, 0
    )
    out_full = lax.dynamic_update_slice_in_dim(
        jnp.zeros((8 * rows, out_shard.shape[1]), BF), out_shard, w * 2 * rows, 0
    )
    width = out_shard.shape[1]
    for k in (1, 2, 3):
        at = slice((k - 1) * rows, k * rows)
        gate_full = lax.dynamic_update_slice_in_dim(gate_full, gates[at], (w ^ k) * rows, 0)
        for i in (0, 1):
            piece = outs[at, i * width : (i + 1) * width]
            out_full = lax.dynamic_update_slice_in_dim(out_full, piece, ((w ^ k) * 2 + i) * rows, 0)
    return gate_full, out_full


def columns_for(left, place):
    w = lax.axis_index("wsh")
    rows = left.shape[1] // 4
    half = rows // 2
    return jnp.concatenate(
        [lax.dynamic_slice_in_dim(left, (w ^ k) * rows + place * half, half, 1) for k in range(4)], axis=1
    )


def cut(value, i):
    rows = value.shape[0] // 2
    return lax.dynamic_slice_in_dim(value, i * rows, rows, 0)


def join(own, other, i):
    return jnp.where(i == 0, jnp.concatenate([own, other]), jnp.concatenate([other, own]))


def gather_z(part):
    if not direct():
        return lax.all_gather(part, "seq", axis=0, tiled=True, axis_index_groups=same_core())
    z = lax.axis_index("seq") // 2
    pair = join(part, across(part, "seq", 2), z % 2)
    return join(pair, across(pair, "seq", 4), z // 2)


def reduce_product(left, right):
    if not direct():
        term = dot_00(left, right).astype(BF)
        part = lax.psum_scatter(term, "wsh", scatter_dimension=0, tiled=True)
        return lax.psum(part, "seq"), right
    me = lax.axis_index("seq")
    core, z = me % 2, me // 2
    sent = across(dot_00(columns_for(left, 1 - core), right).astype(BF), "seq", 1)
    chip = add(dot_00(columns_for(left, core), right), sent)
    chip, right = lax.optimization_barrier((chip, right))
    half = chip.shape[0] // 4
    quarter = half // 2
    a = [chip[k * half : k * half + quarter] for k in range(4)]
    b = [chip[k * half + quarter : (k + 1) * half] for k in range(4)]
    by_x = across(jnp.concatenate([a[1], a[3]], axis=0), "wsh", 1)
    by_y = across(jnp.concatenate([b[2], b[3]], axis=0), "wsh", 2)
    a2 = across(add(a[2], by_x[quarter:]), "wsh", 2)
    b1 = across(add(b[1], by_y[quarter:]), "wsh", 1)
    plane = jnp.concatenate([add(add(a[0], by_x[:quarter]), a2), add(add(b[0], by_y[:quarter]), b1)], axis=0)
    z_low, z_high = z % 2, z // 2
    one = add(cut(plane, z_low), across(cut(plane, 1 - z_low), "seq", 2))
    two = add(cut(one, z_high), across(cut(one, 1 - z_high), "seq", 4))
    one = join(two, across(two, "seq", 4), z_high)
    all_z = join(one, across(one, "seq", 2), z_low)
    return join(all_z, across(all_z, "seq", 1), core), right


def widen_kernel(gate_ref, x_ref, out_ref):
    inner = gate_ref.shape[1]
    out_ref[:, :inner] = gate_ref[...].astype(F32)
    out_ref[:, inner:] = x_ref[:, : out_ref.shape[1] - inner].astype(F32)


def core_sums(normed, dgate, gated_out, cot):
    planes = lax.axis_size("wsh")
    core = lax.axis_index("seq") % 2
    half = normed.shape[1] // planes // 2

    def product(left, start, right):
        rows = left.shape[1] // planes
        picked = [lax.dynamic_slice_in_dim(left, w * rows + start, half, 1) for w in range(planes)]
        return dot_00(jnp.concatenate(picked, axis=1), right).astype(BF)

    def part(place):
        outs = [product(gated_out, (2 * place + i) * half, cot) for i in (0, 1)]
        return jnp.concatenate([product(normed, place * half, dgate)] + outs, axis=1)

    sent = across(part(1 - core), "seq", 1)
    return add(part(core), sent)


def sum_over(value, axis, groups, count):
    every = lax.all_to_all(
        value, axis, split_axis=0, concat_axis=0, tiled=True, axis_index_groups=groups
    )
    rows = every.shape[0] // count
    total = every[:rows].astype(F32)
    for i in range(1, count):
        total = total + every[i * rows : (i + 1) * rows].astype(F32)
    return total.astype(BF)


def same_core():
    seqs = lax.axis_size("seq")
    return [list(range(i, seqs, 2)) for i in (0, 1)]


def spread_back(part, inner):
    core = lax.axis_index("seq") % 2
    other = across(part, "seq", 1)
    low, high = jnp.where(core == 0, part, other), jnp.where(core == 0, other, part)
    width = (part.shape[1] - inner) // 2
    outs = [v[:, inner + i * width : inner + (i + 1) * width] for v in (low, high) for i in (0, 1)]
    return (
        jnp.concatenate([low[:, :inner], high[:, :inner]], axis=0),
        jnp.concatenate(outs, axis=0).astype(F32),
    )


def sum_small(parts):
    if not direct():
        return lax.psum(parts, ("seq", "wsh"))
    flat = jnp.concatenate([p.reshape(-1) for p in parts])
    size = flat.shape[0]
    flat = jnp.pad(flat, (0, -size % 1024)).reshape(-1, 128)
    for axis, bit in (("seq", 1), ("seq", 2), ("seq", 4), ("wsh", 1), ("wsh", 2)):
        flat = flat + across(flat, axis, bit)
    flat = flat.reshape(-1)
    out, at = [], 0
    for p in parts:
        out.append(flat[at : at + p.size].reshape(p.shape))
        at += p.size
    return tuple(out)


def on_device(
    x_in, seg_ids, g_norm, w_in, conv_w, conv_b, dt_bias, a_log, d_skip, g_gate, w_out, cotangent
):
    seqs = lax.axis_size("seq")
    me = lax.axis_index("seq")
    toks = x_in.shape[1]
    width = x_in.shape[2]
    inner = g_gate.shape[0]
    heads = dt_bias.shape[0]
    head_width = inner // heads
    conv_width = conv_w.shape[1]
    taps = conv_w.shape[0]
    chunks = toks // CHUNK
    sds = jax.ShapeDtypeStruct

    used = w_in.shape[1] - inner
    wx, wg, wo = gather_weights(jnp.pad(w_in[:, inner:], ((0, 0), (0, -used % 128))), w_in[:, :inner], w_out)

    up = [(i, i + 1) for i in range(seqs - 1)]
    down = [(i + 1, i) for i in range(seqs - 1)]
    halo = lax.ppermute(x_in[0, toks - HALO :], "seq", up)
    x_ext = jnp.concatenate([halo, x_in[0]], axis=0).astype(F32)
    r_ext = lax.rsqrt(jnp.mean(x_ext * x_ext, axis=1, keepdims=True) + EPSILON)
    start = me * toks
    seg_pad = jnp.concatenate([jnp.full((HALO,), -1, jnp.int32), seg_ids[0], jnp.full((8,), -2, jnp.int32)])
    near = lax.dynamic_slice_in_dim(seg_pad, start, toks + HALO + 8, 0)
    seg = near[HALO : HALO + toks]
    keep = jnp.stack([(near[HALO - k : HALO - k + toks] == seg) for k in range(taps)], axis=1).astype(F32)
    ext_seg = near[: toks + HALO]
    place = jnp.arange(toks + HALO)
    keep_next = jnp.stack(
        [(near[k : k + toks + HALO] == ext_seg) & (place + k < toks + HALO) for k in range(taps)], axis=1
    ).astype(F32)
    seg_before = near[HALO - 1]
    seg_f = seg.astype(F32)
    seg_chunk = seg.reshape(chunks, CHUNK)
    last_chunk = seg_chunk[:, -1]
    prev_chunk = jnp.concatenate([seg_before[None], last_chunk[:-1]])
    lanes = 4 * heads
    owner = jnp.arange(inner)[None, :] // head_width
    slot = jnp.arange(lanes)[:, None]
    spread, spread_ent, spread_leave = [(slot == owner + i * heads).astype(BF) for i in (0, 2, 3)]
    gather = jnp.stack([(slot == owner + i * heads).astype(BF).T for i in (0, 1, 2)])
    skip_wide = jnp.repeat(d_skip, head_width)[None, :]
    tri = jnp.tril(jnp.ones((CHUNK, CHUNK), F32))
    seg_row = seg_f[None, :]
    seg_col = seg_f[:, None]
    fixed = (keep, keep_next, seg_row, seg_col, spread, spread_ent, spread_leave, gather, skip_wide)
    x_ext, fixed = lax.optimization_barrier((x_ext, fixed))
    keep, keep_next, seg_row, seg_col, spread, spread_ent, spread_leave, gather, skip_wide = fixed
    normed_ext = (x_ext * r_ext * g_norm[None, :]).astype(BF)
    normed = normed_ext[HALO:]
    proj = dot(normed_ext, wx).astype(BF)
    gate = dot(normed, wg).astype(BF)
    cot = cotangent[0]
    back = dot_tt(cot, wo).astype(BF)

    step_raw = proj[HALO:, conv_width : conv_width + heads].astype(F32) + dt_bias[None, :]
    dt = jax.nn.softplus(step_raw)
    rates = -jnp.exp(a_log)
    logs = (dt * rates[None, :]).reshape(chunks, CHUNK, heads)
    cum = jnp.einsum("ts,csh->cth", tri, logs, precision=EXACT)
    last = cum[:, -1]
    before = jnp.einsum("cd,dh->ch", jnp.tril(jnp.ones((chunks, chunks), F32), -1), last, precision=EXACT)
    after = jnp.einsum("cd,dh->ch", jnp.triu(jnp.ones((chunks, chunks), F32), 1), last, precision=EXACT)
    total_log = jnp.sum(last, axis=0)
    enter = jnp.exp(cum) * (seg_chunk == prev_chunk[:, None])[:, :, None]
    leave_log = last[:, None] - cum
    leave = jnp.exp(leave_log) * (seg_chunk == last_chunk[:, None])[:, :, None]
    far_enter = jnp.exp(cum + before[:, None]) * (seg_chunk == seg_before)[:, :, None]
    far_leave = (
        jnp.exp(leave_log + after[:, None]) * (seg_chunk == seg[-1])[:, :, None] * dt.reshape(chunks, CHUNK, heads)
    )
    chunk_decay = jnp.exp(last) * (last_chunk == prev_chunk)[:, None]
    decay_wide = jnp.repeat(chunk_decay, head_width, axis=1)[:, None, :]
    flat = lambda v: v.reshape(toks, heads)
    tok = jnp.concatenate([dt, flat(cum), flat(enter), flat(leave)], axis=1)
    far = jnp.concatenate([flat(far_leave), flat(far_leave), flat(far_enter), flat(far_enter)], axis=1)
    cum_rows = flat(cum).T
    block = 256
    mixed, slope = pl.pallas_call(
        conv_kernel,
        grid=(conv_width // block,),
        in_specs=[
            pl.BlockSpec((toks + HALO, block), lambda i: (0, i)),
            pl.BlockSpec((toks, taps), lambda i: (0, 0)),
            pl.BlockSpec((taps, block), lambda i: (0, i)),
            pl.BlockSpec((1, block), lambda i: (0, i)),
        ],
        out_specs=[pl.BlockSpec((toks, block), lambda i: (0, i))] * 2,
        out_shape=[sds((toks, conv_width), BF)] * 2,
        scratch_shapes=[pltpu.VMEM((toks + HALO, block), F32)],
        compiler_params=params(),
        name="conv",
    )(proj, keep, conv_w, conv_b[None, :])

    rows = lambda n: pl.BlockSpec((CHUNK, n), lambda i: (i, 0))
    whole = lambda a, b: pl.BlockSpec((a, b), lambda i: (0, 0))
    own_state = pl.pallas_call(
        state_kernel,
        grid=(chunks,),
        in_specs=[rows(conv_width), rows(lanes), whole(lanes, inner), whole(1, inner)],
        out_specs=whole(STATE + 3 * HALO, inner),
        out_shape=sds((STATE + 3 * HALO, inner), BF),
        scratch_shapes=[pltpu.VMEM((STATE, inner), F32)],
        compiler_params=params(),
        name="own_state",
    )(mixed, far, spread, jnp.repeat(total_log, head_width)[None, :])

    every = lax.all_gather(own_state, "seq", axis=0)
    logs_all = sum(every[:, STATE + i * HALO].astype(F32) for i in range(3))
    ids = jnp.arange(seqs)
    ends = seg_ids[0].reshape(seqs, toks)[:, -1]
    starts_before = jnp.concatenate([jnp.full((1,), -1, jnp.int32), ends[:-1]])
    between = (ids[None, :] > jnp.minimum(ids, me)[:, None]) & (ids[None, :] < jnp.maximum(ids, me)[:, None])
    gap = jnp.exp(jnp.sum(jnp.where(between[:, :, None], logs_all[None], 0.0), axis=1))
    from_past = gap * ((ids < me) & (ends == seg_before))[:, None]
    from_next = gap * ((ids > me) & (starts_before == seg[-1]))[:, None]

    def combine(states, weights):
        return jnp.sum(states[:, :STATE].astype(F32) * weights[:, None, :], axis=0)

    y_inside = pl.pallas_call(
        partial(inside_kernel, heads),
        grid=(chunks,),
        in_specs=[
            rows(conv_width), rows(lanes), rows(1),
            pl.BlockSpec((heads, CHUNK), lambda i: (0, i)),
            pl.BlockSpec((1, CHUNK), lambda i: (0, i)),
            whole(lanes, inner), whole(1, inner),
        ],
        out_specs=rows(inner),
        out_shape=sds((toks, inner), BF),
        compiler_params=params(),
        name="inside",
    )(mixed, tok, seg_col, cum_rows, seg_row, spread, skip_wide)
    first_state = combine(every, from_past)

    states, gated_out, dgate, dy, dgain, dskip_wide, own_ds = pl.pallas_call(
        gate_kernel,
        grid=(chunks,),
        in_specs=[
            rows(inner), rows(conv_width), rows(inner), rows(inner), rows(lanes), rows(lanes),
            pl.BlockSpec((1, 1, inner), lambda i: (i, 0, 0)),
            whole(1, inner), whole(STATE, inner),
            whole(lanes, inner), whole(lanes, inner), whole(lanes, inner),
        ],
        out_specs=[
            pl.BlockSpec((1, STATE, inner), lambda i: (i, 0, 0)),
            rows(inner), rows(inner), rows(inner),
            whole(1, inner), whole(1, inner), whole(STATE, inner),
        ],
        out_shape=[
            sds((chunks, STATE, inner), BF),
            sds((toks, inner), BF), sds((toks, inner), BF), sds((toks, inner), BF),
            sds((1, inner), F32), sds((1, inner), F32), sds((STATE, inner), BF),
        ],
        scratch_shapes=[pltpu.VMEM((STATE, inner), F32)] * 2,
        compiler_params=params(),
        name="gate",
    )(y_inside, mixed, gate, back, tok, far, decay_wide, g_gate[None, :], first_state, spread, spread_ent, spread_leave)

    last_ds = combine(lax.all_gather(own_ds, "seq", axis=0), from_next)
    result = (x_ext[HALO:] + dot(gated_out, wo)).astype(BF)
    sums = core_sums(normed, dgate, gated_out, cot)
    sums = sum_over(sums, "wsh", None, lax.axis_size("wsh"))

    flip = lambda n: pl.BlockSpec((CHUNK, n), lambda i: (chunks - 1 - i, 0))
    dz, tokg, inlog, carry = pl.pallas_call(
        partial(back_kernel, heads),
        grid=(chunks,),
        in_specs=[
            flip(inner), flip(conv_width), flip(conv_width), flip(lanes), flip(1),
            pl.BlockSpec((heads, CHUNK), lambda i: (0, chunks - 1 - i)),
            pl.BlockSpec((1, CHUNK), lambda i: (0, chunks - 1 - i)),
            pl.BlockSpec((1, 1, inner), lambda i: (chunks - 1 - i, 0, 0)),
            whole(1, inner),
            pl.BlockSpec((1, STATE, inner), lambda i: (chunks - 1 - i, 0, 0)),
            whole(STATE, inner),
            whole(lanes, inner), whole(lanes, inner), whole(lanes, inner),
            pl.BlockSpec((3, inner, lanes), lambda i: (0, 0, 0)),
        ],
        out_specs=[
            flip(conv_width), flip(lanes),
            pl.BlockSpec((heads, CHUNK), lambda i: (0, chunks - 1 - i)),
            pl.BlockSpec((1, 1, inner), lambda i: (chunks - 1 - i, 0, 0)),
        ],
        out_shape=[
            sds((toks, conv_width), BF), sds((toks, lanes), F32), sds((heads, toks), F32),
            sds((chunks, 1, inner), F32),
        ],
        scratch_shapes=[pltpu.VMEM((STATE, inner), F32), pltpu.VMEM((CHUNK, inner), F32)],
        compiler_params=params(),
        name="scan_back",
    )(
        dy, mixed, slope, tok, seg_col, cum_rows, seg_row, decay_wide, skip_wide, states, last_ds,
        spread, spread_ent, spread_leave, gather,
    )

    dz, sums = lax.optimization_barrier((dz, sums))
    sums = sum_over(sums, "seq", same_core(), seqs // 2)

    dxbc, dconv_w, dconv_b = pl.pallas_call(
        conv_back_kernel,
        grid=(conv_width // block,),
        in_specs=[
            pl.BlockSpec((toks, block), lambda i: (0, i)),
            pl.BlockSpec((toks + HALO, block), lambda i: (0, i)),
            pl.BlockSpec((toks, taps), lambda i: (0, 0)),
            pl.BlockSpec((toks + HALO, taps), lambda i: (0, 0)),
            pl.BlockSpec((taps, block), lambda i: (0, i)),
        ],
        out_specs=[
            pl.BlockSpec((toks + HALO, block), lambda i: (0, i)),
            pl.BlockSpec((taps, block), lambda i: (0, i)),
            pl.BlockSpec((1, block), lambda i: (0, i)),
        ],
        out_shape=[
            sds((toks + HALO, conv_width), BF), sds((taps, conv_width), F32), sds((1, conv_width), F32),
        ],
        scratch_shapes=[
            pltpu.VMEM((toks + HALO, block), F32), pltpu.VMEM((toks + HALO + 8, block), F32),
        ],
        compiler_params=params(),
        name="conv_back",
    )(dz, proj, keep, keep_next, conv_w)

    tokg = tokg.reshape(chunks, CHUNK, lanes)
    from_dx, from_enter, from_leave = [tokg[:, :, i * heads : (i + 1) * heads] for i in range(3)]
    whole_chunk = jnp.sum(carry.reshape(chunks, heads, head_width), axis=2) * chunk_decay
    dlog = (
        inlog.T.reshape(chunks, CHUNK, heads)
        + jnp.einsum("ut,cth->cuh", tri.T, from_enter, precision=EXACT)
        + jnp.einsum("us,csh->cuh", tri - jnp.eye(CHUNK, dtype=F32), from_leave, precision=EXACT)
        + whole_chunk[:, None, :]
    )
    dlog = flat(dlog)
    drate = jnp.sum(dlog * dt, axis=0)
    dstep = (flat(from_dx) + dlog * rates[None, :]) * jax.nn.sigmoid(step_raw)
    dstep_bf = dstep.astype(BF)

    dxbc, sums = lax.optimization_barrier((dxbc, sums))
    sums = gather_z(sums)
    dproj = jnp.concatenate([dxbc, jnp.pad(dstep_bf, ((HALO, 0), (0, -heads % 128)))], axis=1)
    x_rows, dproj = reduce_product(normed_ext, dproj)
    gate_rows, w_out_grad = spread_back(sums, inner)
    strip = 64
    w_in_grad = pl.pallas_call(
        widen_kernel,
        grid=(w_in.shape[0] // strip,),
        in_specs=[
            pl.BlockSpec((strip, inner), lambda i: (i, 0)),
            pl.BlockSpec((strip, x_rows.shape[1]), lambda i: (i, 0)),
        ],
        out_specs=pl.BlockSpec((strip, w_in.shape[1]), lambda i: (i, 0)),
        out_shape=sds(w_in.shape, F32),
        compiler_params=params(),
        name="widen",
    )(gate_rows, x_rows)
    dn_ext = dot_tt(dproj, wx)
    over = lax.ppermute(dn_ext[:HALO], "seq", down)
    dn = dn_ext[HALO:] + dot_tt(dgate, wg)
    dn = dn + jnp.pad(over, ((toks - HALO, 0), (0, 0)))
    x_f = x_ext[HALO:]
    r = r_ext[HALO:]
    f = dn * g_norm[None, :]
    x_grad = cot.astype(F32) + r * f - x_f * (r * r * r) * jnp.mean(f * x_f, axis=1, keepdims=True)
    g_norm_part = jnp.sum(dn * x_f * r, axis=0)

    small = (
        g_norm_part,
        dconv_w,
        dconv_b[0],
        jnp.sum(dstep, axis=0),
        drate * rates,
        jnp.sum(dskip_wide.reshape(heads, head_width), axis=1),
        dgain[0],
    )
    small = sum_small(small)
    return (result[None], x_grad[None], small[0], w_in_grad) + tuple(small[1:]) + (w_out_grad,)


def solution(mesh):
    tokens = P("wsh", "seq", None)
    owned = P("wsh", None)
    return jax.shard_map(
        on_device,
        mesh=mesh,
        in_specs=(tokens, owned, P(), owned, P(), P(), P(), P(), P(), P(), owned, tokens),
        out_specs=(tokens, tokens, P(), owned, P(), P(), P(), P(), P(), P(), owned),
        check_vma=False,
    )
```

```python
from functools import partial

import jax
import jax.numpy as jnp
from jax import lax
from jax.experimental import pallas as pl
from jax.experimental.pallas import tpu as pltpu
from jax.sharding import PartitionSpec as P

STATE = 128
CHUNK = 128
HALO = 16
STRIP = 32
EPSILON = 1e-05
EXACT = lax.Precision.HIGHEST
BF = jnp.bfloat16
F32 = jnp.float32
VMEM_LIMIT = 56 * 1024 * 1024


def dot(a, b):
    return jnp.dot(a, b, preferred_element_type=F32)


def dot_tt(a, b):
    return lax.dot_general(a, b, (((1,), (1,)), ((), ())), preferred_element_type=F32)


def dot_00(a, b):
    return lax.dot_general(a, b, (((0,), (0,)), ((), ())), preferred_element_type=F32)


def sigmoid(v):
    return 0.5 + 0.5 * jnp.tanh(0.5 * v)


def params():
    return pltpu.CompilerParams(vmem_limit_bytes=VMEM_LIMIT, dimension_semantics=("arbitrary",))


def conv_kernel(x_ref, keep_ref, w_ref, b_ref, mixed_ref, slope_ref, buf):
    rows = mixed_ref.shape[0]
    buf[...] = x_ref[...].astype(F32)
    taps = w_ref.shape[0]
    for start in range(0, rows, STRIP):
        keep = keep_ref[start : start + STRIP, :]
        total = b_ref[...] + w_ref[taps - 1 : taps, :] * buf[HALO + start : HALO + start + STRIP, :]
        for k in range(1, taps):
            moved = buf[HALO + start - k : HALO + start - k + STRIP, :]
            total = total + w_ref[taps - 1 - k : taps - k, :] * (moved * keep[:, k : k + 1])
        sg = sigmoid(total)
        mixed = total * sg
        mixed_ref[start : start + STRIP, :] = mixed.astype(BF)
        slope_ref[start : start + STRIP, :] = (sg + mixed * (1.0 - sg)).astype(BF)


def conv_back_kernel(dz_ref, x_ref, keep_ref, next_ref, w_ref, dx_ref, dw_ref, db_ref, buf, dbuf):
    rows, width = dz_ref.shape
    taps = w_ref.shape[0]
    buf[...] = x_ref[...].astype(F32)
    dbuf[0:HALO, :] = jnp.zeros((HALO, width), F32)
    dbuf[HALO : HALO + rows, :] = dz_ref[...].astype(F32)
    dbuf[HALO + rows :, :] = jnp.zeros((8, width), F32)
    sums = [jnp.zeros((8, width), F32) for _ in range(taps + 1)]
    eights = lambda v: jnp.sum(v.reshape(STRIP // 8, 8, width), axis=0)
    for start in range(0, rows, STRIP):
        keep = keep_ref[start : start + STRIP, :]
        dz = dbuf[HALO + start : HALO + start + STRIP, :]
        sums[taps] = sums[taps] + eights(dz)
        for k in range(taps):
            moved = buf[HALO + start - k : HALO + start - k + STRIP, :]
            if k:
                moved = moved * keep[:, k : k + 1]
            sums[k] = sums[k] + eights(dz * moved)
    for k in range(taps):
        dw_ref[taps - 1 - k : taps - k, :] = jnp.sum(sums[k], axis=0, keepdims=True)
    db_ref[...] = jnp.sum(sums[taps], axis=0, keepdims=True)
    for start in range(0, rows + HALO, STRIP):
        count = min(STRIP, rows + HALO - start)
        total = w_ref[taps - 1 : taps, :] * dbuf[start : start + count, :]
        nxt = next_ref[start : start + count, :]
        for k in range(1, taps):
            moved = dbuf[start + k : start + k + count, :]
            total = total + w_ref[taps - 1 - k : taps - k, :] * (moved * nxt[:, k : k + 1])
        dx_ref[start : start + count, :] = total.astype(BF)


def state_kernel(mixed_ref, tok_ref, spread_ref, log_ref, s_ref, total):
    inner = s_ref.shape[1]

    @pl.when(pl.program_id(0) == 0)
    def _():
        total[...] = jnp.zeros_like(total)

    factor = dot(tok_ref[...].astype(BF), spread_ref[...])
    left = (mixed_ref[:, :inner].astype(F32) * factor).astype(BF)
    total[...] += dot_00(mixed_ref[:, inner : inner + STATE], left)

    @pl.when(pl.program_id(0) == pl.num_programs(0) - 1)
    def _():
        s_ref[:STATE, :] = total[...].astype(BF)
        rest = jnp.broadcast_to(log_ref[...], (HALO, inner))
        for i in range(3):
            piece = rest.astype(BF)
            s_ref[STATE + i * HALO : STATE + (i + 1) * HALO, :] = piece
            rest = rest - piece.astype(F32)


def decay_pair(tok, cum_rows, head, heads):
    gap = tok[:, heads + head : heads + head + 1] - cum_rows[head : head + 1, :]
    return jnp.exp(jnp.minimum(gap, 0.0))


def linked_mask(seg_col, seg_row):
    later = lax.broadcasted_iota(jnp.int32, (CHUNK, CHUNK), 0)
    earlier = lax.broadcasted_iota(jnp.int32, (CHUNK, CHUNK), 1)
    return (seg_col == seg_row) & (later >= earlier)


def two_heads(pair):
    lane = lax.broadcasted_iota(jnp.int32, pair.shape, 1)
    zero = jnp.zeros_like(pair)
    half = pair.shape[1] // 2
    return jnp.where(lane < half, pair, zero), jnp.where(lane >= half, pair, zero)


def inside_kernel(heads, mixed_ref, tok_ref, seg_ref, cum_ref, segrow_ref, spread_ref, skip_ref, y_ref):
    inner = y_ref.shape[1]
    pair_width = 2 * inner // heads
    tok = tok_ref[...]
    xc = mixed_ref[:, :inner].astype(F32)
    xt = (xc * dot(tok.astype(BF), spread_ref[...])).astype(BF)
    b_rows = mixed_ref[:, inner : inner + STATE]
    c_rows = mixed_ref[:, inner + STATE :]
    mask = linked_mask(seg_ref[...], segrow_ref[...])
    cross = jnp.where(mask, dot_tt(c_rows, b_rows), 0.0)
    cum_rows = cum_ref[...]
    for j in range(heads // 2):
        at = slice(j * pair_width, (j + 1) * pair_width)
        left = [(cross * decay_pair(tok, cum_rows, 2 * j + i, heads)).astype(BF) for i in (0, 1)]
        right = two_heads(xt[:, at])
        part = dot(jnp.concatenate(left, axis=1), jnp.concatenate(right, axis=0))
        y_ref[:, at] = (part + skip_ref[:, at] * xc[:, at]).astype(BF)


def gate_kernel(
    yi_ref, mixed_ref, gate_ref, back_ref, tok_ref, far_ref, decay_ref, gain_ref, s0_ref,
    spread_ref, spread_ent_ref, spread_leave_ref,
    sin_ref, out_ref, dgate_ref, dy_ref, dgain_ref, dskip_ref, ds_out_ref, state, ds_ref,
):
    inner = yi_ref.shape[1]

    @pl.when(pl.program_id(0) == 0)
    def _():
        state[...] = s0_ref[...]
        dgain_ref[...] = jnp.zeros_like(dgain_ref)
        dskip_ref[...] = jnp.zeros_like(dskip_ref)
        ds_ref[...] = jnp.zeros_like(ds_ref)

    xc = mixed_ref[:, :inner].astype(F32)
    b_rows = mixed_ref[:, inner : inner + STATE]
    c_rows = mixed_ref[:, inner + STATE :]
    tok = tok_ref[...].astype(BF)
    now = state[...]
    now_bf = now.astype(BF)
    sin_ref[0] = now_bf
    y = yi_ref[...].astype(F32) + dot(c_rows, now_bf) * dot(tok, spread_ent_ref[...])
    leave = (xc * dot(tok, spread_ref[...])) * dot(tok, spread_leave_ref[...])
    state[...] = now * decay_ref[0] + dot_00(b_rows, leave.astype(BF))
    gate = gate_ref[...].astype(F32)
    sg = sigmoid(gate)
    silu = gate * sg
    v = y * silu
    gain = gain_ref[...]
    q = lax.rsqrt(jnp.mean(v * v, axis=1, keepdims=True) + EPSILON)
    vq = v * q
    out_ref[...] = (vq * gain).astype(BF)
    back = back_ref[...].astype(F32)
    e = back * gain
    cross = jnp.mean(vq * e, axis=1, keepdims=True)
    dv = q * (e - vq * cross)
    dgain_ref[...] += jnp.sum(back * vq, axis=0, keepdims=True)
    dgate_ref[...] = (dv * y * (sg * (1.0 + gate * (1.0 - sg)))).astype(BF)
    dy = dv * silu
    dy_ref[...] = dy.astype(BF)
    dskip_ref[...] += jnp.sum(dy * xc, axis=0, keepdims=True)
    ds_ref[...] += dot_00(c_rows, (dy * dot(far_ref[...].astype(BF), spread_ent_ref[...])).astype(BF))

    @pl.when(pl.program_id(0) == pl.num_programs(0) - 1)
    def _():
        ds_out_ref[...] = ds_ref[...].astype(BF)


def back_kernel(
    heads, dy_ref, mixed_ref, slope_ref, tok_ref, seg_ref, cum_ref, segrow_ref, decay_ref, skip_ref, sin_ref, ds0_ref,
    spread_ref, spread_ent_ref, spread_leave_ref, gather_ref,
    dz_ref, tokg_ref, inlog_ref, carry_ref, dstate, dxt,
):
    inner = dy_ref.shape[1]
    pair_width = 2 * inner // heads

    @pl.when(pl.program_id(0) == 0)
    def _():
        dstate[...] = ds0_ref[...]

    tok = tok_ref[...]
    tok_bf = tok.astype(BF)
    xc = mixed_ref[:, :inner].astype(F32)
    dt_wide = dot(tok_bf, spread_ref[...])
    xt = (xc * dt_wide).astype(BF)
    b_rows = mixed_ref[:, inner : inner + STATE]
    c_rows = mixed_ref[:, inner + STATE :]
    ent = dot(tok_bf, spread_ent_ref[...])
    leave = dot(tok_bf, spread_leave_ref[...])
    dy = dy_ref[...]
    sin = sin_ref[0]
    ds = dstate[...]
    ds_bf = ds.astype(BF)
    dye = dy.astype(F32) * ent
    tokg = dot((dye * dot(c_rows, sin)).astype(BF), gather_ref[1])
    dye = dye.astype(BF)
    dc = dot_tt(dye, sin)
    xt_f = xt.astype(F32)
    dx_state = dot(b_rows, ds_bf) * leave
    dxt[...] = dx_state
    tokg = tokg + dot((xt_f * dx_state).astype(BF), gather_ref[2])
    db = dot_tt((xt_f * leave).astype(BF), ds_bf)
    carry_ref[0] = jnp.sum(ds * sin.astype(F32), axis=0, keepdims=True)
    dstate[...] = ds * decay_ref[0] + dot_00(c_rows, dye)
    mask = linked_mask(seg_ref[...], segrow_ref[...])
    cross = jnp.where(mask, dot_tt(c_rows, b_rows), 0.0)
    later = lax.broadcasted_iota(jnp.int32, (CHUNK, CHUNK), 0)
    earlier = lax.broadcasted_iota(jnp.int32, (CHUNK, CHUNK), 1)
    before = (later < earlier).astype(BF)
    upto = (later >= earlier).astype(F32)
    cum_rows = cum_ref[...]
    dcross = jnp.zeros((CHUNK, CHUNK), F32)
    for j in range(heads // 2):
        at = slice(j * pair_width, (j + 1) * pair_width)
        xp = xt[:, at]
        dys = two_heads(dy[:, at])
        lefts = []
        for i in (0, 1):
            head = 2 * j + i
            decay = decay_pair(tok, cum_rows, head, heads)
            lefts.append((cross * decay).astype(BF))
            w = dot_tt(dys[i], xp) * decay
            dcross = dcross + w
            spans = dot((w * cross).astype(BF), before)
            inlog_ref[head : head + 1, :] = jnp.sum(spans * upto, axis=0, keepdims=True)
        dxt[:, at] += dot_00(jnp.concatenate(lefts, axis=0), jnp.concatenate(dys, axis=0))
    dcross = jnp.where(mask, dcross, 0.0).astype(BF)
    dc = dc + dot(dcross, b_rows)
    db = db + dot_00(dcross, c_rows)
    dx = dxt[...]
    tokg_ref[...] = tokg + dot((xc * dx).astype(BF), gather_ref[0])
    slope = slope_ref[...].astype(F32)
    dz_ref[:, :inner] = ((dx * dt_wide + skip_ref[...] * dy.astype(F32)) * slope[:, :inner]).astype(BF)
    dz_ref[:, inner : inner + STATE] = (db * slope[:, inner : inner + STATE]).astype(BF)
    dz_ref[:, inner + STATE :] = (dc * slope[:, inner + STATE :]).astype(BF)


def add(a, b):
    return (a.astype(F32) + b.astype(F32)).astype(BF)


def across(value, axis, bit):
    count = lax.axis_size(axis)
    return lax.ppermute(value, axis, [(i, i ^ bit) for i in range(count)])


def direct():
    return lax.axis_size("wsh") == 4 and lax.axis_size("seq") == 8


def fetch(half):
    rows = half.shape[0] // 2
    by_x, by_y = across(half, "wsh", 1), across(half, "wsh", 2)
    far_a, far_b = across(by_y[:rows], "wsh", 1), across(by_x[rows:], "wsh", 2)
    return jnp.concatenate([by_x, by_y, far_a, far_b], axis=0)


def gather_weights(shard, gate_shard, out_shard):
    if not direct():
        return tuple(lax.all_gather(v, "wsh", axis=0, tiled=True) for v in (shard, gate_shard, out_shard))
    core, w = lax.axis_index("seq") % 2, lax.axis_index("wsh")
    rows = shard.shape[0]
    half, quarter = rows // 2, rows // 4
    own = lax.dynamic_slice_in_dim(shard, core * half, half, 0)
    by_x, by_y = across(own, "wsh", 1), across(own, "wsh", 2)
    far_a, far_b = across(by_y[:quarter], "wsh", 1), across(by_x[quarter:], "wsh", 2)
    far_a, far_b, gate_shard, out_shard = lax.optimization_barrier((far_a, far_b, gate_shard, out_shard))
    out = lax.dynamic_update_slice_in_dim(
        jnp.zeros((4 * rows, shard.shape[1]), shard.dtype), shard, w * rows, 0
    )
    for piece, k, extra in ((by_x, 1, 0), (by_y, 2, 0), (far_a, 3, 0), (far_b, 3, quarter)):
        other = across(piece, "seq", 1)
        for part, place in ((piece, core), (other, 1 - core)):
            out = lax.dynamic_update_slice_in_dim(out, part, (w ^ k) * rows + place * half + extra, 0)
    return (out,) + gather_two(gate_shard, out_shard)


def gather_two(gate_shard, out_shard):
    core, w = lax.axis_index("seq") % 2, lax.axis_index("wsh")
    rows = gate_shard.shape[0]
    folded = jnp.concatenate([out_shard[:rows], out_shard[rows:]], axis=1)
    mine = fetch(jnp.where(core == 0, gate_shard, folded))
    other = across(mine, "seq", 1)
    gates, outs = jnp.where(core == 0, mine, other), jnp.where(core == 0, other, mine)
    gate_full = lax.dynamic_update_slice_in_dim(
        jnp.zeros((4 * rows, gate_shard.shape[1]), BF), gate_shard, w * rows, 0
    )
    out_full = lax.dynamic_update_slice_in_dim(
        jnp.zeros((8 * rows, out_shard.shape[1]), BF), out_shard, w * 2 * rows, 0
    )
    width = out_shard.shape[1]
    for k in (1, 2, 3):
        at = slice((k - 1) * rows, k * rows)
        gate_full = lax.dynamic_update_slice_in_dim(gate_full, gates[at], (w ^ k) * rows, 0)
        for i in (0, 1):
            piece = outs[at, i * width : (i + 1) * width]
            out_full = lax.dynamic_update_slice_in_dim(out_full, piece, ((w ^ k) * 2 + i) * rows, 0)
    return gate_full, out_full


def columns_for(left, place):
    w = lax.axis_index("wsh")
    rows = left.shape[1] // 4
    half = rows // 2
    return jnp.concatenate(
        [lax.dynamic_slice_in_dim(left, (w ^ k) * rows + place * half, half, 1) for k in range(4)], axis=1
    )


def cut(value, i):
    rows = value.shape[0] // 2
    return lax.dynamic_slice_in_dim(value, i * rows, rows, 0)


def join(own, other, i):
    return jnp.where(i == 0, jnp.concatenate([own, other]), jnp.concatenate([other, own]))


def gather_z(part):
    if not direct():
        return lax.all_gather(part, "seq", axis=0, tiled=True, axis_index_groups=same_core())
    z = lax.axis_index("seq") // 2
    pair = join(part, across(part, "seq", 2), z % 2)
    return join(pair, across(pair, "seq", 4), z // 2)


def reduce_product(left, right, beside, first, held):
    if not direct():
        term = dot_00(left, right).astype(BF)
        part = lax.psum_scatter(term, "wsh", scatter_dimension=0, tiled=True)
        return lax.psum(part, "seq"), right, gather_z(beside), first(held)
    me = lax.axis_index("seq")
    core, z = me % 2, me // 2
    sent = across(dot_00(columns_for(left, 1 - core), right).astype(BF), "seq", 1)
    chip = add(dot_00(columns_for(left, core), right), sent)
    chip, beside, held = lax.optimization_barrier((chip, beside, held))
    first = first(held)
    beside = gather_z(beside)
    half = chip.shape[0] // 4
    quarter = half // 2
    a = [chip[k * half : k * half + quarter] for k in range(4)]
    b = [chip[k * half + quarter : (k + 1) * half] for k in range(4)]
    by_x = across(jnp.concatenate([a[1], a[3]], axis=0), "wsh", 1)
    by_y = across(jnp.concatenate([b[2], b[3]], axis=0), "wsh", 2)
    by_x, by_y, right, first = lax.optimization_barrier((by_x, by_y, right, first))
    a2, b1 = lax.optimization_barrier((add(a[2], by_x[quarter:]), add(b[1], by_y[quarter:])))
    a2, b1 = across(a2, "wsh", 2), across(b1, "wsh", 1)
    plane = jnp.concatenate([add(add(a[0], by_x[:quarter]), a2), add(add(b[0], by_y[:quarter]), b1)], axis=0)
    z_low, z_high = z % 2, z // 2
    plane, beside = lax.optimization_barrier((plane, beside))
    one = add(cut(plane, z_low), across(cut(plane, 1 - z_low), "seq", 2))
    two = add(cut(one, z_high), across(cut(one, 1 - z_high), "seq", 4))
    one = join(two, across(two, "seq", 4), z_high)
    all_z = join(one, across(one, "seq", 2), z_low)
    return join(all_z, across(all_z, "seq", 1), core), right, beside, first


def widen_kernel(gate_ref, x_ref, out_ref):
    inner = gate_ref.shape[1]
    for ref, first, end in ((gate_ref, 0, inner), (x_ref, inner, out_ref.shape[0])):
        for at in range(0, end - first, CHUNK):
            count = min(CHUNK, end - first - at)
            turned = ref[:, at : at + CHUNK].astype(F32).T
            out_ref[first + at : first + at + count, :] = turned[:count]


def core_sums(normed, dgate, gated_out, cot):
    planes = lax.axis_size("wsh")
    core = lax.axis_index("seq") % 2
    half = normed.shape[1] // planes // 2

    def product(left, start, right):
        rows = left.shape[1] // planes
        picked = [lax.dynamic_slice_in_dim(left, w * rows + start, half, 1) for w in range(planes)]
        return dot_00(jnp.concatenate(picked, axis=1), right).astype(BF)

    def part(place):
        outs = [product(gated_out, (2 * place + i) * half, cot) for i in (0, 1)]
        return jnp.concatenate([product(normed, place * half, dgate)] + outs, axis=1)

    sent = across(part(1 - core), "seq", 1)
    return add(part(core), sent)


def sum_over(value, axis, groups, count):
    every = lax.all_to_all(
        value, axis, split_axis=0, concat_axis=0, tiled=True, axis_index_groups=groups
    )
    rows = every.shape[0] // count
    total = every[:rows].astype(F32)
    for i in range(1, count):
        total = total + every[i * rows : (i + 1) * rows].astype(F32)
    return total.astype(BF)


def same_core():
    seqs = lax.axis_size("seq")
    return [list(range(i, seqs, 2)) for i in (0, 1)]


def spread_back(part, inner):
    core = lax.axis_index("seq") % 2
    other = across(part, "seq", 1)
    low, high = jnp.where(core == 0, part, other), jnp.where(core == 0, other, part)
    width = (part.shape[1] - inner) // 2
    outs = [v[:, inner + i * width : inner + (i + 1) * width] for v in (low, high) for i in (0, 1)]
    return (
        jnp.concatenate([low[:, :inner], high[:, :inner]], axis=0),
        jnp.concatenate(outs, axis=0).astype(F32),
    )


def sum_small(parts):
    if not direct():
        return lax.psum(parts, ("seq", "wsh"))
    flat = jnp.concatenate([p.reshape(-1) for p in parts])
    size = flat.shape[0]
    flat = jnp.pad(flat, (0, -size % 1024)).reshape(-1, 128)
    for axis, bit in (("seq", 1), ("seq", 2), ("seq", 4), ("wsh", 1), ("wsh", 2)):
        flat = flat + across(flat, axis, bit)
    flat = flat.reshape(-1)
    out, at = [], 0
    for p in parts:
        out.append(flat[at : at + p.size].reshape(p.shape))
        at += p.size
    return tuple(out)


def on_device(
    x_in, seg_ids, g_norm, w_in, conv_w, conv_b, dt_bias, a_log, d_skip, g_gate, w_out, cotangent
):
    seqs = lax.axis_size("seq")
    me = lax.axis_index("seq")
    toks = x_in.shape[1]
    width = x_in.shape[2]
    inner = g_gate.shape[0]
    heads = dt_bias.shape[0]
    head_width = inner // heads
    conv_width = conv_w.shape[1]
    taps = conv_w.shape[0]
    chunks = toks // CHUNK
    sds = jax.ShapeDtypeStruct

    used = w_in.shape[1] - inner
    wx, wg, wo = gather_weights(jnp.pad(w_in[:, inner:], ((0, 0), (0, -used % 128))), w_in[:, :inner], w_out)

    up = [(i, i + 1) for i in range(seqs - 1)]
    down = [(i + 1, i) for i in range(seqs - 1)]
    halo = lax.ppermute(x_in[0, toks - HALO :], "seq", up)
    x_ext = jnp.concatenate([halo, x_in[0]], axis=0).astype(F32)
    r_ext = lax.rsqrt(jnp.mean(x_ext * x_ext, axis=1, keepdims=True) + EPSILON)
    start = me * toks
    seg_pad = jnp.concatenate([jnp.full((HALO,), -1, jnp.int32), seg_ids[0], jnp.full((8,), -2, jnp.int32)])
    near = lax.dynamic_slice_in_dim(seg_pad, start, toks + HALO + 8, 0)
    seg = near[HALO : HALO + toks]
    keep = jnp.stack([(near[HALO - k : HALO - k + toks] == seg) for k in range(taps)], axis=1).astype(F32)
    ext_seg = near[: toks + HALO]
    place = jnp.arange(toks + HALO)
    keep_next = jnp.stack(
        [(near[k : k + toks + HALO] == ext_seg) & (place + k < toks + HALO) for k in range(taps)], axis=1
    ).astype(F32)
    seg_before = near[HALO - 1]
    seg_f = seg.astype(F32)
    seg_chunk = seg.reshape(chunks, CHUNK)
    last_chunk = seg_chunk[:, -1]
    prev_chunk = jnp.concatenate([seg_before[None], last_chunk[:-1]])
    lanes = 4 * heads
    owner = jnp.arange(inner)[None, :] // head_width
    slot = jnp.arange(lanes)[:, None]
    spread, spread_ent, spread_leave = [(slot == owner + i * heads).astype(BF) for i in (0, 2, 3)]
    gather = jnp.stack([(slot == owner + i * heads).astype(BF).T for i in (0, 1, 2)])
    skip_wide = jnp.repeat(d_skip, head_width)[None, :]
    tri = jnp.tril(jnp.ones((CHUNK, CHUNK), F32))
    seg_row = seg_f[None, :]
    seg_col = seg_f[:, None]
    fixed = (keep, seg_row, seg_col, spread, spread_ent, spread_leave, skip_wide)
    x_ext, fixed = lax.optimization_barrier((x_ext, fixed))
    keep, seg_row, seg_col, spread, spread_ent, spread_leave, skip_wide = fixed
    normed_ext = (x_ext * r_ext * g_norm[None, :]).astype(BF)
    normed = normed_ext[HALO:]
    proj = dot(normed_ext, wx).astype(BF)
    gate = dot(normed, wg).astype(BF)
    cot = cotangent[0]
    back = dot_tt(cot, wo).astype(BF)

    step_raw = proj[HALO:, conv_width : conv_width + heads].astype(F32) + dt_bias[None, :]
    dt = jax.nn.softplus(step_raw)
    rates = -jnp.exp(a_log)
    logs = (dt * rates[None, :]).reshape(chunks, CHUNK, heads)
    cum = jnp.einsum("ts,csh->cth", tri, logs, precision=EXACT)
    last = cum[:, -1]
    before = jnp.einsum("cd,dh->ch", jnp.tril(jnp.ones((chunks, chunks), F32), -1), last, precision=EXACT)
    after = jnp.einsum("cd,dh->ch", jnp.triu(jnp.ones((chunks, chunks), F32), 1), last, precision=EXACT)
    total_log = jnp.sum(last, axis=0)
    enter = jnp.exp(cum) * (seg_chunk == prev_chunk[:, None])[:, :, None]
    leave_log = last[:, None] - cum
    leave = jnp.exp(leave_log) * (seg_chunk == last_chunk[:, None])[:, :, None]
    far_enter = jnp.exp(cum + before[:, None]) * (seg_chunk == seg_before)[:, :, None]
    far_leave = (
        jnp.exp(leave_log + after[:, None]) * (seg_chunk == seg[-1])[:, :, None] * dt.reshape(chunks, CHUNK, heads)
    )
    chunk_decay = jnp.exp(last) * (last_chunk == prev_chunk)[:, None]
    decay_wide = jnp.repeat(chunk_decay, head_width, axis=1)[:, None, :]
    flat = lambda v: v.reshape(toks, heads)
    tok = jnp.concatenate([dt, flat(cum), flat(enter), flat(leave)], axis=1)
    far = jnp.concatenate([flat(far_leave), flat(far_leave), flat(far_enter), flat(far_enter)], axis=1)
    cum_rows = flat(cum).T
    block = conv_width // 3
    mixed, slope = pl.pallas_call(
        conv_kernel,
        grid=(conv_width // block,),
        in_specs=[
            pl.BlockSpec((toks + HALO, block), lambda i: (0, i)),
            pl.BlockSpec((toks, taps), lambda i: (0, 0)),
            pl.BlockSpec((taps, block), lambda i: (0, i)),
            pl.BlockSpec((1, block), lambda i: (0, i)),
        ],
        out_specs=[pl.BlockSpec((toks, block), lambda i: (0, i))] * 2,
        out_shape=[sds((toks, conv_width), BF)] * 2,
        scratch_shapes=[pltpu.VMEM((toks + HALO, block), F32)],
        compiler_params=params(),
        name="conv",
    )(proj, keep, conv_w, conv_b[None, :])

    rows = lambda n: pl.BlockSpec((CHUNK, n), lambda i: (i, 0))
    whole = lambda a, b: pl.BlockSpec((a, b), lambda i: (0, 0))
    own_state = pl.pallas_call(
        state_kernel,
        grid=(chunks,),
        in_specs=[rows(conv_width), rows(lanes), whole(lanes, inner), whole(1, inner)],
        out_specs=whole(STATE + 3 * HALO, inner),
        out_shape=sds((STATE + 3 * HALO, inner), BF),
        scratch_shapes=[pltpu.VMEM((STATE, inner), F32)],
        compiler_params=params(),
        name="own_state",
    )(mixed, far, spread, jnp.repeat(total_log, head_width)[None, :])

    every = lax.all_gather(own_state, "seq", axis=0)
    logs_all = sum(every[:, STATE + i * HALO].astype(F32) for i in range(3))
    ids = jnp.arange(seqs)
    ends = seg_ids[0].reshape(seqs, toks)[:, -1]
    starts_before = jnp.concatenate([jnp.full((1,), -1, jnp.int32), ends[:-1]])
    between = (ids[None, :] > jnp.minimum(ids, me)[:, None]) & (ids[None, :] < jnp.maximum(ids, me)[:, None])
    gap = jnp.exp(jnp.sum(jnp.where(between[:, :, None], logs_all[None], 0.0), axis=1))
    from_past = gap * ((ids < me) & (ends == seg_before))[:, None]
    from_next = gap * ((ids > me) & (starts_before == seg[-1]))[:, None]

    def combine(states, weights):
        return jnp.sum(states[:, :STATE].astype(F32) * weights[:, None, :], axis=0)

    y_inside = pl.pallas_call(
        partial(inside_kernel, heads),
        grid=(chunks,),
        in_specs=[
            rows(conv_width), rows(lanes), rows(1),
            pl.BlockSpec((heads, CHUNK), lambda i: (0, i)),
            pl.BlockSpec((1, CHUNK), lambda i: (0, i)),
            whole(lanes, inner), whole(1, inner),
        ],
        out_specs=rows(inner),
        out_shape=sds((toks, inner), BF),
        compiler_params=params(),
        name="inside",
    )(mixed, tok, seg_col, cum_rows, seg_row, spread, skip_wide)
    first_state = combine(every, from_past)

    states, gated_out, dgate, dy, dgain, dskip_wide, own_ds = pl.pallas_call(
        gate_kernel,
        grid=(chunks,),
        in_specs=[
            rows(inner), rows(conv_width), rows(inner), rows(inner), rows(lanes), rows(lanes),
            pl.BlockSpec((1, 1, inner), lambda i: (i, 0, 0)),
            whole(1, inner), whole(STATE, inner),
            whole(lanes, inner), whole(lanes, inner), whole(lanes, inner),
        ],
        out_specs=[
            pl.BlockSpec((1, STATE, inner), lambda i: (i, 0, 0)),
            rows(inner), rows(inner), rows(inner),
            whole(1, inner), whole(1, inner), whole(STATE, inner),
        ],
        out_shape=[
            sds((chunks, STATE, inner), BF),
            sds((toks, inner), BF), sds((toks, inner), BF), sds((toks, inner), BF),
            sds((1, inner), F32), sds((1, inner), F32), sds((STATE, inner), BF),
        ],
        scratch_shapes=[pltpu.VMEM((STATE, inner), F32)] * 2,
        compiler_params=params(),
        name="gate",
    )(y_inside, mixed, gate, back, tok, far, decay_wide, g_gate[None, :], first_state, spread, spread_ent, spread_leave)

    last_ds = combine(lax.all_gather(own_ds, "seq", axis=0), from_next)
    sums = core_sums(normed, dgate, gated_out, cot)
    dn_gate = dot_tt(dgate, wg)
    last_ds, dn_gate = lax.optimization_barrier((last_ds, dn_gate))
    sums = sum_over(sums, "wsh", None, lax.axis_size("wsh"))

    flip = lambda n: pl.BlockSpec((CHUNK, n), lambda i: (chunks - 1 - i, 0))
    dz, tokg, inlog, carry = pl.pallas_call(
        partial(back_kernel, heads),
        grid=(chunks,),
        in_specs=[
            flip(inner), flip(conv_width), flip(conv_width), flip(lanes), flip(1),
            pl.BlockSpec((heads, CHUNK), lambda i: (0, chunks - 1 - i)),
            pl.BlockSpec((1, CHUNK), lambda i: (0, chunks - 1 - i)),
            pl.BlockSpec((1, 1, inner), lambda i: (chunks - 1 - i, 0, 0)),
            whole(1, inner),
            pl.BlockSpec((1, STATE, inner), lambda i: (chunks - 1 - i, 0, 0)),
            whole(STATE, inner),
            whole(lanes, inner), whole(lanes, inner), whole(lanes, inner),
            pl.BlockSpec((3, inner, lanes), lambda i: (0, 0, 0)),
        ],
        out_specs=[
            flip(conv_width), flip(lanes),
            pl.BlockSpec((heads, CHUNK), lambda i: (0, chunks - 1 - i)),
            pl.BlockSpec((1, 1, inner), lambda i: (chunks - 1 - i, 0, 0)),
        ],
        out_shape=[
            sds((toks, conv_width), BF), sds((toks, lanes), F32), sds((heads, toks), F32),
            sds((chunks, 1, inner), F32),
        ],
        scratch_shapes=[pltpu.VMEM((STATE, inner), F32), pltpu.VMEM((CHUNK, inner), F32)],
        compiler_params=params(),
        name="scan_back",
    )(
        dy, mixed, slope, tok, seg_col, cum_rows, seg_row, decay_wide, skip_wide, states, last_ds,
        spread, spread_ent, spread_leave, gather,
    )

    dz, sums = lax.optimization_barrier((dz, sums))
    sums = sum_over(sums, "seq", same_core(), seqs // 2)

    dxbc, dconv_w, dconv_b = pl.pallas_call(
        conv_back_kernel,
        grid=(conv_width // block,),
        in_specs=[
            pl.BlockSpec((toks, block), lambda i: (0, i)),
            pl.BlockSpec((toks + HALO, block), lambda i: (0, i)),
            pl.BlockSpec((toks, taps), lambda i: (0, 0)),
            pl.BlockSpec((toks + HALO, taps), lambda i: (0, 0)),
            pl.BlockSpec((taps, block), lambda i: (0, i)),
        ],
        out_specs=[
            pl.BlockSpec((toks + HALO, block), lambda i: (0, i)),
            pl.BlockSpec((taps, block), lambda i: (0, i)),
            pl.BlockSpec((1, block), lambda i: (0, i)),
        ],
        out_shape=[
            sds((toks + HALO, conv_width), BF), sds((taps, conv_width), F32), sds((1, conv_width), F32),
        ],
        scratch_shapes=[
            pltpu.VMEM((toks + HALO, block), F32), pltpu.VMEM((toks + HALO + 8, block), F32),
        ],
        compiler_params=params(),
        name="conv_back",
    )(dz, proj, keep, keep_next, conv_w)

    tokg = tokg.reshape(chunks, CHUNK, lanes)
    from_dx, from_enter, from_leave = [tokg[:, :, i * heads : (i + 1) * heads] for i in range(3)]
    whole_chunk = jnp.sum(carry.reshape(chunks, heads, head_width), axis=2) * chunk_decay
    dlog = (
        inlog.T.reshape(chunks, CHUNK, heads)
        + jnp.einsum("ut,cth->cuh", tri.T, from_enter, precision=EXACT)
        + jnp.einsum("us,csh->cuh", tri - jnp.eye(CHUNK, dtype=F32), from_leave, precision=EXACT)
        + whole_chunk[:, None, :]
    )
    dlog = flat(dlog)
    drate = jnp.sum(dlog * dt, axis=0)
    dstep = (flat(from_dx) + dlog * rates[None, :]) * jax.nn.sigmoid(step_raw)
    dstep_bf = dstep.astype(BF)

    dxbc, sums = lax.optimization_barrier((dxbc, sums))
    dproj = jnp.concatenate([dxbc, jnp.pad(dstep_bf, ((HALO, 0), (0, -heads % 128)))], axis=1)
    x_rows, dproj, sums, result = reduce_product(
        normed_ext, dproj, sums, lambda left: (x_ext[HALO:] + dot(left, wo)).astype(BF), gated_out
    )
    gate_rows, w_out_grad = spread_back(sums, inner)
    w_in_grad = pl.pallas_call(
        widen_kernel,
        out_shape=sds(w_in.shape[::-1], F32),
        in_specs=[pl.BlockSpec(memory_space=pltpu.VMEM)] * 2,
        out_specs=pl.BlockSpec(memory_space=pltpu.VMEM),
        compiler_params=pltpu.CompilerParams(vmem_limit_bytes=VMEM_LIMIT),
        name="widen",
    )(gate_rows, x_rows).T
    dn_ext = dot_tt(dproj, wx)
    over = lax.ppermute(dn_ext[:HALO], "seq", down)
    dn = dn_ext[HALO:] + dn_gate
    dn = dn + jnp.pad(over, ((toks - HALO, 0), (0, 0)))
    x_f = x_ext[HALO:]
    r = r_ext[HALO:]
    f = dn * g_norm[None, :]
    x_grad = cot.astype(F32) + r * f - x_f * (r * r * r) * jnp.mean(f * x_f, axis=1, keepdims=True)
    g_norm_part = jnp.sum(dn * x_f * r, axis=0)

    small = (
        g_norm_part,
        dconv_w,
        dconv_b[0],
        jnp.sum(dstep, axis=0),
        drate * rates,
        jnp.sum(dskip_wide.reshape(heads, head_width), axis=1),
        dgain[0],
    )
    small = sum_small(small)
    return (result[None], x_grad[None], small[0], w_in_grad) + tuple(small[1:]) + (w_out_grad,)


def solution(mesh):
    tokens = P("wsh", "seq", None)
    owned = P("wsh", None)
    return jax.shard_map(
        on_device,
        mesh=mesh,
        in_specs=(tokens, owned, P(), owned, P(), P(), P(), P(), P(), P(), owned, tokens),
        out_specs=(tokens, tokens, P(), owned, P(), P(), P(), P(), P(), P(), owned),
        check_vma=False,
    )
```

```python
from functools import partial

import jax
import jax.numpy as jnp
from jax import lax
from jax.experimental import pallas as pl
from jax.experimental.pallas import tpu as pltpu
from jax.sharding import PartitionSpec as P

STATE = 128
CHUNK = 128
HALO = 16
STRIP = 32
EPSILON = 1e-05
EXACT = lax.Precision.HIGHEST
BF = jnp.bfloat16
F32 = jnp.float32
VMEM_LIMIT = 56 * 1024 * 1024


def dot(a, b):
    return jnp.dot(a, b, preferred_element_type=F32)


def dot_tt(a, b):
    return lax.dot_general(a, b, (((1,), (1,)), ((), ())), preferred_element_type=F32)


def dot_00(a, b):
    return lax.dot_general(a, b, (((0,), (0,)), ((), ())), preferred_element_type=F32)


def sigmoid(v):
    return 0.5 + 0.5 * jnp.tanh(0.5 * v)


def params():
    return pltpu.CompilerParams(vmem_limit_bytes=VMEM_LIMIT, dimension_semantics=("arbitrary",))


def conv_kernel(x_ref, keep_ref, w_ref, b_ref, mixed_ref, slope_ref, buf):
    rows = mixed_ref.shape[0]
    buf[...] = x_ref[...].astype(F32)
    taps = w_ref.shape[0]
    for start in range(0, rows, STRIP):
        keep = keep_ref[start : start + STRIP, :]
        total = b_ref[...] + w_ref[taps - 1 : taps, :] * buf[HALO + start : HALO + start + STRIP, :]
        for k in range(1, taps):
            moved = buf[HALO + start - k : HALO + start - k + STRIP, :]
            total = total + w_ref[taps - 1 - k : taps - k, :] * (moved * keep[:, k : k + 1])
        sg = sigmoid(total)
        mixed = total * sg
        mixed_ref[start : start + STRIP, :] = mixed.astype(BF)
        slope_ref[start : start + STRIP, :] = (sg + mixed * (1.0 - sg)).astype(BF)


def conv_back_kernel(dz_ref, x_ref, keep_ref, next_ref, w_ref, dx_ref, dw_ref, db_ref, buf, dbuf):
    rows, width = dz_ref.shape
    taps = w_ref.shape[0]
    buf[...] = x_ref[...].astype(F32)
    dbuf[0:HALO, :] = jnp.zeros((HALO, width), F32)
    dbuf[HALO : HALO + rows, :] = dz_ref[...].astype(F32)
    dbuf[HALO + rows :, :] = jnp.zeros((8, width), F32)
    sums = [jnp.zeros((8, width), F32) for _ in range(taps + 1)]
    eights = lambda v: jnp.sum(v.reshape(STRIP // 8, 8, width), axis=0)
    for start in range(0, rows, STRIP):
        keep = keep_ref[start : start + STRIP, :]
        dz = dbuf[HALO + start : HALO + start + STRIP, :]
        sums[taps] = sums[taps] + eights(dz)
        for k in range(taps):
            moved = buf[HALO + start - k : HALO + start - k + STRIP, :]
            if k:
                moved = moved * keep[:, k : k + 1]
            sums[k] = sums[k] + eights(dz * moved)
    for k in range(taps):
        dw_ref[taps - 1 - k : taps - k, :] = jnp.sum(sums[k], axis=0, keepdims=True)
    db_ref[...] = jnp.sum(sums[taps], axis=0, keepdims=True)
    for start in range(0, rows + HALO, STRIP):
        count = min(STRIP, rows + HALO - start)
        total = w_ref[taps - 1 : taps, :] * dbuf[start : start + count, :]
        nxt = next_ref[start : start + count, :]
        for k in range(1, taps):
            moved = dbuf[start + k : start + k + count, :]
            total = total + w_ref[taps - 1 - k : taps - k, :] * (moved * nxt[:, k : k + 1])
        dx_ref[start : start + count, :] = total.astype(BF)


def state_kernel(mixed_ref, tok_ref, spread_ref, log_ref, s_ref, total):
    inner = s_ref.shape[1]

    @pl.when(pl.program_id(0) == 0)
    def _():
        total[...] = jnp.zeros_like(total)

    factor = dot(tok_ref[...].astype(BF), spread_ref[...])
    left = (mixed_ref[:, :inner].astype(F32) * factor).astype(BF)
    total[...] += dot_00(mixed_ref[:, inner : inner + STATE], left)

    @pl.when(pl.program_id(0) == pl.num_programs(0) - 1)
    def _():
        s_ref[:STATE, :] = total[...].astype(BF)
        rest = jnp.broadcast_to(log_ref[...], (HALO, inner))
        for i in range(3):
            piece = rest.astype(BF)
            s_ref[STATE + i * HALO : STATE + (i + 1) * HALO, :] = piece
            rest = rest - piece.astype(F32)


def decay_pair(tok, cum_rows, head, heads):
    gap = tok[:, heads + head : heads + head + 1] - cum_rows[head : head + 1, :]
    return jnp.exp(jnp.minimum(gap, 0.0))


def linked_mask(seg_col, seg_row):
    later = lax.broadcasted_iota(jnp.int32, (CHUNK, CHUNK), 0)
    earlier = lax.broadcasted_iota(jnp.int32, (CHUNK, CHUNK), 1)
    return (seg_col == seg_row) & (later >= earlier)


def two_heads(pair):
    lane = lax.broadcasted_iota(jnp.int32, pair.shape, 1)
    zero = jnp.zeros_like(pair)
    half = pair.shape[1] // 2
    return jnp.where(lane < half, pair, zero), jnp.where(lane >= half, pair, zero)


def inside_kernel(heads, mixed_ref, tok_ref, seg_ref, cum_ref, segrow_ref, spread_ref, skip_ref, y_ref):
    inner = y_ref.shape[1]
    pair_width = 2 * inner // heads
    tok = tok_ref[...]
    xc = mixed_ref[:, :inner].astype(F32)
    xt = (xc * dot(tok.astype(BF), spread_ref[...])).astype(BF)
    b_rows = mixed_ref[:, inner : inner + STATE]
    c_rows = mixed_ref[:, inner + STATE :]
    mask = linked_mask(seg_ref[...], segrow_ref[...])
    cross = jnp.where(mask, dot_tt(c_rows, b_rows), 0.0)
    cum_rows = cum_ref[...]
    for j in range(heads // 2):
        at = slice(j * pair_width, (j + 1) * pair_width)
        left = [(cross * decay_pair(tok, cum_rows, 2 * j + i, heads)).astype(BF) for i in (0, 1)]
        right = two_heads(xt[:, at])
        part = dot(jnp.concatenate(left, axis=1), jnp.concatenate(right, axis=0))
        y_ref[:, at] = (part + skip_ref[:, at] * xc[:, at]).astype(BF)


def gate_kernel(
    yi_ref, mixed_ref, gate_ref, back_ref, tok_ref, far_ref, decay_ref, gain_ref, s0_ref,
    spread_ref, spread_ent_ref, spread_leave_ref,
    sin_ref, out_ref, dgate_ref, dy_ref, dgain_ref, dskip_ref, ds_out_ref, state, ds_ref,
):
    inner = yi_ref.shape[1]

    @pl.when(pl.program_id(0) == 0)
    def _():
        state[...] = s0_ref[...]
        dgain_ref[...] = jnp.zeros_like(dgain_ref)
        dskip_ref[...] = jnp.zeros_like(dskip_ref)
        ds_ref[...] = jnp.zeros_like(ds_ref)

    xc = mixed_ref[:, :inner].astype(F32)
    b_rows = mixed_ref[:, inner : inner + STATE]
    c_rows = mixed_ref[:, inner + STATE :]
    tok = tok_ref[...].astype(BF)
    now = state[...]
    now_bf = now.astype(BF)
    sin_ref[0] = now_bf
    y = yi_ref[...].astype(F32) + dot(c_rows, now_bf) * dot(tok, spread_ent_ref[...])
    leave = (xc * dot(tok, spread_ref[...])) * dot(tok, spread_leave_ref[...])
    state[...] = now * decay_ref[0] + dot_00(b_rows, leave.astype(BF))
    gate = gate_ref[...].astype(F32)
    sg = sigmoid(gate)
    silu = gate * sg
    v = y * silu
    gain = gain_ref[...]
    q = lax.rsqrt(jnp.mean(v * v, axis=1, keepdims=True) + EPSILON)
    vq = v * q
    out_ref[...] = (vq * gain).astype(BF)
    back = back_ref[...].astype(F32)
    e = back * gain
    cross = jnp.mean(vq * e, axis=1, keepdims=True)
    dv = q * (e - vq * cross)
    dgain_ref[...] += jnp.sum(back * vq, axis=0, keepdims=True)
    dgate_ref[...] = (dv * y * (sg * (1.0 + gate * (1.0 - sg)))).astype(BF)
    dy = dv * silu
    dy_ref[...] = dy.astype(BF)
    dskip_ref[...] += jnp.sum(dy * xc, axis=0, keepdims=True)
    ds_ref[...] += dot_00(c_rows, (dy * dot(far_ref[...].astype(BF), spread_ent_ref[...])).astype(BF))

    @pl.when(pl.program_id(0) == pl.num_programs(0) - 1)
    def _():
        ds_out_ref[...] = ds_ref[...].astype(BF)


def back_kernel(
    heads, dy_ref, mixed_ref, slope_ref, tok_ref, seg_ref, cum_ref, segrow_ref, decay_ref, skip_ref, sin_ref, ds0_ref,
    spread_ref, spread_ent_ref, spread_leave_ref, gather_ref,
    dz_ref, tokg_ref, inlog_ref, carry_ref, dstate, dxt,
):
    inner = dy_ref.shape[1]
    pair_width = 2 * inner // heads

    @pl.when(pl.program_id(0) == 0)
    def _():
        dstate[...] = ds0_ref[...]

    tok = tok_ref[...]
    tok_bf = tok.astype(BF)
    xc = mixed_ref[:, :inner].astype(F32)
    dt_wide = dot(tok_bf, spread_ref[...])
    xt = (xc * dt_wide).astype(BF)
    b_rows = mixed_ref[:, inner : inner + STATE]
    c_rows = mixed_ref[:, inner + STATE :]
    ent = dot(tok_bf, spread_ent_ref[...])
    leave = dot(tok_bf, spread_leave_ref[...])
    dy = dy_ref[...]
    sin = sin_ref[0]
    ds = dstate[...]
    ds_bf = ds.astype(BF)
    dye = dy.astype(F32) * ent
    tokg = dot((dye * dot(c_rows, sin)).astype(BF), gather_ref[1])
    dye = dye.astype(BF)
    dc = dot_tt(dye, sin)
    xt_f = xt.astype(F32)
    dx_state = dot(b_rows, ds_bf) * leave
    dxt[...] = dx_state
    tokg = tokg + dot((xt_f * dx_state).astype(BF), gather_ref[2])
    db = dot_tt((xt_f * leave).astype(BF), ds_bf)
    carry_ref[0] = jnp.sum(ds * sin.astype(F32), axis=0, keepdims=True)
    dstate[...] = ds * decay_ref[0] + dot_00(c_rows, dye)
    mask = linked_mask(seg_ref[...], segrow_ref[...])
    cross = jnp.where(mask, dot_tt(c_rows, b_rows), 0.0)
    later = lax.broadcasted_iota(jnp.int32, (CHUNK, CHUNK), 0)
    earlier = lax.broadcasted_iota(jnp.int32, (CHUNK, CHUNK), 1)
    before = (later < earlier).astype(BF)
    upto = (later >= earlier).astype(F32)
    cum_rows = cum_ref[...]
    dcross = jnp.zeros((CHUNK, CHUNK), F32)
    for j in range(heads // 2):
        at = slice(j * pair_width, (j + 1) * pair_width)
        xp = xt[:, at]
        dys = two_heads(dy[:, at])
        lefts = []
        for i in (0, 1):
            head = 2 * j + i
            decay = decay_pair(tok, cum_rows, head, heads)
            lefts.append((cross * decay).astype(BF))
            w = dot_tt(dys[i], xp) * decay
            dcross = dcross + w
            spans = dot((w * cross).astype(BF), before)
            inlog_ref[head : head + 1, :] = jnp.sum(spans * upto, axis=0, keepdims=True)
        dxt[:, at] += dot_00(jnp.concatenate(lefts, axis=0), jnp.concatenate(dys, axis=0))
    dcross = jnp.where(mask, dcross, 0.0).astype(BF)
    dc = dc + dot(dcross, b_rows)
    db = db + dot_00(dcross, c_rows)
    dx = dxt[...]
    tokg_ref[...] = tokg + dot((xc * dx).astype(BF), gather_ref[0])
    slope = slope_ref[...].astype(F32)
    dz_ref[:, :inner] = ((dx * dt_wide + skip_ref[...] * dy.astype(F32)) * slope[:, :inner]).astype(BF)
    dz_ref[:, inner : inner + STATE] = (db * slope[:, inner : inner + STATE]).astype(BF)
    dz_ref[:, inner + STATE :] = (dc * slope[:, inner + STATE :]).astype(BF)


def add(a, b):
    return (a.astype(F32) + b.astype(F32)).astype(BF)


def across(value, axis, bit):
    count = lax.axis_size(axis)
    return lax.ppermute(value, axis, [(i, i ^ bit) for i in range(count)])


def direct():
    return lax.axis_size("wsh") == 4 and lax.axis_size("seq") == 8


def fetch(half):
    rows = half.shape[0] // 2
    by_x, by_y = across(half, "wsh", 1), across(half, "wsh", 2)
    far_a, far_b = across(by_y[:rows], "wsh", 1), across(by_x[rows:], "wsh", 2)
    return by_x, by_y, far_a, far_b


def gather_weights(shard, gate_shard, out_shard):
    if not direct():
        full = [lax.all_gather(v, "wsh", axis=0, tiled=True) for v in (shard, gate_shard, out_shard)]
        return full[0], lambda value: (full[1], full[2], value)
    core, w = lax.axis_index("seq") % 2, lax.axis_index("wsh")
    rows = shard.shape[0]
    half, quarter = rows // 2, rows // 4
    own = lax.dynamic_slice_in_dim(shard, core * half, half, 0)
    by_x, by_y = across(own, "wsh", 1), across(own, "wsh", 2)
    far_a, far_b = across(by_y[:quarter], "wsh", 1), across(by_x[quarter:], "wsh", 2)
    far_a, far_b, gate_shard, out_shard = lax.optimization_barrier((far_a, far_b, gate_shard, out_shard))
    out = lax.dynamic_update_slice_in_dim(
        jnp.zeros((4 * rows, shard.shape[1]), shard.dtype), shard, w * rows, 0
    )
    for piece, k, extra in ((by_x, 1, 0), (by_y, 2, 0), (far_a, 3, 0), (far_b, 3, quarter)):
        other = across(piece, "seq", 1)
        for part, place in ((piece, core), (other, 1 - core)):
            out = lax.dynamic_update_slice_in_dim(out, part, (w ^ k) * rows + place * half + extra, 0)
    core_half, finish = gather_two(gate_shard, out_shard)

    def rest(value):
        held, value = lax.optimization_barrier((core_half, value))
        return finish(held) + (value,)

    return out, rest


def gather_two(gate_shard, out_shard):
    core, w = lax.axis_index("seq") % 2, lax.axis_index("wsh")
    rows = gate_shard.shape[0]
    folded = jnp.concatenate([out_shard[:rows], out_shard[rows:]], axis=1)
    pieces = fetch(jnp.where(core == 0, gate_shard, folded))
    width = out_shard.shape[1]

    def finish(pieces):
        mine = jnp.concatenate(pieces, axis=0)
        other = across(mine, "seq", 1)
        gates, outs = jnp.where(core == 0, mine, other), jnp.where(core == 0, other, mine)
        gate_full = lax.dynamic_update_slice_in_dim(
            jnp.zeros((4 * rows, gate_shard.shape[1]), BF), gate_shard, w * rows, 0
        )
        out_full = lax.dynamic_update_slice_in_dim(
            jnp.zeros((8 * rows, width), BF), out_shard, w * 2 * rows, 0
        )
        for k in (1, 2, 3):
            at = slice((k - 1) * rows, k * rows)
            gate_full = lax.dynamic_update_slice_in_dim(gate_full, gates[at], (w ^ k) * rows, 0)
            for i in (0, 1):
                piece = outs[at, i * width : (i + 1) * width]
                out_full = lax.dynamic_update_slice_in_dim(out_full, piece, ((w ^ k) * 2 + i) * rows, 0)
        return gate_full, out_full

    return pieces, finish


def columns_for(left, place):
    w = lax.axis_index("wsh")
    rows = left.shape[1] // 4
    half = rows // 2
    return jnp.concatenate(
        [lax.dynamic_slice_in_dim(left, (w ^ k) * rows + place * half, half, 1) for k in range(4)], axis=1
    )


def cut(value, i):
    rows = value.shape[0] // 2
    return lax.dynamic_slice_in_dim(value, i * rows, rows, 0)


def join(own, other, i):
    return jnp.where(i == 0, jnp.concatenate([own, other]), jnp.concatenate([other, own]))


def gather_z(part):
    if not direct():
        return lax.all_gather(part, "seq", axis=0, tiled=True, axis_index_groups=same_core())
    z = lax.axis_index("seq") // 2
    rows = part.shape[0]
    pair = join(part, across(part, "seq", 4), z // 2)
    other = across(pair, "seq", 2)
    return jnp.concatenate([join(pair[at : at + rows], other[at : at + rows], z % 2) for at in (0, rows)])


def reduce_product(left, right, beside, first, held, after):
    if not direct():
        term = dot_00(left, right).astype(BF)
        part = lax.psum_scatter(term, "wsh", scatter_dimension=0, tiled=True)
        return lax.psum(part, "seq"), gather_z(beside), first(held), after(right)
    me = lax.axis_index("seq")
    core, z = me % 2, me // 2
    sent = across(dot_00(columns_for(left, 1 - core), right).astype(BF), "seq", 1)
    chip = add(dot_00(columns_for(left, core), right), sent)
    chip, beside, held = lax.optimization_barrier((chip, beside, held))
    first = first(held)
    beside = gather_z(beside)
    half = chip.shape[0] // 4
    quarter = half // 2
    a = [chip[k * half : k * half + quarter] for k in range(4)]
    b = [chip[k * half + quarter : (k + 1) * half] for k in range(4)]
    by_x = across(jnp.concatenate([a[1], a[3]], axis=0), "wsh", 1)
    by_y = across(jnp.concatenate([b[2], b[3]], axis=0), "wsh", 2)
    by_x, by_y, first = lax.optimization_barrier((by_x, by_y, first))
    a2, b1, right = lax.optimization_barrier(
        (add(a[2], by_x[quarter:]), add(b[1], by_y[quarter:]), right)
    )
    a2, b1 = across(a2, "wsh", 2), across(b1, "wsh", 1)
    plane = jnp.concatenate([add(add(a[0], by_x[:quarter]), a2), add(add(b[0], by_y[:quarter]), b1)], axis=0)
    z_low, z_high = z % 2, z // 2
    plane, beside = lax.optimization_barrier((plane, beside))
    one = add(cut(plane, z_low), across(cut(plane, 1 - z_low), "seq", 2))
    one, after = lax.optimization_barrier((one, after(right)))
    two = add(cut(one, z_high), across(cut(one, 1 - z_high), "seq", 4))
    one = join(two, across(two, "seq", 4), z_high)
    all_z = join(one, across(one, "seq", 2), z_low)
    return join(all_z, across(all_z, "seq", 1), core), beside, first, after


def widen_kernel(gate_ref, x_ref, out_ref):
    inner = gate_ref.shape[1]
    for ref, first, end in ((gate_ref, 0, inner), (x_ref, inner, out_ref.shape[0])):
        for at in range(0, end - first, CHUNK):
            count = min(CHUNK, end - first - at)
            turned = ref[:, at : at + CHUNK].astype(F32).T
            out_ref[first + at : first + at + count, :] = turned[:count]


def core_sums(normed, dgate, gated_out, cot):
    planes = lax.axis_size("wsh")
    core = lax.axis_index("seq") % 2
    half = normed.shape[1] // planes // 2

    def product(left, start, right):
        rows = left.shape[1] // planes
        picked = [lax.dynamic_slice_in_dim(left, w * rows + start, half, 1) for w in range(planes)]
        return dot_00(jnp.concatenate(picked, axis=1), right).astype(BF)

    def part(place):
        outs = [product(gated_out, (2 * place + i) * half, cot) for i in (0, 1)]
        return jnp.concatenate([product(normed, place * half, dgate)] + outs, axis=1)

    sent = across(part(1 - core), "seq", 1)
    return add(part(core), sent)


def sum_over(value, axis, groups, count):
    every = lax.all_to_all(
        value, axis, split_axis=0, concat_axis=0, tiled=True, axis_index_groups=groups
    )
    rows = every.shape[0] // count
    total = every[:rows].astype(F32)
    for i in range(1, count):
        total = total + every[i * rows : (i + 1) * rows].astype(F32)
    return total.astype(BF)


def same_core():
    seqs = lax.axis_size("seq")
    return [list(range(i, seqs, 2)) for i in (0, 1)]


def spread_back(part, inner):
    core = lax.axis_index("seq") % 2
    other = across(part, "seq", 1)
    low, high = jnp.where(core == 0, part, other), jnp.where(core == 0, other, part)
    width = (part.shape[1] - inner) // 2
    outs = [v[:, inner + i * width : inner + (i + 1) * width] for v in (low, high) for i in (0, 1)]
    return (
        jnp.concatenate([low[:, :inner], high[:, :inner]], axis=0),
        jnp.concatenate(outs, axis=0).astype(F32),
    )


def sum_small(parts):
    if not direct():
        return lax.psum(parts, ("seq", "wsh"))
    flat = jnp.concatenate([p.reshape(-1) for p in parts])
    size = flat.shape[0]
    flat = jnp.pad(flat, (0, -size % 1024)).reshape(-1, 128)
    for axis, bit in (("seq", 1), ("seq", 2), ("seq", 4), ("wsh", 1), ("wsh", 2)):
        flat = flat + across(flat, axis, bit)
    flat = flat.reshape(-1)
    out, at = [], 0
    for p in parts:
        out.append(flat[at : at + p.size].reshape(p.shape))
        at += p.size
    return tuple(out)


def on_device(
    x_in, seg_ids, g_norm, w_in, conv_w, conv_b, dt_bias, a_log, d_skip, g_gate, w_out, cotangent
):
    seqs = lax.axis_size("seq")
    me = lax.axis_index("seq")
    toks = x_in.shape[1]
    width = x_in.shape[2]
    inner = g_gate.shape[0]
    heads = dt_bias.shape[0]
    head_width = inner // heads
    conv_width = conv_w.shape[1]
    taps = conv_w.shape[0]
    chunks = toks // CHUNK
    sds = jax.ShapeDtypeStruct

    used = w_in.shape[1] - inner
    wx, finish_weights = gather_weights(jnp.pad(w_in[:, inner:], ((0, 0), (0, -used % 128))), w_in[:, :inner], w_out)

    up = [(i, i + 1) for i in range(seqs - 1)]
    down = [(i + 1, i) for i in range(seqs - 1)]
    halo = lax.ppermute(x_in[0, toks - HALO :], "seq", up)
    x_ext = jnp.concatenate([halo, x_in[0]], axis=0).astype(F32)
    r_ext = lax.rsqrt(jnp.mean(x_ext * x_ext, axis=1, keepdims=True) + EPSILON)
    start = me * toks
    seg_pad = jnp.concatenate([jnp.full((HALO,), -1, jnp.int32), seg_ids[0], jnp.full((8,), -2, jnp.int32)])
    near = lax.dynamic_slice_in_dim(seg_pad, start, toks + HALO + 8, 0)
    seg = near[HALO : HALO + toks]
    keep = jnp.stack([(near[HALO - k : HALO - k + toks] == seg) for k in range(taps)], axis=1).astype(F32)
    ext_seg = near[: toks + HALO]
    place = jnp.arange(toks + HALO)
    keep_next = jnp.stack(
        [(near[k : k + toks + HALO] == ext_seg) & (place + k < toks + HALO) for k in range(taps)], axis=1
    ).astype(F32)
    seg_before = near[HALO - 1]
    seg_f = seg.astype(F32)
    seg_chunk = seg.reshape(chunks, CHUNK)
    last_chunk = seg_chunk[:, -1]
    prev_chunk = jnp.concatenate([seg_before[None], last_chunk[:-1]])
    lanes = 4 * heads
    owner = jnp.arange(inner)[None, :] // head_width
    slot = jnp.arange(lanes)[:, None]
    spread, spread_ent, spread_leave = [(slot == owner + i * heads).astype(BF) for i in (0, 2, 3)]
    gather = jnp.stack([(slot == owner + i * heads).astype(BF).T for i in (0, 1, 2)])
    skip_wide = jnp.repeat(d_skip, head_width)[None, :]
    tri = jnp.tril(jnp.ones((CHUNK, CHUNK), F32))
    seg_row = seg_f[None, :]
    seg_col = seg_f[:, None]
    fixed = (keep, seg_row, seg_col, spread, spread_ent, spread_leave, skip_wide)
    x_ext, fixed = lax.optimization_barrier((x_ext, fixed))
    keep, seg_row, seg_col, spread, spread_ent, spread_leave, skip_wide = fixed
    normed_ext = (x_ext * r_ext * g_norm[None, :]).astype(BF)
    normed = normed_ext[HALO:]
    proj = dot(normed_ext, wx).astype(BF)

    step_raw = proj[HALO:, conv_width : conv_width + heads].astype(F32) + dt_bias[None, :]
    dt = jax.nn.softplus(step_raw)
    rates = -jnp.exp(a_log)
    logs = (dt * rates[None, :]).reshape(chunks, CHUNK, heads)
    cum = jnp.einsum("ts,csh->cth", tri, logs, precision=EXACT)
    last = cum[:, -1]
    before = jnp.einsum("cd,dh->ch", jnp.tril(jnp.ones((chunks, chunks), F32), -1), last, precision=EXACT)
    after = jnp.einsum("cd,dh->ch", jnp.triu(jnp.ones((chunks, chunks), F32), 1), last, precision=EXACT)
    total_log = jnp.sum(last, axis=0)
    enter = jnp.exp(cum) * (seg_chunk == prev_chunk[:, None])[:, :, None]
    leave_log = last[:, None] - cum
    leave = jnp.exp(leave_log) * (seg_chunk == last_chunk[:, None])[:, :, None]
    far_enter = jnp.exp(cum + before[:, None]) * (seg_chunk == seg_before)[:, :, None]
    far_leave = (
        jnp.exp(leave_log + after[:, None]) * (seg_chunk == seg[-1])[:, :, None] * dt.reshape(chunks, CHUNK, heads)
    )
    chunk_decay = jnp.exp(last) * (last_chunk == prev_chunk)[:, None]
    decay_wide = jnp.repeat(chunk_decay, head_width, axis=1)[:, None, :]
    flat = lambda v: v.reshape(toks, heads)
    tok = jnp.concatenate([dt, flat(cum), flat(enter), flat(leave)], axis=1)
    far = jnp.concatenate([flat(far_leave), flat(far_leave), flat(far_enter), flat(far_enter)], axis=1)
    cum_rows = flat(cum).T
    block = conv_width // 3
    mixed, slope = pl.pallas_call(
        conv_kernel,
        grid=(conv_width // block,),
        in_specs=[
            pl.BlockSpec((toks + HALO, block), lambda i: (0, i)),
            pl.BlockSpec((toks, taps), lambda i: (0, 0)),
            pl.BlockSpec((taps, block), lambda i: (0, i)),
            pl.BlockSpec((1, block), lambda i: (0, i)),
        ],
        out_specs=[pl.BlockSpec((toks, block), lambda i: (0, i))] * 2,
        out_shape=[sds((toks, conv_width), BF)] * 2,
        scratch_shapes=[pltpu.VMEM((toks + HALO, block), F32)],
        compiler_params=params(),
        name="conv",
    )(proj, keep, conv_w, conv_b[None, :])

    rows = lambda n: pl.BlockSpec((CHUNK, n), lambda i: (i, 0))
    whole = lambda a, b: pl.BlockSpec((a, b), lambda i: (0, 0))
    own_state = pl.pallas_call(
        state_kernel,
        grid=(chunks,),
        in_specs=[rows(conv_width), rows(lanes), whole(lanes, inner), whole(1, inner)],
        out_specs=whole(STATE + 3 * HALO, inner),
        out_shape=sds((STATE + 3 * HALO, inner), BF),
        scratch_shapes=[pltpu.VMEM((STATE, inner), F32)],
        compiler_params=params(),
        name="own_state",
    )(mixed, far, spread, jnp.repeat(total_log, head_width)[None, :])

    every = lax.all_gather(own_state, "seq", axis=0)
    logs_all = sum(every[:, STATE + i * HALO].astype(F32) for i in range(3))
    ids = jnp.arange(seqs)
    ends = seg_ids[0].reshape(seqs, toks)[:, -1]
    starts_before = jnp.concatenate([jnp.full((1,), -1, jnp.int32), ends[:-1]])
    between = (ids[None, :] > jnp.minimum(ids, me)[:, None]) & (ids[None, :] < jnp.maximum(ids, me)[:, None])
    gap = jnp.exp(jnp.sum(jnp.where(between[:, :, None], logs_all[None], 0.0), axis=1))
    from_past = gap * ((ids < me) & (ends == seg_before))[:, None]
    from_next = gap * ((ids > me) & (starts_before == seg[-1]))[:, None]

    def combine(states, weights):
        return jnp.sum(states[:, :STATE].astype(F32) * weights[:, None, :], axis=0)

    y_inside = pl.pallas_call(
        partial(inside_kernel, heads),
        grid=(chunks,),
        in_specs=[
            rows(conv_width), rows(lanes), rows(1),
            pl.BlockSpec((heads, CHUNK), lambda i: (0, i)),
            pl.BlockSpec((1, CHUNK), lambda i: (0, i)),
            whole(lanes, inner), whole(1, inner),
        ],
        out_specs=rows(inner),
        out_shape=sds((toks, inner), BF),
        compiler_params=params(),
        name="inside",
    )(mixed, tok, seg_col, cum_rows, seg_row, spread, skip_wide)
    wg, wo, y_inside = finish_weights(y_inside)
    gate = dot(normed, wg).astype(BF)
    cot = cotangent[0]
    back = dot_tt(cot, wo).astype(BF)
    first_state = combine(every, from_past)

    states, gated_out, dgate, dy, dgain, dskip_wide, own_ds = pl.pallas_call(
        gate_kernel,
        grid=(chunks,),
        in_specs=[
            rows(inner), rows(conv_width), rows(inner), rows(inner), rows(lanes), rows(lanes),
            pl.BlockSpec((1, 1, inner), lambda i: (i, 0, 0)),
            whole(1, inner), whole(STATE, inner),
            whole(lanes, inner), whole(lanes, inner), whole(lanes, inner),
        ],
        out_specs=[
            pl.BlockSpec((1, STATE, inner), lambda i: (i, 0, 0)),
            rows(inner), rows(inner), rows(inner),
            whole(1, inner), whole(1, inner), whole(STATE, inner),
        ],
        out_shape=[
            sds((chunks, STATE, inner), BF),
            sds((toks, inner), BF), sds((toks, inner), BF), sds((toks, inner), BF),
            sds((1, inner), F32), sds((1, inner), F32), sds((STATE, inner), BF),
        ],
        scratch_shapes=[pltpu.VMEM((STATE, inner), F32)] * 2,
        compiler_params=params(),
        name="gate",
    )(y_inside, mixed, gate, back, tok, far, decay_wide, g_gate[None, :], first_state, spread, spread_ent, spread_leave)

    last_ds = combine(lax.all_gather(own_ds, "seq", axis=0), from_next)
    later, dgate = lax.optimization_barrier((normed, dgate))
    sums = core_sums(later, dgate, gated_out, cot)
    dn_gate = dot_tt(dgate, wg)
    last_ds, dn_gate = lax.optimization_barrier((last_ds, dn_gate))
    sums = sum_over(sums, "wsh", None, lax.axis_size("wsh"))

    flip = lambda n: pl.BlockSpec((CHUNK, n), lambda i: (chunks - 1 - i, 0))
    dz, tokg, inlog, carry = pl.pallas_call(
        partial(back_kernel, heads),
        grid=(chunks,),
        in_specs=[
            flip(inner), flip(conv_width), flip(conv_width), flip(lanes), flip(1),
            pl.BlockSpec((heads, CHUNK), lambda i: (0, chunks - 1 - i)),
            pl.BlockSpec((1, CHUNK), lambda i: (0, chunks - 1 - i)),
            pl.BlockSpec((1, 1, inner), lambda i: (chunks - 1 - i, 0, 0)),
            whole(1, inner),
            pl.BlockSpec((1, STATE, inner), lambda i: (chunks - 1 - i, 0, 0)),
            whole(STATE, inner),
            whole(lanes, inner), whole(lanes, inner), whole(lanes, inner),
            pl.BlockSpec((3, inner, lanes), lambda i: (0, 0, 0)),
        ],
        out_specs=[
            flip(conv_width), flip(lanes),
            pl.BlockSpec((heads, CHUNK), lambda i: (0, chunks - 1 - i)),
            pl.BlockSpec((1, 1, inner), lambda i: (chunks - 1 - i, 0, 0)),
        ],
        out_shape=[
            sds((toks, conv_width), BF), sds((toks, lanes), F32), sds((heads, toks), F32),
            sds((chunks, 1, inner), F32),
        ],
        scratch_shapes=[pltpu.VMEM((STATE, inner), F32), pltpu.VMEM((CHUNK, inner), F32)],
        compiler_params=params(),
        name="scan_back",
    )(
        dy, mixed, slope, tok, seg_col, cum_rows, seg_row, decay_wide, skip_wide, states, last_ds,
        spread, spread_ent, spread_leave, gather,
    )

    dz, sums = lax.optimization_barrier((dz, sums))
    sums = sum_over(sums, "seq", same_core(), seqs // 2)

    dxbc, dconv_w, dconv_b = pl.pallas_call(
        conv_back_kernel,
        grid=(conv_width // block,),
        in_specs=[
            pl.BlockSpec((toks, block), lambda i: (0, i)),
            pl.BlockSpec((toks + HALO, block), lambda i: (0, i)),
            pl.BlockSpec((toks, taps), lambda i: (0, 0)),
            pl.BlockSpec((toks + HALO, taps), lambda i: (0, 0)),
            pl.BlockSpec((taps, block), lambda i: (0, i)),
        ],
        out_specs=[
            pl.BlockSpec((toks + HALO, block), lambda i: (0, i)),
            pl.BlockSpec((taps, block), lambda i: (0, i)),
            pl.BlockSpec((1, block), lambda i: (0, i)),
        ],
        out_shape=[
            sds((toks + HALO, conv_width), BF), sds((taps, conv_width), F32), sds((1, conv_width), F32),
        ],
        scratch_shapes=[
            pltpu.VMEM((toks + HALO, block), F32), pltpu.VMEM((toks + HALO + 8, block), F32),
        ],
        compiler_params=params(),
        name="conv_back",
    )(dz, proj, keep, keep_next, conv_w)

    tokg = tokg.reshape(chunks, CHUNK, lanes)
    from_dx, from_enter, from_leave = [tokg[:, :, i * heads : (i + 1) * heads] for i in range(3)]
    whole_chunk = jnp.sum(carry.reshape(chunks, heads, head_width), axis=2) * chunk_decay
    dlog = (
        inlog.T.reshape(chunks, CHUNK, heads)
        + jnp.einsum("ut,cth->cuh", tri.T, from_enter, precision=EXACT)
        + jnp.einsum("us,csh->cuh", tri - jnp.eye(CHUNK, dtype=F32), from_leave, precision=EXACT)
        + whole_chunk[:, None, :]
    )
    dlog = flat(dlog)
    drate = jnp.sum(dlog * dt, axis=0)
    dstep = (flat(from_dx) + dlog * rates[None, :]) * jax.nn.sigmoid(step_raw)
    dstep_bf = dstep.astype(BF)

    dxbc, sums = lax.optimization_barrier((dxbc, sums))
    dproj = jnp.concatenate([dxbc, jnp.pad(dstep_bf, ((HALO, 0), (0, -heads % 128)))], axis=1)

    def input_grads(dproj):
        dn_ext = dot_tt(dproj, wx)
        over = lax.ppermute(dn_ext[:HALO], "seq", down)
        dn = dn_ext[HALO:] + dn_gate
        return dn + jnp.pad(over, ((toks - HALO, 0), (0, 0)))

    x_f = x_ext[HALO:]
    r = r_ext[HALO:]

    def after_product(dproj):
        dn = input_grads(dproj)
        f = dn * g_norm[None, :]
        x_grad = cot.astype(F32) + r * f - x_f * (r * r * r) * jnp.mean(f * x_f, axis=1, keepdims=True)
        return x_grad, jnp.sum(dn * x_f * r, axis=0)

    x_rows, sums, result, (x_grad, g_norm_part) = reduce_product(
        normed_ext, dproj, sums, lambda left: (x_f + dot(left, wo)).astype(BF), gated_out, after_product
    )
    gate_rows, w_out_grad = spread_back(sums, inner)
    w_in_grad = pl.pallas_call(
        widen_kernel,
        out_shape=sds(w_in.shape[::-1], F32),
        in_specs=[pl.BlockSpec(memory_space=pltpu.VMEM)] * 2,
        out_specs=pl.BlockSpec(memory_space=pltpu.VMEM),
        compiler_params=pltpu.CompilerParams(vmem_limit_bytes=VMEM_LIMIT),
        name="widen",
    )(gate_rows, x_rows).T
    small = (
        g_norm_part,
        dconv_w,
        dconv_b[0],
        jnp.sum(dstep, axis=0),
        drate * rates,
        jnp.sum(dskip_wide.reshape(heads, head_width), axis=1),
        dgain[0],
    )
    small = sum_small(small)
    return (result[None], x_grad[None], small[0], w_in_grad) + tuple(small[1:]) + (w_out_grad,)


def solution(mesh):
    tokens = P("wsh", "seq", None)
    owned = P("wsh", None)
    return jax.shard_map(
        on_device,
        mesh=mesh,
        in_specs=(tokens, owned, P(), owned, P(), P(), P(), P(), P(), P(), owned, tokens),
        out_specs=(tokens, tokens, P(), owned, P(), P(), P(), P(), P(), P(), owned),
        check_vma=False,
    )
```

```python
from functools import partial

import jax
import jax.numpy as jnp
from jax import lax
from jax.experimental import pallas as pl
from jax.experimental.pallas import tpu as pltpu
from jax.sharding import PartitionSpec as P

STATE = 128
CHUNK = 128
HALO = 16
STRIP = 32
EPSILON = 1e-05
EXACT = lax.Precision.HIGHEST
BF = jnp.bfloat16
F32 = jnp.float32
VMEM_LIMIT = 56 * 1024 * 1024


def dot(a, b):
    return jnp.dot(a, b, preferred_element_type=F32)


def dot_tt(a, b):
    return lax.dot_general(a, b, (((1,), (1,)), ((), ())), preferred_element_type=F32)


def dot_00(a, b):
    return lax.dot_general(a, b, (((0,), (0,)), ((), ())), preferred_element_type=F32)


def sigmoid(v):
    return 0.5 + 0.5 * jnp.tanh(0.5 * v)


def params():
    return pltpu.CompilerParams(vmem_limit_bytes=VMEM_LIMIT, dimension_semantics=("arbitrary",))


def conv_kernel(x_ref, keep_ref, w_ref, b_ref, mixed_ref, slope_ref, buf):
    rows = mixed_ref.shape[0]
    buf[...] = x_ref[...].astype(F32)
    taps = w_ref.shape[0]
    for start in range(0, rows, STRIP):
        keep = keep_ref[start : start + STRIP, :]
        total = b_ref[...] + w_ref[taps - 1 : taps, :] * buf[HALO + start : HALO + start + STRIP, :]
        for k in range(1, taps):
            moved = buf[HALO + start - k : HALO + start - k + STRIP, :]
            total = total + w_ref[taps - 1 - k : taps - k, :] * (moved * keep[:, k : k + 1])
        sg = sigmoid(total)
        mixed = total * sg
        mixed_ref[start : start + STRIP, :] = mixed.astype(BF)
        slope_ref[start : start + STRIP, :] = (sg + mixed * (1.0 - sg)).astype(BF)


def conv_back_kernel(dz_ref, x_ref, keep_ref, next_ref, w_ref, dx_ref, dw_ref, db_ref, buf, dbuf):
    rows, width = dz_ref.shape
    taps = w_ref.shape[0]
    buf[...] = x_ref[...].astype(F32)
    dbuf[0:HALO, :] = jnp.zeros((HALO, width), F32)
    dbuf[HALO : HALO + rows, :] = dz_ref[...].astype(F32)
    dbuf[HALO + rows :, :] = jnp.zeros((8, width), F32)
    sums = [jnp.zeros((8, width), F32) for _ in range(taps + 1)]
    eights = lambda v: jnp.sum(v.reshape(STRIP // 8, 8, width), axis=0)
    for start in range(0, rows, STRIP):
        keep = keep_ref[start : start + STRIP, :]
        dz = dbuf[HALO + start : HALO + start + STRIP, :]
        sums[taps] = sums[taps] + eights(dz)
        for k in range(taps):
            moved = buf[HALO + start - k : HALO + start - k + STRIP, :]
            if k:
                moved = moved * keep[:, k : k + 1]
            sums[k] = sums[k] + eights(dz * moved)
    for k in range(taps):
        dw_ref[taps - 1 - k : taps - k, :] = jnp.sum(sums[k], axis=0, keepdims=True)
    db_ref[...] = jnp.sum(sums[taps], axis=0, keepdims=True)
    for start in range(0, rows + HALO, STRIP):
        count = min(STRIP, rows + HALO - start)
        total = w_ref[taps - 1 : taps, :] * dbuf[start : start + count, :]
        nxt = next_ref[start : start + count, :]
        for k in range(1, taps):
            moved = dbuf[start + k : start + k + count, :]
            total = total + w_ref[taps - 1 - k : taps - k, :] * (moved * nxt[:, k : k + 1])
        dx_ref[start : start + count, :] = total.astype(BF)


def state_kernel(mixed_ref, tok_ref, spread_ref, log_ref, s_ref, total):
    inner = s_ref.shape[1]

    @pl.when(pl.program_id(0) == 0)
    def _():
        total[...] = jnp.zeros_like(total)

    factor = dot(tok_ref[...].astype(BF), spread_ref[...])
    left = (mixed_ref[:, :inner].astype(F32) * factor).astype(BF)
    total[...] += dot_00(mixed_ref[:, inner : inner + STATE], left)

    @pl.when(pl.program_id(0) == pl.num_programs(0) - 1)
    def _():
        s_ref[:STATE, :] = total[...].astype(BF)
        rest = jnp.broadcast_to(log_ref[...], (HALO, inner))
        for i in range(3):
            piece = rest.astype(BF)
            s_ref[STATE + i * HALO : STATE + (i + 1) * HALO, :] = piece
            rest = rest - piece.astype(F32)


def decay_pair(tok, cum_rows, head, heads):
    gap = tok[:, heads + head : heads + head + 1] - cum_rows[head : head + 1, :]
    return jnp.exp(jnp.minimum(gap, 0.0))


def linked_mask(seg_col, seg_row):
    later = lax.broadcasted_iota(jnp.int32, (CHUNK, CHUNK), 0)
    earlier = lax.broadcasted_iota(jnp.int32, (CHUNK, CHUNK), 1)
    return (seg_col == seg_row) & (later >= earlier)


def two_heads(pair):
    lane = lax.broadcasted_iota(jnp.int32, pair.shape, 1)
    zero = jnp.zeros_like(pair)
    half = pair.shape[1] // 2
    return jnp.where(lane < half, pair, zero), jnp.where(lane >= half, pair, zero)


def inside_kernel(heads, mixed_ref, tok_ref, seg_ref, cum_ref, segrow_ref, spread_ref, skip_ref, y_ref):
    inner = y_ref.shape[1]
    pair_width = 2 * inner // heads
    tok = tok_ref[...]
    xc = mixed_ref[:, :inner].astype(F32)
    xt = (xc * dot(tok.astype(BF), spread_ref[...])).astype(BF)
    b_rows = mixed_ref[:, inner : inner + STATE]
    c_rows = mixed_ref[:, inner + STATE :]
    mask = linked_mask(seg_ref[...], segrow_ref[...])
    cross = jnp.where(mask, dot_tt(c_rows, b_rows), 0.0)
    cum_rows = cum_ref[...]
    for j in range(heads // 2):
        at = slice(j * pair_width, (j + 1) * pair_width)
        left = [(cross * decay_pair(tok, cum_rows, 2 * j + i, heads)).astype(BF) for i in (0, 1)]
        right = two_heads(xt[:, at])
        part = dot(jnp.concatenate(left, axis=1), jnp.concatenate(right, axis=0))
        y_ref[:, at] = (part + skip_ref[:, at] * xc[:, at]).astype(BF)


def gate_kernel(
    yi_ref, mixed_ref, gate_ref, back_ref, tok_ref, far_ref, decay_ref, gain_ref, s0_ref,
    spread_ref, spread_ent_ref, spread_leave_ref,
    sin_ref, out_ref, dgate_ref, dy_ref, dgain_ref, dskip_ref, ds_out_ref, state, ds_ref,
):
    inner = yi_ref.shape[1]

    @pl.when(pl.program_id(0) == 0)
    def _():
        state[...] = s0_ref[...]
        dgain_ref[...] = jnp.zeros_like(dgain_ref)
        dskip_ref[...] = jnp.zeros_like(dskip_ref)
        ds_ref[...] = jnp.zeros_like(ds_ref)

    xc = mixed_ref[:, :inner].astype(F32)
    b_rows = mixed_ref[:, inner : inner + STATE]
    c_rows = mixed_ref[:, inner + STATE :]
    tok = tok_ref[...].astype(BF)
    now = state[...]
    now_bf = now.astype(BF)
    sin_ref[0] = now_bf
    y = yi_ref[...].astype(F32) + dot(c_rows, now_bf) * dot(tok, spread_ent_ref[...])
    leave = (xc * dot(tok, spread_ref[...])) * dot(tok, spread_leave_ref[...])
    state[...] = now * decay_ref[0] + dot_00(b_rows, leave.astype(BF))
    gate = gate_ref[...].astype(F32)
    sg = sigmoid(gate)
    silu = gate * sg
    v = y * silu
    gain = gain_ref[...]
    q = lax.rsqrt(jnp.mean(v * v, axis=1, keepdims=True) + EPSILON)
    vq = v * q
    out_ref[...] = (vq * gain).astype(BF)
    back = back_ref[...].astype(F32)
    e = back * gain
    cross = jnp.mean(vq * e, axis=1, keepdims=True)
    dv = q * (e - vq * cross)
    dgain_ref[...] += jnp.sum(back * vq, axis=0, keepdims=True)
    dgate_ref[...] = (dv * y * (sg * (1.0 + gate * (1.0 - sg)))).astype(BF)
    dy = dv * silu
    dy_ref[...] = dy.astype(BF)
    dskip_ref[...] += jnp.sum(dy * xc, axis=0, keepdims=True)
    ds_ref[...] += dot_00(c_rows, (dy * dot(far_ref[...].astype(BF), spread_ent_ref[...])).astype(BF))

    @pl.when(pl.program_id(0) == pl.num_programs(0) - 1)
    def _():
        ds_out_ref[...] = ds_ref[...].astype(BF)


def back_kernel(
    heads, dy_ref, mixed_ref, slope_ref, tok_ref, seg_ref, cum_ref, segrow_ref, decay_ref, skip_ref, sin_ref, ds0_ref,
    spread_ref, spread_ent_ref, spread_leave_ref, gather_ref,
    dz_ref, tokg_ref, inlog_ref, carry_ref, dstate, dxt,
):
    inner = dy_ref.shape[1]
    pair_width = 2 * inner // heads

    @pl.when(pl.program_id(0) == 0)
    def _():
        dstate[...] = ds0_ref[...]

    tok = tok_ref[...]
    tok_bf = tok.astype(BF)
    xc = mixed_ref[:, :inner].astype(F32)
    dt_wide = dot(tok_bf, spread_ref[...])
    xt = (xc * dt_wide).astype(BF)
    b_rows = mixed_ref[:, inner : inner + STATE]
    c_rows = mixed_ref[:, inner + STATE :]
    ent = dot(tok_bf, spread_ent_ref[...])
    leave = dot(tok_bf, spread_leave_ref[...])
    dy = dy_ref[...]
    sin = sin_ref[0]
    ds = dstate[...]
    ds_bf = ds.astype(BF)
    dye = dy.astype(F32) * ent
    tokg = dot((dye * dot(c_rows, sin)).astype(BF), gather_ref[1])
    dye = dye.astype(BF)
    dc = dot_tt(dye, sin)
    xt_f = xt.astype(F32)
    dx_state = dot(b_rows, ds_bf) * leave
    dxt[...] = dx_state
    tokg = tokg + dot((xt_f * dx_state).astype(BF), gather_ref[2])
    db = dot_tt((xt_f * leave).astype(BF), ds_bf)
    carry_ref[0] = jnp.sum(ds * sin.astype(F32), axis=0, keepdims=True)
    dstate[...] = ds * decay_ref[0] + dot_00(c_rows, dye)
    mask = linked_mask(seg_ref[...], segrow_ref[...])
    cross = jnp.where(mask, dot_tt(c_rows, b_rows), 0.0)
    later = lax.broadcasted_iota(jnp.int32, (CHUNK, CHUNK), 0)
    earlier = lax.broadcasted_iota(jnp.int32, (CHUNK, CHUNK), 1)
    before = (later < earlier).astype(BF)
    upto = (later >= earlier).astype(F32)
    cum_rows = cum_ref[...]
    dcross = jnp.zeros((CHUNK, CHUNK), F32)
    for j in range(heads // 2):
        at = slice(j * pair_width, (j + 1) * pair_width)
        xp = xt[:, at]
        dys = two_heads(dy[:, at])
        lefts = []
        for i in (0, 1):
            head = 2 * j + i
            decay = decay_pair(tok, cum_rows, head, heads)
            lefts.append((cross * decay).astype(BF))
            w = dot_tt(dys[i], xp) * decay
            dcross = dcross + w
            spans = dot((w * cross).astype(BF), before)
            inlog_ref[head : head + 1, :] = jnp.sum(spans * upto, axis=0, keepdims=True)
        dxt[:, at] += dot_00(jnp.concatenate(lefts, axis=0), jnp.concatenate(dys, axis=0))
    dcross = jnp.where(mask, dcross, 0.0).astype(BF)
    dc = dc + dot(dcross, b_rows)
    db = db + dot_00(dcross, c_rows)
    dx = dxt[...]
    tokg_ref[...] = tokg + dot((xc * dx).astype(BF), gather_ref[0])
    slope = slope_ref[...].astype(F32)
    dz_ref[:, :inner] = ((dx * dt_wide + skip_ref[...] * dy.astype(F32)) * slope[:, :inner]).astype(BF)
    dz_ref[:, inner : inner + STATE] = (db * slope[:, inner : inner + STATE]).astype(BF)
    dz_ref[:, inner + STATE :] = (dc * slope[:, inner + STATE :]).astype(BF)


def add(a, b):
    return (a.astype(F32) + b.astype(F32)).astype(BF)


def across(value, axis, bit):
    count = lax.axis_size(axis)
    return lax.ppermute(value, axis, [(i, i ^ bit) for i in range(count)])


def direct():
    return lax.axis_size("wsh") == 4 and lax.axis_size("seq") == 8


def fetch(half):
    rows = half.shape[0] // 2
    by_x, by_y = across(half, "wsh", 1), across(half, "wsh", 2)
    far_a, far_b = across(by_y[:rows], "wsh", 1), across(by_x[rows:], "wsh", 2)
    return by_x, by_y, far_a, far_b


def gather_weights(shard, gate_shard, out_shard):
    if not direct():
        full = [lax.all_gather(v, "wsh", axis=0, tiled=True) for v in (shard, gate_shard, out_shard)]
        return full[0], lambda value: (full[1], full[2], value)
    core, w = lax.axis_index("seq") % 2, lax.axis_index("wsh")
    rows = shard.shape[0]
    half, quarter = rows // 2, rows // 4
    own = lax.dynamic_slice_in_dim(shard, core * half, half, 0)
    by_x, by_y = across(own, "wsh", 1), across(own, "wsh", 2)
    far_a, far_b = across(by_y[:quarter], "wsh", 1), across(by_x[quarter:], "wsh", 2)
    far_a, far_b, gate_shard, out_shard = lax.optimization_barrier((far_a, far_b, gate_shard, out_shard))
    out = lax.dynamic_update_slice_in_dim(
        jnp.zeros((4 * rows, shard.shape[1]), shard.dtype), shard, w * rows, 0
    )
    for piece, k, extra in ((by_x, 1, 0), (by_y, 2, 0), (far_a, 3, 0), (far_b, 3, quarter)):
        other = across(piece, "seq", 1)
        for part, place in ((piece, core), (other, 1 - core)):
            out = lax.dynamic_update_slice_in_dim(out, part, (w ^ k) * rows + place * half + extra, 0)
    core_half, finish = gather_two(gate_shard, out_shard)

    def rest(value):
        return finish(core_half) + (value,)

    return out, rest


def gather_two(gate_shard, out_shard):
    core, w = lax.axis_index("seq") % 2, lax.axis_index("wsh")
    rows = gate_shard.shape[0]
    folded = jnp.concatenate([out_shard[:rows], out_shard[rows:]], axis=1)
    pieces = fetch(jnp.where(core == 0, gate_shard, folded))
    width = out_shard.shape[1]

    def finish(pieces):
        mine = jnp.concatenate(pieces, axis=0)
        other = across(mine, "seq", 1)
        gates, outs = jnp.where(core == 0, mine, other), jnp.where(core == 0, other, mine)
        gate_full = lax.dynamic_update_slice_in_dim(
            jnp.zeros((4 * rows, gate_shard.shape[1]), BF), gate_shard, w * rows, 0
        )
        out_full = lax.dynamic_update_slice_in_dim(
            jnp.zeros((8 * rows, width), BF), out_shard, w * 2 * rows, 0
        )
        for k in (1, 2, 3):
            at = slice((k - 1) * rows, k * rows)
            gate_full = lax.dynamic_update_slice_in_dim(gate_full, gates[at], (w ^ k) * rows, 0)
            for i in (0, 1):
                piece = outs[at, i * width : (i + 1) * width]
                out_full = lax.dynamic_update_slice_in_dim(out_full, piece, ((w ^ k) * 2 + i) * rows, 0)
        return gate_full, out_full

    return pieces, finish


def columns_for(left, place):
    w = lax.axis_index("wsh")
    rows = left.shape[1] // 4
    half = rows // 2
    return jnp.concatenate(
        [lax.dynamic_slice_in_dim(left, (w ^ k) * rows + place * half, half, 1) for k in range(4)], axis=1
    )


def cut(value, i):
    rows = value.shape[0] // 2
    return lax.dynamic_slice_in_dim(value, i * rows, rows, 0)


def join(own, other, i):
    return jnp.where(i == 0, jnp.concatenate([own, other]), jnp.concatenate([other, own]))


def gather_z(part):
    if not direct():
        return lax.all_gather(part, "seq", axis=0, tiled=True, axis_index_groups=same_core())
    z = lax.axis_index("seq") // 2
    rows = part.shape[0]
    pair = join(part, across(part, "seq", 4), z // 2)
    other = across(pair, "seq", 2)
    return jnp.concatenate([join(pair[at : at + rows], other[at : at + rows], z % 2) for at in (0, rows)])


def reduce_product(left, right, beside, first, held, after):
    if not direct():
        term = dot_00(left, right).astype(BF)
        part = lax.psum_scatter(term, "wsh", scatter_dimension=0, tiled=True)
        return lax.psum(part, "seq"), gather_z(beside), first(held), after(right)
    me = lax.axis_index("seq")
    core, z = me % 2, me // 2
    sent = across(dot_00(columns_for(left, 1 - core), right).astype(BF), "seq", 1)
    chip = add(dot_00(columns_for(left, core), right), sent)
    chip, beside, held = lax.optimization_barrier((chip, beside, held))
    first = first(held)
    beside = gather_z(beside)
    half = chip.shape[0] // 4
    quarter = half // 2
    a = [chip[k * half : k * half + quarter] for k in range(4)]
    b = [chip[k * half + quarter : (k + 1) * half] for k in range(4)]
    by_x = across(jnp.concatenate([a[1], a[3]], axis=0), "wsh", 1)
    by_y = across(jnp.concatenate([b[2], b[3]], axis=0), "wsh", 2)
    by_x, by_y, first = lax.optimization_barrier((by_x, by_y, first))
    a2, b1, right = lax.optimization_barrier(
        (add(a[2], by_x[quarter:]), add(b[1], by_y[quarter:]), right)
    )
    a2, b1 = across(a2, "wsh", 2), across(b1, "wsh", 1)
    plane = jnp.concatenate([add(add(a[0], by_x[:quarter]), a2), add(add(b[0], by_y[:quarter]), b1)], axis=0)
    z_low, z_high = z % 2, z // 2
    plane, beside = lax.optimization_barrier((plane, beside))
    one = add(cut(plane, z_low), across(cut(plane, 1 - z_low), "seq", 2))
    one, after = lax.optimization_barrier((one, after(right)))
    two = add(cut(one, z_high), across(cut(one, 1 - z_high), "seq", 4))
    one = join(two, across(two, "seq", 4), z_high)
    all_z = join(one, across(one, "seq", 2), z_low)
    return join(all_z, across(all_z, "seq", 1), core), beside, first, after


def widen_kernel(gate_ref, x_ref, out_ref):
    inner = gate_ref.shape[1]
    for ref, first, end in ((gate_ref, 0, inner), (x_ref, inner, out_ref.shape[0])):
        for at in range(0, end - first, CHUNK):
            count = min(CHUNK, end - first - at)
            turned = ref[:, at : at + CHUNK].astype(F32).T
            out_ref[first + at : first + at + count, :] = turned[:count]


def core_sums(normed, dgate, gated_out, cot):
    planes = lax.axis_size("wsh")
    core = lax.axis_index("seq") % 2
    half = normed.shape[1] // planes // 2

    def product(left, start, right):
        rows = left.shape[1] // planes
        picked = [lax.dynamic_slice_in_dim(left, w * rows + start, half, 1) for w in range(planes)]
        return dot_00(jnp.concatenate(picked, axis=1), right).astype(BF)

    def part(place):
        outs = [product(gated_out, (2 * place + i) * half, cot) for i in (0, 1)]
        return jnp.concatenate([product(normed, place * half, dgate)] + outs, axis=1)

    sent = across(part(1 - core), "seq", 1)
    return add(part(core), sent)


def sum_over(value, axis, groups, count):
    every = lax.all_to_all(
        value, axis, split_axis=0, concat_axis=0, tiled=True, axis_index_groups=groups
    )
    rows = every.shape[0] // count
    total = every[:rows].astype(F32)
    for i in range(1, count):
        total = total + every[i * rows : (i + 1) * rows].astype(F32)
    return total.astype(BF)


def same_core():
    seqs = lax.axis_size("seq")
    return [list(range(i, seqs, 2)) for i in (0, 1)]


def spread_back(part, inner):
    core = lax.axis_index("seq") % 2
    other = across(part, "seq", 1)
    low, high = jnp.where(core == 0, part, other), jnp.where(core == 0, other, part)
    width = (part.shape[1] - inner) // 2
    outs = [v[:, inner + i * width : inner + (i + 1) * width] for v in (low, high) for i in (0, 1)]
    return (
        jnp.concatenate([low[:, :inner], high[:, :inner]], axis=0),
        jnp.concatenate(outs, axis=0).astype(F32),
    )


def sum_small(parts):
    if not direct():
        return lax.psum(parts, ("seq", "wsh"))
    flat = jnp.concatenate([p.reshape(-1) for p in parts])
    size = flat.shape[0]
    flat = jnp.pad(flat, (0, -size % 1024)).reshape(-1, 128)
    for axis, bit in (("seq", 1), ("seq", 2), ("seq", 4), ("wsh", 1), ("wsh", 2)):
        flat = flat + across(flat, axis, bit)
    flat = flat.reshape(-1)
    out, at = [], 0
    for p in parts:
        out.append(flat[at : at + p.size].reshape(p.shape))
        at += p.size
    return tuple(out)


def on_device(
    x_in, seg_ids, g_norm, w_in, conv_w, conv_b, dt_bias, a_log, d_skip, g_gate, w_out, cotangent
):
    seqs = lax.axis_size("seq")
    me = lax.axis_index("seq")
    toks = x_in.shape[1]
    width = x_in.shape[2]
    inner = g_gate.shape[0]
    heads = dt_bias.shape[0]
    head_width = inner // heads
    conv_width = conv_w.shape[1]
    taps = conv_w.shape[0]
    chunks = toks // CHUNK
    sds = jax.ShapeDtypeStruct

    used = w_in.shape[1] - inner
    wx, finish_weights = gather_weights(jnp.pad(w_in[:, inner:], ((0, 0), (0, -used % 128))), w_in[:, :inner], w_out)

    up = [(i, i + 1) for i in range(seqs - 1)]
    down = [(i + 1, i) for i in range(seqs - 1)]
    halo = lax.ppermute(x_in[0, toks - HALO :], "seq", up)
    x_ext = jnp.concatenate([halo, x_in[0]], axis=0).astype(F32)
    r_ext = lax.rsqrt(jnp.mean(x_ext * x_ext, axis=1, keepdims=True) + EPSILON)
    start = me * toks
    seg_pad = jnp.concatenate([jnp.full((HALO,), -1, jnp.int32), seg_ids[0], jnp.full((8,), -2, jnp.int32)])
    near = lax.dynamic_slice_in_dim(seg_pad, start, toks + HALO + 8, 0)
    seg = near[HALO : HALO + toks]
    keep = jnp.stack([(near[HALO - k : HALO - k + toks] == seg) for k in range(taps)], axis=1).astype(F32)
    ext_seg = near[: toks + HALO]
    place = jnp.arange(toks + HALO)
    keep_next = jnp.stack(
        [(near[k : k + toks + HALO] == ext_seg) & (place + k < toks + HALO) for k in range(taps)], axis=1
    ).astype(F32)
    seg_before = near[HALO - 1]
    seg_f = seg.astype(F32)
    seg_chunk = seg.reshape(chunks, CHUNK)
    last_chunk = seg_chunk[:, -1]
    prev_chunk = jnp.concatenate([seg_before[None], last_chunk[:-1]])
    lanes = 4 * heads
    owner = jnp.arange(inner)[None, :] // head_width
    slot = jnp.arange(lanes)[:, None]
    spread, spread_ent, spread_leave = [(slot == owner + i * heads).astype(BF) for i in (0, 2, 3)]
    gather = jnp.stack([(slot == owner + i * heads).astype(BF).T for i in (0, 1, 2)])
    skip_wide = jnp.repeat(d_skip, head_width)[None, :]
    tri = jnp.tril(jnp.ones((CHUNK, CHUNK), F32))
    seg_row = seg_f[None, :]
    seg_col = seg_f[:, None]
    fixed = (keep, seg_row, seg_col, spread, spread_ent, spread_leave, skip_wide)
    x_ext, fixed = lax.optimization_barrier((x_ext, fixed))
    keep, seg_row, seg_col, spread, spread_ent, spread_leave, skip_wide = fixed
    normed_ext = (x_ext * r_ext * g_norm[None, :]).astype(BF)
    normed = normed_ext[HALO:]
    proj = dot(normed_ext, wx).astype(BF)

    step_raw = proj[HALO:, conv_width : conv_width + heads].astype(F32) + dt_bias[None, :]
    dt = jax.nn.softplus(step_raw)
    rates = -jnp.exp(a_log)
    logs = (dt * rates[None, :]).reshape(chunks, CHUNK, heads)
    cum = jnp.einsum("ts,csh->cth", tri, logs, precision=EXACT)
    last = cum[:, -1]
    before = jnp.einsum("cd,dh->ch", jnp.tril(jnp.ones((chunks, chunks), F32), -1), last, precision=EXACT)
    after = jnp.einsum("cd,dh->ch", jnp.triu(jnp.ones((chunks, chunks), F32), 1), last, precision=EXACT)
    total_log = jnp.sum(last, axis=0)
    enter = jnp.exp(cum) * (seg_chunk == prev_chunk[:, None])[:, :, None]
    leave_log = last[:, None] - cum
    leave = jnp.exp(leave_log) * (seg_chunk == last_chunk[:, None])[:, :, None]
    far_enter = jnp.exp(cum + before[:, None]) * (seg_chunk == seg_before)[:, :, None]
    far_leave = (
        jnp.exp(leave_log + after[:, None]) * (seg_chunk == seg[-1])[:, :, None] * dt.reshape(chunks, CHUNK, heads)
    )
    chunk_decay = jnp.exp(last) * (last_chunk == prev_chunk)[:, None]
    decay_wide = jnp.repeat(chunk_decay, head_width, axis=1)[:, None, :]
    flat = lambda v: v.reshape(toks, heads)
    tok = jnp.concatenate([dt, flat(cum), flat(enter), flat(leave)], axis=1)
    far = jnp.concatenate([flat(far_leave), flat(far_leave), flat(far_enter), flat(far_enter)], axis=1)
    cum_rows = flat(cum).T
    block = conv_width // 3
    mixed, slope = pl.pallas_call(
        conv_kernel,
        grid=(conv_width // block,),
        in_specs=[
            pl.BlockSpec((toks + HALO, block), lambda i: (0, i)),
            pl.BlockSpec((toks, taps), lambda i: (0, 0)),
            pl.BlockSpec((taps, block), lambda i: (0, i)),
            pl.BlockSpec((1, block), lambda i: (0, i)),
        ],
        out_specs=[pl.BlockSpec((toks, block), lambda i: (0, i))] * 2,
        out_shape=[sds((toks, conv_width), BF)] * 2,
        scratch_shapes=[pltpu.VMEM((toks + HALO, block), F32)],
        compiler_params=params(),
        name="conv",
    )(proj, keep, conv_w, conv_b[None, :])

    rows = lambda n: pl.BlockSpec((CHUNK, n), lambda i: (i, 0))
    whole = lambda a, b: pl.BlockSpec((a, b), lambda i: (0, 0))
    own_state = pl.pallas_call(
        state_kernel,
        grid=(chunks,),
        in_specs=[rows(conv_width), rows(lanes), whole(lanes, inner), whole(1, inner)],
        out_specs=whole(STATE + 3 * HALO, inner),
        out_shape=sds((STATE + 3 * HALO, inner), BF),
        scratch_shapes=[pltpu.VMEM((STATE, inner), F32)],
        compiler_params=params(),
        name="own_state",
    )(mixed, far, spread, jnp.repeat(total_log, head_width)[None, :])

    every = lax.all_gather(own_state, "seq", axis=0)
    logs_all = sum(every[:, STATE + i * HALO].astype(F32) for i in range(3))
    ids = jnp.arange(seqs)
    ends = seg_ids[0].reshape(seqs, toks)[:, -1]
    starts_before = jnp.concatenate([jnp.full((1,), -1, jnp.int32), ends[:-1]])
    between = (ids[None, :] > jnp.minimum(ids, me)[:, None]) & (ids[None, :] < jnp.maximum(ids, me)[:, None])
    gap = jnp.exp(jnp.sum(jnp.where(between[:, :, None], logs_all[None], 0.0), axis=1))
    from_past = gap * ((ids < me) & (ends == seg_before))[:, None]
    from_next = gap * ((ids > me) & (starts_before == seg[-1]))[:, None]

    def combine(states, weights):
        return jnp.sum(states[:, :STATE].astype(F32) * weights[:, None, :], axis=0)

    y_inside = pl.pallas_call(
        partial(inside_kernel, heads),
        grid=(chunks,),
        in_specs=[
            rows(conv_width), rows(lanes), rows(1),
            pl.BlockSpec((heads, CHUNK), lambda i: (0, i)),
            pl.BlockSpec((1, CHUNK), lambda i: (0, i)),
            whole(lanes, inner), whole(1, inner),
        ],
        out_specs=rows(inner),
        out_shape=sds((toks, inner), BF),
        compiler_params=params(),
        name="inside",
    )(mixed, tok, seg_col, cum_rows, seg_row, spread, skip_wide)
    wg, wo, y_inside = finish_weights(y_inside)
    gate = dot(normed, wg).astype(BF)
    cot = cotangent[0]
    back = dot_tt(cot, wo).astype(BF)
    first_state = combine(every, from_past)

    states, gated_out, dgate, dy, dgain, dskip_wide, own_ds = pl.pallas_call(
        gate_kernel,
        grid=(chunks,),
        in_specs=[
            rows(inner), rows(conv_width), rows(inner), rows(inner), rows(lanes), rows(lanes),
            pl.BlockSpec((1, 1, inner), lambda i: (i, 0, 0)),
            whole(1, inner), whole(STATE, inner),
            whole(lanes, inner), whole(lanes, inner), whole(lanes, inner),
        ],
        out_specs=[
            pl.BlockSpec((1, STATE, inner), lambda i: (i, 0, 0)),
            rows(inner), rows(inner), rows(inner),
            whole(1, inner), whole(1, inner), whole(STATE, inner),
        ],
        out_shape=[
            sds((chunks, STATE, inner), BF),
            sds((toks, inner), BF), sds((toks, inner), BF), sds((toks, inner), BF),
            sds((1, inner), F32), sds((1, inner), F32), sds((STATE, inner), BF),
        ],
        scratch_shapes=[pltpu.VMEM((STATE, inner), F32)] * 2,
        compiler_params=params(),
        name="gate",
    )(y_inside, mixed, gate, back, tok, far, decay_wide, g_gate[None, :], first_state, spread, spread_ent, spread_leave)

    last_ds = combine(lax.all_gather(own_ds, "seq", axis=0), from_next)
    later, dgate = lax.optimization_barrier((normed, dgate))
    sums = core_sums(later, dgate, gated_out, cot)
    dn_gate = dot_tt(dgate, wg)
    last_ds, dn_gate = lax.optimization_barrier((last_ds, dn_gate))
    sums = sum_over(sums, "wsh", None, lax.axis_size("wsh"))

    flip = lambda n: pl.BlockSpec((CHUNK, n), lambda i: (chunks - 1 - i, 0))
    dz, tokg, inlog, carry = pl.pallas_call(
        partial(back_kernel, heads),
        grid=(chunks,),
        in_specs=[
            flip(inner), flip(conv_width), flip(conv_width), flip(lanes), flip(1),
            pl.BlockSpec((heads, CHUNK), lambda i: (0, chunks - 1 - i)),
            pl.BlockSpec((1, CHUNK), lambda i: (0, chunks - 1 - i)),
            pl.BlockSpec((1, 1, inner), lambda i: (chunks - 1 - i, 0, 0)),
            whole(1, inner),
            pl.BlockSpec((1, STATE, inner), lambda i: (chunks - 1 - i, 0, 0)),
            whole(STATE, inner),
            whole(lanes, inner), whole(lanes, inner), whole(lanes, inner),
            pl.BlockSpec((3, inner, lanes), lambda i: (0, 0, 0)),
        ],
        out_specs=[
            flip(conv_width), flip(lanes),
            pl.BlockSpec((heads, CHUNK), lambda i: (0, chunks - 1 - i)),
            pl.BlockSpec((1, 1, inner), lambda i: (chunks - 1 - i, 0, 0)),
        ],
        out_shape=[
            sds((toks, conv_width), BF), sds((toks, lanes), F32), sds((heads, toks), F32),
            sds((chunks, 1, inner), F32),
        ],
        scratch_shapes=[pltpu.VMEM((STATE, inner), F32), pltpu.VMEM((CHUNK, inner), F32)],
        compiler_params=params(),
        name="scan_back",
    )(
        dy, mixed, slope, tok, seg_col, cum_rows, seg_row, decay_wide, skip_wide, states, last_ds,
        spread, spread_ent, spread_leave, gather,
    )

    dz, sums = lax.optimization_barrier((dz, sums))
    sums = sum_over(sums, "seq", same_core(), seqs // 2)

    dxbc, dconv_w, dconv_b = pl.pallas_call(
        conv_back_kernel,
        grid=(conv_width // block,),
        in_specs=[
            pl.BlockSpec((toks, block), lambda i: (0, i)),
            pl.BlockSpec((toks + HALO, block), lambda i: (0, i)),
            pl.BlockSpec((toks, taps), lambda i: (0, 0)),
            pl.BlockSpec((toks + HALO, taps), lambda i: (0, 0)),
            pl.BlockSpec((taps, block), lambda i: (0, i)),
        ],
        out_specs=[
            pl.BlockSpec((toks + HALO, block), lambda i: (0, i)),
            pl.BlockSpec((taps, block), lambda i: (0, i)),
            pl.BlockSpec((1, block), lambda i: (0, i)),
        ],
        out_shape=[
            sds((toks + HALO, conv_width), BF), sds((taps, conv_width), F32), sds((1, conv_width), F32),
        ],
        scratch_shapes=[
            pltpu.VMEM((toks + HALO, block), F32), pltpu.VMEM((toks + HALO + 8, block), F32),
        ],
        compiler_params=params(),
        name="conv_back",
    )(dz, proj, keep, keep_next, conv_w)

    tokg = tokg.reshape(chunks, CHUNK, lanes)
    from_dx, from_enter, from_leave = [tokg[:, :, i * heads : (i + 1) * heads] for i in range(3)]
    whole_chunk = jnp.sum(carry.reshape(chunks, heads, head_width), axis=2) * chunk_decay
    dlog = (
        inlog.T.reshape(chunks, CHUNK, heads)
        + jnp.einsum("ut,cth->cuh", tri.T, from_enter, precision=EXACT)
        + jnp.einsum("us,csh->cuh", tri - jnp.eye(CHUNK, dtype=F32), from_leave, precision=EXACT)
        + whole_chunk[:, None, :]
    )
    dlog = flat(dlog)
    drate = jnp.sum(dlog * dt, axis=0)
    dstep = (flat(from_dx) + dlog * rates[None, :]) * jax.nn.sigmoid(step_raw)
    dstep_bf = dstep.astype(BF)

    dxbc, sums = lax.optimization_barrier((dxbc, sums))
    dproj = jnp.concatenate([dxbc, jnp.pad(dstep_bf, ((HALO, 0), (0, -heads % 128)))], axis=1)

    def input_grads(dproj):
        dn_ext = dot_tt(dproj, wx)
        over = lax.ppermute(dn_ext[:HALO], "seq", down)
        dn = dn_ext[HALO:] + dn_gate
        return dn + jnp.pad(over, ((toks - HALO, 0), (0, 0)))

    x_f = x_ext[HALO:]
    r = r_ext[HALO:]

    def after_product(dproj):
        dn = input_grads(dproj)
        f = dn * g_norm[None, :]
        x_grad = cot.astype(F32) + r * f - x_f * (r * r * r) * jnp.mean(f * x_f, axis=1, keepdims=True)
        return x_grad, jnp.sum(dn * x_f * r, axis=0)

    x_rows, sums, result, (x_grad, g_norm_part) = reduce_product(
        normed_ext, dproj, sums, lambda left: (x_f + dot(left, wo)).astype(BF), gated_out, after_product
    )
    gate_rows, w_out_grad = spread_back(sums, inner)
    w_in_grad = pl.pallas_call(
        widen_kernel,
        out_shape=sds(w_in.shape[::-1], F32),
        in_specs=[pl.BlockSpec(memory_space=pltpu.VMEM)] * 2,
        out_specs=pl.BlockSpec(memory_space=pltpu.VMEM),
        compiler_params=pltpu.CompilerParams(vmem_limit_bytes=VMEM_LIMIT),
        name="widen",
    )(gate_rows, x_rows).T
    small = (
        g_norm_part,
        dconv_w,
        dconv_b[0],
        jnp.sum(dstep, axis=0),
        drate * rates,
        jnp.sum(dskip_wide.reshape(heads, head_width), axis=1),
        dgain[0],
    )
    small = sum_small(small)
    return (result[None], x_grad[None], small[0], w_in_grad) + tuple(small[1:]) + (w_out_grad,)


def solution(mesh):
    tokens = P("wsh", "seq", None)
    owned = P("wsh", None)
    return jax.shard_map(
        on_device,
        mesh=mesh,
        in_specs=(tokens, owned, P(), owned, P(), P(), P(), P(), P(), P(), owned, tokens),
        out_specs=(tokens, tokens, P(), owned, P(), P(), P(), P(), P(), P(), owned),
        check_vma=False,
    )
```
